512 devices in a mesh: seq: 128 (over y, z_lo, x), ch: 4 (over z_hi, core).
Axes of the slice: x: 4, y: 8, z: 8 (z_hi: 2, z_lo: 4; z = z_hi * 4 + z_lo), core: 2. Of those that a mesh axis runs over, the one named last changes fastest.
Arguments:
- inputs: bfloat16 [256, 32768], P('ch', 'seq'), may hold values from -120 to 120
- clip_len: int32 [16], replicated, may hold values from 1 to 8192, 32768 in all
- clip_order: int32 [16], replicated, may hold values from 0 to 15, each once
- in_proj: bfloat16 [3, 256, 256], P(None, 'ch'), may hold values from -0.375 to 0.375
- out_proj: bfloat16 [256, 256], P(None, 'ch'), may hold values from -0.375 to 0.375
- filt_in: float32 [33, 64], replicated, may hold values from -4 to 4
- filt_out: float32 [2, 256, 64], P(None, 'ch'), may hold values from -0.75 to 0.75
- decay_rate: float32 [2, 256], P(None, 'ch'), may hold values from 0.2 to 1092.2667
- skip_gain: float32 [2, 256], P(None, 'ch'), may hold values from -4 to 4
- cotangent: bfloat16 [256, 32768], P('ch', 'seq'), may hold values from -6 to 6
Outputs:
- mixed: bfloat16 [256, 32768], P('ch', 'seq')
- grad_inputs: bfloat16 [256, 32768], P('ch', 'seq')
- grad_in_proj: float32 [3, 256, 256], P(None, 'ch')
- grad_out_proj: float32 [256, 256], P(None, 'ch')
- grad_filter: float32 [2, 256, 64], P(None, 'ch')
- grad_skip: float32 [2, 256], P(None, 'ch')
The draws below stay inside these ranges and needn't reach their ends.
Inputs may be any that keep to these rules, and one draw needn't show every extreme that they name: `clip_len`: the lengths sum to 32768. `clip_order`: each clip appears once.
All inputs are finite; a program needn't handle non-finite values.
Results may differ from the reference program's by a relative error of at most 0.02.
Values may be sent and summed in bfloat16 or wider, within the bound.
No kernel may reach another device: no remote copies, remote signals or barrier semaphores. Data moves between devices by JAX's collectives and lax.ppermute only.
A program may use at most 128 MiB of HBM per device.

```python
import math
import jax
import jax.numpy as jnp
import numpy as np
from jax import lax

D = 256
E = 64
BANDS = 16
NCLIP = 16
L = 32768
MOST = 8192


def draw_inputs(key, part):
    key = jax.random.fold_in(key, 7)
    noise_key, channel_key, sample_key = jax.random.split(key, 3)
    channel_scale = jnp.exp(jax.random.uniform(channel_key, (D, 1), jnp.float32, 0.0, math.log(10.0)))
    ramp = jnp.arange(L, dtype=jnp.float32)[None, :] / L
    sample_scale = jnp.exp(jax.random.uniform(sample_key, (1, L), jnp.float32, 0.0, math.log(10.0)) + math.log(3.0) * ramp)
    noise = jnp.clip(jax.random.normal(noise_key, (D, L), jnp.float32), -4.0, 4.0)
    return (0.1 * noise * channel_scale * sample_scale).astype(jnp.bfloat16)


def draw_decay_rate(key, part):
    key = jax.random.fold_in(key, 11)
    pick_key, slow_key, fast_key = jax.random.split(key, 3)
    share = 0.5
    slow_rates = jnp.exp(jax.random.uniform(slow_key, (2, D), jnp.float32, math.log(0.2), math.log(2.0)))
    fast_rates = jnp.exp(jax.random.uniform(fast_key, (2, D), jnp.float32, math.log(L / 50.0), math.log(L / 30.0)))
    chosen = jax.random.uniform(pick_key, (2, D), jnp.float32) < share
    return jnp.where(chosen, slow_rates, fast_rates).astype(jnp.float32)


def block_levels(stream_key, shape, shards, low, top_value):
    loudness = 1.0
    for axis_at, parts in shards:
        steps = jax.random.uniform(jax.random.fold_in(jax.random.fold_in(stream_key, 6), axis_at), (parts,), jnp.float32, low / len(shards), top_value / len(shards))
        loudness = loudness * jnp.repeat(jnp.exp(steps), shape[axis_at] // parts).reshape((-1,) + (1,) * (len(shape) - 1 - axis_at))
    return loudness


def length_profile(amount, total, limit, lean):
    portions = [(1 << 20) // math.isqrt(standing ** lean) + 1 for standing in range(2, amount + 1)]
    surplus, holding = total - limit - (amount - 1), [1] * (amount - 1)
    while surplus > 0:
        movable = [i for i in range(amount - 1) if holding[i] < limit]
        pool, budget = sum([portions[i] for i in movable]), surplus
        for i in movable:
            extra = min(limit - holding[i], max(1, budget * portions[i] // pool), surplus)
            holding[i] = holding[i] + extra
            surplus = surplus - extra
    return np.array([limit] + holding)


def ragged(rng, number_of, total, bound, slope):
    if number_of == 2:
        one = jax.random.randint(rng, (), max(1, total - bound), min(bound, total - 1) + 1)
        return jnp.stack([one, total - one])
    sizes = jnp.asarray(length_profile(number_of, total, bound, slope), jnp.int32)
    pairs = (number_of - 1) // 2
    donor, receiver = sizes[1:1 + 2 * pairs:2], sizes[2:2 + 2 * pairs:2]
    room = jnp.minimum(donor - 1, bound - receiver)
    passed = jax.random.randint(jax.random.fold_in(rng, 1), (pairs,), 0, 1 << 20) % (room + 1)
    sizes = sizes.at[1:1 + 2 * pairs:2].set(donor - passed).at[2:2 + 2 * pairs:2].set(receiver + passed)
    return sizes[jax.random.permutation(jax.random.fold_in(rng, 2), number_of)]


def centred(own_key, extent, width, limit, cuts=(), kind=jnp.bfloat16):
    loudness = block_levels(own_key, extent, cuts, -0.22, 0.18) if cuts else 1.0
    values = jax.random.normal(own_key, extent, jnp.float32) * width * loudness
    return jnp.minimum(jnp.maximum(values, -limit), limit).astype(kind)


def setup_inputs(seed: int = 0) -> dict:
    splits = jax.random.split(jax.random.key(seed), 11)
    return {
        "inputs": draw_inputs(jax.random.fold_in(splits[10], 71), 0),
        "clip_len": ragged(splits[1], NCLIP, L, MOST, 2).astype(jnp.int32),
        "clip_order": jax.random.permutation(splits[2], NCLIP).astype(jnp.int32),
        "in_proj": centred(splits[3], (3, D, D), D ** -0.5, 0.375, ((1, 4),)),
        "out_proj": centred(splits[4], (D, D), D ** -0.5, 0.375, ((1, 4),)),
        "filt_in": centred(splits[5], (2 * BANDS + 1, E), 1.0, 4.0, (), jnp.float32),
        "filt_out": centred(splits[6], (2, D, E), E ** -0.5, 0.75, ((1, 4),), jnp.float32),
        "decay_rate": draw_decay_rate(jax.random.fold_in(splits[10], 71), 0),
        "skip_gain": centred(splits[8], (2, D), 1.0, 4.0, ((1, 4),), jnp.float32),
        "cotangent": centred(splits[9], (D, L), 1.0, 6.0, ((0, 4), (1, 128))),
    }


EPSILON = 1e-05
HIGHEST_PRECISION = lax.Precision.HIGHEST

def clip_scale(inputs, clip_len, clip_order):
    lengths = jnp.take(clip_len, clip_order)
    starts = jnp.cumsum(lengths, dtype=jnp.int32) - lengths
    positions = jnp.arange(L, dtype=jnp.int32)
    member = ((positions[:, None] >= starts[None, :]) & (positions[:, None] < (starts + lengths)[None, :])).astype(jnp.float32)
    squares = lax.optimization_barrier(jnp.sum(jnp.square(inputs.astype(jnp.float32)), axis=0))
    power = jnp.dot(squares, member, precision=HIGHEST_PRECISION)
    inverse_rms = lax.rsqrt(power / (D * lengths.astype(jnp.float32)) + EPSILON)
    return jnp.dot(member, inverse_rms, precision=HIGHEST_PRECISION)

def filter_bank(filt_in, filt_out, decay_rate):
    positions = jnp.arange(L, dtype=jnp.int32)
    bands = jnp.arange(1, BANDS + 1, dtype=jnp.int32)
    phases = (positions[:, None] * bands[None, :] % L).astype(jnp.float32) * (2.0 * math.pi / L)
    ramp = positions.astype(jnp.float32) / L
    features = jnp.concatenate([ramp[:, None], jnp.cos(phases), jnp.sin(phases)], axis=1)
    hidden = jnp.sin(jnp.dot(features, filt_in, precision=HIGHEST_PRECISION))
    window = jnp.exp(-decay_rate[:, :, None] * ramp[None, None, :]) * L ** (-0.5)
    shapes = jnp.einsum('te,ice->ict', hidden, filt_out, precision=HIGHEST_PRECISION) * window
    return (hidden, window, shapes)

def spectrum(signal):
    return jnp.fft.rfft(signal, n=2 * L, axis=-1)

def inverse(product):
    return jnp.fft.irfft(product, n=2 * L, axis=-1)[..., :L]

def reference(inputs, clip_len, clip_order, in_proj, out_proj, filt_in, filt_out, decay_rate, skip_gain, cotangent):
    scale = clip_scale(inputs, clip_len, clip_order)
    raw = jnp.einsum('icd,dt->ict', in_proj.astype(jnp.float32), inputs.astype(jnp.float32), precision=HIGHEST_PRECISION)
    projected = lax.optimization_barrier((raw * scale).astype(jnp.bfloat16)).astype(jnp.float32)
    value_in = projected[0]
    gate_one = projected[1]
    gate_two = projected[2]
    hidden, window, shapes = filter_bank(filt_in, filt_out, decay_rate)
    value_spec = spectrum(value_in)
    filter_one = spectrum(shapes[0])
    filter_two = spectrum(shapes[1])
    carry_one = inverse(value_spec * filter_one) + skip_gain[0][:, None] * value_in
    level_one = gate_one * carry_one
    level_spec = spectrum(level_one)
    carry_two = inverse(level_spec * filter_two) + skip_gain[1][:, None] * level_one
    gated = (gate_two * carry_two).astype(jnp.bfloat16)
    mixed = jnp.dot(out_proj, gated, preferred_element_type=jnp.float32).astype(jnp.bfloat16)
    out_grad = jnp.dot(out_proj.T, cotangent, preferred_element_type=jnp.float32)
    out_weight = jnp.dot(cotangent, gated.T, preferred_element_type=jnp.float32)
    scaled_two = gate_two * out_grad
    gate_two_grad = out_grad * carry_two
    second_spec = spectrum(scaled_two)
    level_grad = inverse(second_spec * jnp.conj(filter_two)) + skip_gain[1][:, None] * scaled_two
    shape_two_grad = inverse(second_spec * jnp.conj(level_spec))
    skip_two = lax.optimization_barrier(jnp.sum(scaled_two * level_one, axis=1))
    scaled_one = gate_one * level_grad
    gate_one_grad = level_grad * carry_one
    first_spec = spectrum(scaled_one)
    value_grad = inverse(first_spec * jnp.conj(filter_one)) + skip_gain[0][:, None] * scaled_one
    shape_one_grad = inverse(first_spec * jnp.conj(value_spec))
    skip_one = lax.optimization_barrier(jnp.sum(scaled_one * value_in, axis=1))
    stacked = jnp.stack([value_grad, gate_one_grad, gate_two_grad])
    scaled_grad = (stacked * scale).astype(jnp.bfloat16)
    grad_inputs = jnp.einsum('icd,ict->dt', in_proj.astype(jnp.float32), scaled_grad.astype(jnp.float32), precision=HIGHEST_PRECISION).astype(jnp.bfloat16)
    in_weight = jnp.einsum('ict,dt->icd', scaled_grad.astype(jnp.float32), inputs.astype(jnp.float32), precision=HIGHEST_PRECISION)
    filter_grad = jnp.einsum('te,ict->ice', hidden, jnp.stack([shape_one_grad, shape_two_grad]) * window, precision=HIGHEST_PRECISION)
    skip_grad = jnp.stack([skip_one, skip_two])
    factor = L ** (-0.5)
    return (mixed, grad_inputs, in_weight * factor, out_weight * factor, filter_grad * factor, skip_grad * factor)
```

```python
import functools
import math

import jax
import jax.numpy as jnp
import numpy as np
from jax import lax
from jax.experimental import pallas as pl
from jax.experimental.pallas import tpu as pltpu
from jax.sharding import PartitionSpec as P

EPSILON = 1e-05
HIGHEST = lax.Precision.HIGHEST
F32 = jnp.float32
BF16 = jnp.bfloat16

WIDTH = 256
TOTAL = 32768
SEQ = 128
CHUNK = 256
LOCAL = 64
HIDDEN = 64
BANDS = 16
CLIPS = 16
SEND_ROWS = 16
BACK_ROWS = 8


def halves(table):
    high = table.astype(BF16)
    low = (table - high.astype(np.float32)).astype(BF16)
    return high, low


def tables():
    k1 = np.arange(SEQ)[:, None] + 0.25
    s = np.arange(SEQ)[None, :]
    u = np.arange(CHUNK)[None, :]
    first = 2.0 * np.pi * k1 * s / SEQ
    analysis = np.concatenate([np.cos(first), -np.sin(first)], 0).astype(np.float32)
    synthesis = (np.concatenate([np.cos(first), -np.sin(first)], 0).T / TOTAL).astype(np.float32)
    twist = 2.0 * np.pi * k1 * u / TOTAL
    k2 = np.arange(CHUNK)
    second = 2.0 * np.pi * ((k2[:, None] * k2[None, :]) % CHUNK) / CHUNK
    inner = np.concatenate([np.cos(second), np.sin(second)], 1).astype(np.float32)
    return (
        *halves(analysis),
        *halves(synthesis),
        *halves(inner),
        np.cos(twist).astype(np.float32),
        np.sin(twist).astype(np.float32),
    )


def dot(a, b, dims=((1,), (0,)), precision=None):
    return lax.dot_general(a, b, (dims, ((), ())), precision=precision, preferred_element_type=F32)


def split(x):
    high = x.astype(BF16)
    return high, (x - high.astype(F32)).astype(BF16)


def clip_bounds(clip_len, clip_order):
    starts, lengths = [], []
    start = jnp.int32(0)
    for p in range(CLIPS):
        length = clip_len[clip_order[p]]
        starts.append(start)
        lengths.append(length)
        start = start + length
    return starts, lengths


def front_kernel(
    rank, clip_len, clip_order, full, in_proj, out_proj, filt_in, filt_out, decay,
    send, gate_out, grad_out, hidden_out, window_out, scratch,
):
    inputs = jnp.concatenate([full[128 * j : 128 * j + 64, :] for j in range(4)], 0)
    cotangent = jnp.concatenate([full[128 * j + 64 : 128 * j + 128, :] for j in range(4)], 0)
    raw = dot(in_proj[...], inputs)
    out_grad = dot(out_proj[...], cotangent, ((0,), (0,)))
    gate_two = raw[2 * LOCAL :, :]
    gate_out[...] = gate_two
    grad_out[...] = out_grad

    offset = rank[0] * CHUNK
    starts, lengths = clip_bounds(clip_len, clip_order)
    time = offset + lax.broadcasted_iota(jnp.int32, (SEQ, CHUNK), 1)
    place = lax.broadcasted_iota(jnp.int32, (SEQ, CHUNK), 0)
    member = jnp.zeros((SEQ, CHUNK), F32)
    for p in range(CLIPS):
        inside = (time >= starts[p]) & (time < starts[p] + lengths[p]) & (place == p)
        member = jnp.where(inside, 1.0, member)
    wide = inputs.astype(F32)
    squares = jnp.sum(wide * wide, 0, keepdims=True)
    power = dot(jnp.broadcast_to(squares, (8, CHUNK)), member, ((1,), (1,)), HIGHEST)[:1, :]
    high, low = split(power)
    mid = low.astype(F32)
    low = power - high.astype(F32) - mid
    high = high.astype(F32)

    step = offset + lax.broadcasted_iota(jnp.int32, (BANDS, CHUNK), 1)
    band = 1 + lax.broadcasted_iota(jnp.int32, (BANDS, CHUNK), 0)
    phases = ((step * band) & (TOTAL - 1)).astype(F32) * (2.0 * math.pi / TOTAL)
    ramp = (offset + lax.broadcasted_iota(jnp.int32, (8, CHUNK), 1)).astype(F32) * (1.0 / TOTAL)
    first_row = lax.broadcasted_iota(jnp.int32, (8, HIDDEN), 0) == 0
    ramp_weight = jnp.where(first_row, filt_in[:8, :], 0.0)
    first = ((0,), (0,))
    hidden = jnp.sin(
        dot(ramp_weight, ramp, first, HIGHEST)
        + dot(filt_in[1 : 1 + BANDS, :], jnp.cos(phases), first, HIGHEST)
        + dot(filt_in[1 + BANDS : 1 + 2 * BANDS, :], jnp.sin(phases), first, HIGHEST)
    )
    hidden_out[...] = hidden
    rows = lax.broadcasted_iota(jnp.int32, (LOCAL, LOCAL), 0)
    columns = lax.broadcasted_iota(jnp.int32, (LOCAL, LOCAL), 1)
    shapes = []
    for i in range(2):
        spread = jnp.broadcast_to(decay[i : i + 1, :], (LOCAL, LOCAL))
        rate = jnp.sum(jnp.where(rows == columns, spread, 0.0), 1, keepdims=True)
        window = jnp.exp(-rate * ramp[:1, :]) * TOTAL ** (-0.5)
        window_out[i * LOCAL : (i + 1) * LOCAL, :] = window
        weights = filt_out[i * LOCAL : (i + 1) * LOCAL, :]
        shapes.append(dot(weights, hidden, precision=HIGHEST) * window)

    arrays = [raw[:LOCAL, :], raw[LOCAL : 2 * LOCAL, :], gate_two * out_grad, *shapes]
    for at, values in enumerate(arrays):
        scratch[pl.ds(2 * at, LOCAL, stride=SEND_ROWS), :] = values[:, :128]
        scratch[pl.ds(2 * at + 1, LOCAL, stride=SEND_ROWS), :] = values[:, 128:]
    for at, values in enumerate([high, mid, low]):
        scratch[pl.ds(10 + at, LOCAL, stride=SEND_ROWS), :] = jnp.broadcast_to(values, (LOCAL, 128))
    for at in range(13, SEND_ROWS):
        scratch[pl.ds(at, LOCAL, stride=SEND_ROWS), :] = jnp.zeros((LOCAL, 128), F32)
    packed = scratch[...].astype(BF16)
    send[: LOCAL * SEND_ROWS, :] = packed
    send[LOCAL * SEND_ROWS :, :] = packed


def series_kernel(
    rank, clip_len, clip_order, skip_gain, received,
    analysis_high, analysis_low, synthesis_high, synthesis_low, inner_high, inner_low,
    twist_cos, twist_sin, back, scratch, packed,
):
    role = rank[0] // LOCAL
    channel = rank[0] % LOCAL
    forward = role == 0
    skip_one = skip_gain[0, channel]
    skip_two = skip_gain[1, channel]
    scratch[...] = received[...].astype(F32)

    def plane(row):
        return scratch[pl.ds(row, SEQ, stride=SEND_ROWS), :]

    def signal(at):
        return jnp.concatenate([plane(2 * at), plane(2 * at + 1)], 1)

    power = jnp.sum(plane(10) + (plane(11) + plane(12)), 0, keepdims=True)
    starts, lengths = clip_bounds(clip_len, clip_order)
    time = lax.broadcasted_iota(jnp.int32, (SEQ, CHUNK), 0) * CHUNK + lax.broadcasted_iota(
        jnp.int32, (SEQ, CHUNK), 1
    )
    lane = lax.broadcasted_iota(jnp.int32, (1, 128), 1)
    counts = jnp.ones((1, 128), F32)
    for p in range(CLIPS):
        counts = jnp.where(lane == p, lengths[p].astype(F32), counts)
    inverse_rms = lax.rsqrt(power / (WIDTH * counts) + EPSILON)
    scale = jnp.zeros((SEQ, CHUNK), F32)
    for p in range(CLIPS):
        scale = jnp.where(time >= starts[p], inverse_rms[:, p : p + 1], scale)

    cosines = twist_cos[...]
    sines = twist_sin[...]

    def turn(values, count):
        high, low = split(values)
        product = (
            dot(high, inner_high[...]) + dot(low, inner_high[...]) + dot(high, inner_low[...])
        )
        pieces = []
        for at in range(count):
            real = product[256 * at : 256 * at + 128, :]
            imag = product[256 * at + 128 : 256 * at + 256, :]
            pieces.append((real[:, :256], real[:, 256:], imag[:, :256], imag[:, 256:]))
        return pieces

    def to_spectrum(signals):
        stacked = jnp.concatenate(signals, 1)
        high, low = split(stacked)
        rows = (
            dot(analysis_high[...], high)
            + dot(analysis_high[...], low)
            + dot(analysis_low[...], high)
        )
        twisted = []
        for at in range(len(signals)):
            real = rows[:128, 256 * at : 256 * at + 256]
            imag = rows[128:, 256 * at : 256 * at + 256]
            twisted.append(cosines * real + sines * imag)
            twisted.append(cosines * imag - sines * real)
        pieces = turn(jnp.concatenate(twisted, 0), len(signals))
        return [(rc + is_, ic - rs) for rc, rs, ic, is_ in pieces]

    def to_signal(spectra):
        stacked = jnp.concatenate([part for pair in spectra for part in pair], 0)
        columns = []
        for rc, rs, ic, is_ in turn(stacked, len(spectra)):
            real = rc - is_
            imag = ic + rs
            columns.append(
                jnp.concatenate([cosines * real - sines * imag, cosines * imag + sines * real], 0)
            )
        high, low = split(jnp.concatenate(columns, 1))
        rows = (
            dot(synthesis_high[...], high)
            + dot(synthesis_high[...], low)
            + dot(synthesis_low[...], high)
        )
        return [rows[:, 256 * at : 256 * at + 256] for at in range(len(spectra))]

    def times(a, b, sign):
        return (a[0] * b[0] - sign * (a[1] * b[1]), a[1] * b[0] + sign * (a[0] * b[1]))

    def choose(a, b):
        return jnp.where(forward, a, b)

    def choose_spectrum(a, b):
        return tuple(choose(x, y) for x, y in zip(a, b))

    value = signal(0) * scale
    gate_one = signal(1) * scale
    scaled_two = signal(2) * scale
    value_spec, second_spec, filter_one, filter_two = to_spectrum(
        [value, scaled_two, signal(3), signal(4)]
    )
    carry_one, level_grad = to_signal(
        [times(value_spec, filter_one, 1.0), times(second_spec, filter_two, -1.0)]
    )
    carry_one = carry_one + skip_one * value
    level_grad = level_grad + skip_two * scaled_two
    level_one = gate_one * carry_one
    scaled_one = gate_one * level_grad
    level_spec, first_spec = to_spectrum([level_one, scaled_one])
    sign = choose(jnp.float32(1.0), jnp.float32(-1.0))
    chain, shape_grad = to_signal(
        [
            times(
                choose_spectrum(level_spec, first_spec),
                choose_spectrum(filter_two, filter_one),
                sign,
            ),
            times(
                choose_spectrum(second_spec, first_spec),
                choose_spectrum(level_spec, value_spec),
                -1.0,
            ),
        ]
    )
    source = choose(level_one, scaled_one)
    chain = scale * (chain + choose(skip_two, skip_one) * source)
    gate_grad = scale * (level_grad * carry_one)
    partner = choose(scaled_two, value)
    skip_grad = jnp.sum(jnp.sum(source * partner, 0, keepdims=True), 1, keepdims=True)
    high, low = split(skip_grad)
    mid = low.astype(F32)
    low = skip_grad - high.astype(F32) - mid
    high = high.astype(F32)
    skip_row = jnp.where(
        lane == 0, high, jnp.where(lane == 1, mid, jnp.where(lane == 2, low, 0.0))
    )
    for at, values in enumerate([chain, shape_grad, gate_grad]):
        packed[pl.ds(2 * at, SEQ, stride=BACK_ROWS), :] = values[:, :128]
        packed[pl.ds(2 * at + 1, SEQ, stride=BACK_ROWS), :] = values[:, 128:]
    packed[pl.ds(6, SEQ, stride=BACK_ROWS), :] = jnp.broadcast_to(skip_row, (SEQ, 128))
    packed[pl.ds(7, SEQ, stride=BACK_ROWS), :] = jnp.zeros((SEQ, 128), F32)
    back[...] = packed[...].astype(BF16)


def back_kernel(
    received, full, in_proj, out_proj, gate_in, grad_in, hidden, window,
    partial, weights, skip_out, scratch,
):
    scratch[...] = received[...].astype(F32)

    def plane(role, row):
        return scratch[pl.ds(role * LOCAL * BACK_ROWS + row, LOCAL, stride=BACK_ROWS), :]

    def signal(role, at):
        return jnp.concatenate([plane(role, 2 * at), plane(role, 2 * at + 1)], 1)

    carry = signal(0, 0)
    gated = (gate_in[...] * carry).astype(BF16)
    scaled_grad = jnp.concatenate(
        [signal(1, 0).astype(BF16), signal(1, 2).astype(BF16), (grad_in[...] * carry).astype(BF16)],
        0,
    )
    inputs = jnp.concatenate([full[128 * j : 128 * j + 64, :] for j in range(4)], 0)
    cotangent = jnp.concatenate([full[128 * j + 64 : 128 * j + 128, :] for j in range(4)], 0)
    mixed = dot(out_proj[...], gated).astype(BF16)
    grad_inputs = dot(in_proj[...], scaled_grad, ((0,), (0,))).astype(BF16)
    for j in range(4):
        partial[128 * j : 128 * j + 64, :] = mixed[64 * j : 64 * j + 64, :]
        partial[128 * j + 64 : 128 * j + 128, :] = grad_inputs[64 * j : 64 * j + 64, :]
    last = ((1,), (1,))
    in_weight = dot(scaled_grad, inputs, last)
    empty = jnp.zeros((LOCAL, CHUNK), BF16)
    out_weight = dot(cotangent, jnp.concatenate([gated, empty], 0), last)
    shape_grads = jnp.concatenate([signal(1, 1), signal(0, 1)], 0) * window[...]
    padded = jnp.concatenate([hidden[...], jnp.zeros((LOCAL, CHUNK), F32)], 0)
    filter_grad = dot(shape_grads, padded, last, HIGHEST)
    for at in range(24):
        for half in range(2):
            weights[2 * at + half] = in_weight[
                8 * at : 8 * at + 8, 128 * half : 128 * half + 128
            ].astype(BF16)
    for at in range(32):
        weights[48 + at] = out_weight[8 * at : 8 * at + 8, :].astype(BF16)
    for at in range(16):
        weights[80 + at] = filter_grad[8 * at : 8 * at + 8, :].astype(BF16)
    for at in range(96, 128):
        weights[at] = jnp.zeros((8, 128), BF16)
    lane = lax.broadcasted_iota(jnp.int32, (8, 128), 1)
    pick = jnp.where(lane < 3, 1.0, 0.0).astype(BF16)
    for role in range(2):
        total = dot(pick, plane(role, 6).astype(BF16), last)[:1, :]
        skip_out[1 - role : 2 - role, :] = total * TOTAL ** (-0.5)


def sum_kernel(received, spread):
    total = jnp.sum(received[...].astype(F32), 0, keepdims=True) * TOTAL ** (-0.5)
    spread[...] = jnp.broadcast_to(total, (SEQ, 8, 128)).astype(BF16)


def last_kernel(received, in_weight, out_weight, filter_grad):
    for at in range(24):
        for half in range(2):
            in_weight[8 * at : 8 * at + 8, 128 * half : 128 * half + 128] = received[
                2 * at + half
            ].astype(F32)
    for at in range(32):
        out_weight[8 * at : 8 * at + 8, :] = received[48 + at].astype(F32)[:, :LOCAL]
    for at in range(16):
        filter_grad[8 * at : 8 * at + 8, :] = received[80 + at].astype(F32)[:, :HIDDEN]


def call(kernel, name, outs, scalars, arrays, scratch=()):
    def vmem():
        return pl.BlockSpec(memory_space=pltpu.VMEM)

    return pl.pallas_call(
        kernel,
        name=name,
        out_shape=[jax.ShapeDtypeStruct(shape, kind) for shape, kind in outs],
        in_specs=[pl.BlockSpec(memory_space=pltpu.SMEM)] * scalars + [vmem() for _ in range(arrays)],
        out_specs=[vmem() for _ in outs],
        scratch_shapes=[pltpu.VMEM(shape, F32) for shape in scratch],
        compiler_params=pltpu.CompilerParams(vmem_limit_bytes=32 * 1024 * 1024),
    )


def front():
    return call(
        front_kernel,
        "project",
        [
            ((SEQ * SEND_ROWS, 128), BF16),
            ((LOCAL, CHUNK), F32),
            ((LOCAL, CHUNK), F32),
            ((HIDDEN, CHUNK), F32),
            ((2 * LOCAL, CHUNK), F32),
        ],
        3,
        6,
        [(LOCAL * SEND_ROWS, 128)],
    )


def series():
    return call(
        series_kernel,
        "convolve",
        [((SEQ * BACK_ROWS, 128), BF16)],
        4,
        9,
        [(SEQ * SEND_ROWS, 128), (SEQ * BACK_ROWS, 128)],
    )


def rear():
    return call(
        back_kernel,
        "weigh",
        [((4 * 128, CHUNK), BF16), ((SEQ, 8, 128), BF16), ((2, LOCAL), F32)],
        0,
        8,
        [(SEQ * BACK_ROWS, 128)],
    )


def total():
    return call(sum_kernel, "add_up", [((SEQ, 8, 128), BF16)], 0, 1)


def finish():
    return call(
        last_kernel,
        "unpack",
        [((3 * LOCAL, WIDTH), F32), ((WIDTH, LOCAL), F32), ((2 * LOCAL, HIDDEN), F32)],
        0,
        1,
    )


def swap(values):
    return lax.all_to_all(values, "seq", split_axis=0, concat_axis=0, tiled=True)


def shards(
    inputs,
    clip_len,
    clip_order,
    in_proj,
    out_proj,
    filt_in,
    filt_out,
    decay_rate,
    skip_gain,
    cotangent,
):
    rank = lax.axis_index("seq").astype(jnp.int32).reshape(1)
    in_rows = in_proj.reshape(3 * LOCAL, WIDTH)
    full = lax.all_gather(jnp.concatenate([inputs, cotangent], 0), "ch", axis=0, tiled=True)
    send, gate_two, out_grad, hidden, window = front()(
        rank, clip_len, clip_order, full, in_rows, out_proj, filt_in,
        filt_out.reshape(2 * LOCAL, HIDDEN), decay_rate,
    )
    received = swap(send.reshape(SEQ, SEND_ROWS, 128)).reshape(SEQ * SEND_ROWS, 128)
    (back,) = series()(
        rank, clip_len, clip_order, skip_gain, received, *[jnp.asarray(x) for x in tables()]
    )
    returned = swap(back.reshape(SEQ, BACK_ROWS, 128)).reshape(SEQ * BACK_ROWS, 128)
    partial, weights, grad_skip = rear()(
        returned, full, in_rows, out_proj, gate_two, out_grad, hidden, window
    )
    rows = lax.psum_scatter(partial, "ch", scatter_dimension=0, tiled=True)
    (spread,) = total()(swap(weights))
    in_weight, out_weight, filter_grad = finish()(swap(spread))
    return (
        rows[:64],
        rows[64:],
        in_weight.reshape(3, LOCAL, WIDTH),
        out_weight,
        filter_grad.reshape(2, LOCAL, HIDDEN),
        grad_skip,
    )


def solution(mesh):
    return jax.shard_map(
        shards,
        mesh=mesh,
        in_specs=(
            P("ch", "seq"),
            P(),
            P(),
            P(None, "ch", None),
            P(None, "ch"),
            P(),
            P(None, "ch", None),
            P(None, "ch"),
            P(None, "ch"),
            P("ch", "seq"),
        ),
        out_specs=(
            P("ch", "seq"),
            P("ch", "seq"),
            P(None, "ch", None),
            P(None, "ch"),
            P(None, "ch", None),
            P(None, "ch"),
        ),
        check_vma=False,
    )
```

```python
import functools
import math

import jax
import jax.numpy as jnp
import numpy as np
from jax import lax
from jax.experimental import pallas as pl
from jax.experimental.pallas import tpu as pltpu
from jax.sharding import PartitionSpec as P

EPSILON = 1e-05
HIGHEST = lax.Precision.HIGHEST
F32 = jnp.float32
BF16 = jnp.bfloat16

WIDTH = 256
TOTAL = 32768
SEQ = 128
CHUNK = 256
LOCAL = 64
HIDDEN = 64
BANDS = 16
CLIPS = 16
SHAPE_ROWS = 4
SEND_ROWS = 8
BACK_ROWS = 8


def halves(table):
    high = table.astype(BF16)
    low = (table - high.astype(np.float32)).astype(BF16)
    return high, low


def tables():
    k1 = np.arange(SEQ)[:, None] + 0.25
    s = np.arange(SEQ)[None, :]
    u = np.arange(CHUNK)[None, :]
    first = 2.0 * np.pi * k1 * s / SEQ
    analysis = np.concatenate([np.cos(first), -np.sin(first)], 0).astype(np.float32)
    synthesis = (np.concatenate([np.cos(first), -np.sin(first)], 0).T / TOTAL).astype(np.float32)
    twist = 2.0 * np.pi * k1 * u / TOTAL
    k2 = np.arange(CHUNK)
    second = 2.0 * np.pi * ((k2[:, None] * k2[None, :]) % CHUNK) / CHUNK
    inner = np.concatenate([np.cos(second), np.sin(second)], 1).astype(np.float32)
    return (
        *halves(analysis),
        *halves(synthesis),
        *halves(inner),
        np.cos(twist).astype(np.float32),
        np.sin(twist).astype(np.float32),
    )


def dot(a, b, dims=((1,), (0,)), precision=None):
    return lax.dot_general(a, b, (dims, ((), ())), precision=precision, preferred_element_type=F32)


def split(x):
    high = x.astype(BF16)
    return high, (x - high.astype(F32)).astype(BF16)


def clip_bounds(clip_len, clip_order):
    starts, lengths = [], []
    start = jnp.int32(0)
    for p in range(CLIPS):
        length = clip_len[clip_order[p]]
        starts.append(start)
        lengths.append(length)
        start = start + length
    return starts, lengths


def shape_kernel(rank, filt_in, filt_out, decay, send, hidden_out, window_out, scratch):
    offset = rank[0] * CHUNK
    step = offset + lax.broadcasted_iota(jnp.int32, (BANDS, CHUNK), 1)
    band = 1 + lax.broadcasted_iota(jnp.int32, (BANDS, CHUNK), 0)
    phases = ((step * band) & (TOTAL - 1)).astype(F32) * (2.0 * math.pi / TOTAL)
    ramp = (offset + lax.broadcasted_iota(jnp.int32, (8, CHUNK), 1)).astype(F32) * (1.0 / TOTAL)
    first_row = lax.broadcasted_iota(jnp.int32, (8, HIDDEN), 0) == 0
    ramp_weight = jnp.where(first_row, filt_in[:8, :], 0.0)
    first = ((0,), (0,))
    hidden = jnp.sin(
        dot(ramp_weight, ramp, first, HIGHEST)
        + dot(filt_in[1 : 1 + BANDS, :], jnp.cos(phases), first, HIGHEST)
        + dot(filt_in[1 + BANDS : 1 + 2 * BANDS, :], jnp.sin(phases), first, HIGHEST)
    )
    hidden_out[...] = hidden
    rows = lax.broadcasted_iota(jnp.int32, (LOCAL, LOCAL), 0)
    columns = lax.broadcasted_iota(jnp.int32, (LOCAL, LOCAL), 1)
    for i in range(2):
        spread = jnp.broadcast_to(decay[i : i + 1, :], (LOCAL, LOCAL))
        rate = jnp.sum(jnp.where(rows == columns, spread, 0.0), 1, keepdims=True)
        window = jnp.exp(-rate * ramp[:1, :]) * TOTAL ** (-0.5)
        window_out[i * LOCAL : (i + 1) * LOCAL, :] = window
        weights = filt_out[i * LOCAL : (i + 1) * LOCAL, :]
        shape = dot(weights, hidden, precision=HIGHEST) * window
        scratch[pl.ds(2 * i, LOCAL, stride=SHAPE_ROWS), :] = shape[:, :128]
        scratch[pl.ds(2 * i + 1, LOCAL, stride=SHAPE_ROWS), :] = shape[:, 128:]
    packed = scratch[...].astype(BF16)
    send[: LOCAL * SHAPE_ROWS, :] = packed
    send[LOCAL * SHAPE_ROWS :, :] = packed


def front_kernel(
    rank, clip_len, clip_order, full, in_proj, out_proj, send, gate_out, grad_out, scratch
):
    inputs = jnp.concatenate([full[128 * j : 128 * j + 64, :] for j in range(4)], 0)
    cotangent = jnp.concatenate([full[128 * j + 64 : 128 * j + 128, :] for j in range(4)], 0)
    raw = dot(in_proj[...], inputs)
    out_grad = dot(out_proj[...], cotangent)
    gate_two = raw[2 * LOCAL :, :]
    gate_out[...] = gate_two
    grad_out[...] = out_grad

    offset = rank[0] * CHUNK
    starts, lengths = clip_bounds(clip_len, clip_order)
    time = offset + lax.broadcasted_iota(jnp.int32, (SEQ, CHUNK), 1)
    place = lax.broadcasted_iota(jnp.int32, (SEQ, CHUNK), 0)
    member = jnp.zeros((SEQ, CHUNK), F32)
    for p in range(CLIPS):
        inside = (time >= starts[p]) & (time < starts[p] + lengths[p]) & (place == p)
        member = jnp.where(inside, 1.0, member)
    wide = inputs.astype(F32)
    squares = jnp.sum(wide * wide, 0, keepdims=True)
    power = dot(jnp.broadcast_to(squares, (8, CHUNK)), member, ((1,), (1,)), HIGHEST)[:1, :]
    high, low = split(power)

    arrays = [raw[:LOCAL, :], raw[LOCAL : 2 * LOCAL, :], gate_two * out_grad]
    for at, values in enumerate(arrays):
        scratch[pl.ds(2 * at, LOCAL, stride=SEND_ROWS), :] = values[:, :128]
        scratch[pl.ds(2 * at + 1, LOCAL, stride=SEND_ROWS), :] = values[:, 128:]
    for at, values in enumerate([high, low]):
        scratch[pl.ds(6 + at, LOCAL, stride=SEND_ROWS), :] = jnp.broadcast_to(
            values.astype(F32), (LOCAL, 128)
        )
    packed = scratch[...].astype(BF16)
    send[: LOCAL * SEND_ROWS, :] = packed
    send[LOCAL * SEND_ROWS :, :] = packed


def turn(values, count, inner_high, inner_low):
    high, low = split(values)
    product = dot(high, inner_high[...]) + dot(low, inner_high[...]) + dot(high, inner_low[...])
    pieces = []
    for at in range(count):
        real = product[256 * at : 256 * at + 128, :]
        imag = product[256 * at + 128 : 256 * at + 256, :]
        pieces.append((real[:, :256], real[:, 256:], imag[:, :256], imag[:, 256:]))
    return pieces


def to_spectrum(signals, cosines, sines, analysis_high, analysis_low, inner_high, inner_low):
    high, low = split(jnp.concatenate(signals, 1))
    rows = (
        dot(analysis_high[...], high)
        + dot(analysis_high[...], low)
        + dot(analysis_low[...], high)
    )
    twisted = []
    for at in range(len(signals)):
        real = rows[:128, 256 * at : 256 * at + 256]
        imag = rows[128:, 256 * at : 256 * at + 256]
        twisted.append(cosines * real + sines * imag)
        twisted.append(cosines * imag - sines * real)
    pieces = turn(jnp.concatenate(twisted, 0), len(signals), inner_high, inner_low)
    return [(rc + is_, ic - rs) for rc, rs, ic, is_ in pieces]


def to_signal(spectra, cosines, sines, synthesis_high, synthesis_low, inner_high, inner_low):
    stacked = jnp.concatenate([part for pair in spectra for part in pair], 0)
    columns = []
    for rc, rs, ic, is_ in turn(stacked, len(spectra), inner_high, inner_low):
        real = rc - is_
        imag = ic + rs
        columns.append(
            jnp.concatenate([cosines * real - sines * imag, cosines * imag + sines * real], 0)
        )
    high, low = split(jnp.concatenate(columns, 1))
    rows = (
        dot(synthesis_high[...], high)
        + dot(synthesis_high[...], low)
        + dot(synthesis_low[...], high)
    )
    return [rows[:, 256 * at : 256 * at + 256] for at in range(len(spectra))]


def filter_kernel(
    received, analysis_high, analysis_low, inner_high, inner_low, twist_cos, twist_sin,
    spectra, scratch,
):
    scratch[...] = received[...].astype(F32)

    def signal(at):
        return jnp.concatenate(
            [scratch[pl.ds(2 * at + half, SEQ, stride=SHAPE_ROWS), :] for half in range(2)], 1
        )

    filters = to_spectrum(
        [signal(0), signal(1)],
        twist_cos[...], twist_sin[...], analysis_high, analysis_low, inner_high, inner_low,
    )
    for at, (real, imag) in enumerate(filters):
        spectra[256 * at : 256 * at + 128, :] = real
        spectra[256 * at + 128 : 256 * at + 256, :] = imag


def series_kernel(
    rank, clip_len, clip_order, skip_gain, received, spectra,
    analysis_high, analysis_low, synthesis_high, synthesis_low, inner_high, inner_low,
    twist_cos, twist_sin, back, scratch, packed,
):
    role = rank[0] // LOCAL
    channel = rank[0] % LOCAL
    forward = role == 0
    skip_one = skip_gain[0, channel]
    skip_two = skip_gain[1, channel]
    scratch[...] = received[...].astype(F32)

    def plane(row):
        return scratch[pl.ds(row, SEQ, stride=SEND_ROWS), :]

    def signal(at):
        return jnp.concatenate([plane(2 * at), plane(2 * at + 1)], 1)

    power = jnp.sum(plane(6) + plane(7), 0, keepdims=True)
    starts, lengths = clip_bounds(clip_len, clip_order)
    time = lax.broadcasted_iota(jnp.int32, (SEQ, CHUNK), 0) * CHUNK + lax.broadcasted_iota(
        jnp.int32, (SEQ, CHUNK), 1
    )
    lane = lax.broadcasted_iota(jnp.int32, (1, 128), 1)
    counts = jnp.ones((1, 128), F32)
    for p in range(CLIPS):
        counts = jnp.where(lane == p, lengths[p].astype(F32), counts)
    inverse_rms = lax.rsqrt(power / (WIDTH * counts) + EPSILON)
    scale = jnp.zeros((SEQ, CHUNK), F32)
    for p in range(CLIPS):
        scale = jnp.where(time >= starts[p], inverse_rms[:, p : p + 1], scale)

    cosines = twist_cos[...]
    sines = twist_sin[...]

    def analyse(signals):
        return to_spectrum(
            signals, cosines, sines, analysis_high, analysis_low, inner_high, inner_low
        )

    def synthesise(parts):
        return to_signal(
            parts, cosines, sines, synthesis_high, synthesis_low, inner_high, inner_low
        )

    def times(a, b, sign):
        return (a[0] * b[0] - sign * (a[1] * b[1]), a[1] * b[0] + sign * (a[0] * b[1]))

    def choose(a, b):
        return jnp.where(forward, a, b)

    def choose_spectrum(a, b):
        return tuple(choose(x, y) for x, y in zip(a, b))

    value = signal(0) * scale
    gate_one = signal(1) * scale
    scaled_two = signal(2) * scale
    filter_one, filter_two = [
        (spectra[256 * at : 256 * at + 128, :], spectra[256 * at + 128 : 256 * at + 256, :])
        for at in range(2)
    ]
    value_spec, second_spec = analyse([value, scaled_two])
    carry_one, level_grad = synthesise(
        [times(value_spec, filter_one, 1.0), times(second_spec, filter_two, -1.0)]
    )
    carry_one = carry_one + skip_one * value
    level_grad = level_grad + skip_two * scaled_two
    level_one = gate_one * carry_one
    scaled_one = gate_one * level_grad
    level_spec, first_spec = analyse([level_one, scaled_one])
    sign = choose(jnp.float32(1.0), jnp.float32(-1.0))
    chain, shape_grad = synthesise(
        [
            times(
                choose_spectrum(level_spec, first_spec),
                choose_spectrum(filter_two, filter_one),
                sign,
            ),
            times(
                choose_spectrum(second_spec, first_spec),
                choose_spectrum(level_spec, value_spec),
                -1.0,
            ),
        ]
    )
    source = choose(level_one, scaled_one)
    chain = scale * (chain + choose(skip_two, skip_one) * source)
    gate_grad = scale * (level_grad * carry_one)
    partner = choose(scaled_two, value)
    skip_grad = jnp.sum(jnp.sum(source * partner, 0, keepdims=True), 1, keepdims=True)
    high, low = split(skip_grad)
    mid = low.astype(F32)
    low = skip_grad - high.astype(F32) - mid
    high = high.astype(F32)
    skip_row = jnp.where(
        lane == 0, high, jnp.where(lane == 1, mid, jnp.where(lane == 2, low, 0.0))
    )
    for at, values in enumerate([chain, shape_grad, gate_grad]):
        packed[pl.ds(2 * at, SEQ, stride=BACK_ROWS), :] = values[:, :128]
        packed[pl.ds(2 * at + 1, SEQ, stride=BACK_ROWS), :] = values[:, 128:]
    packed[pl.ds(6, SEQ, stride=BACK_ROWS), :] = jnp.broadcast_to(skip_row, (SEQ, 128))
    packed[pl.ds(7, SEQ, stride=BACK_ROWS), :] = jnp.zeros((SEQ, 128), F32)
    back[...] = packed[...].astype(BF16)


def back_kernel(
    place, received, full, in_proj, out_proj, gate_in, grad_in, hidden, window,
    given, kept, weights, skip_out, scratch,
):
    scratch[...] = received[...].astype(F32)

    def plane(role, row):
        return scratch[pl.ds(role * LOCAL * BACK_ROWS + row, LOCAL, stride=BACK_ROWS), :]

    def signal(role, at):
        return jnp.concatenate([plane(role, 2 * at), plane(role, 2 * at + 1)], 1)

    carry = signal(0, 0)
    gated = (gate_in[...] * carry).astype(BF16)
    scaled_grad = jnp.concatenate(
        [signal(1, 0).astype(BF16), signal(1, 2).astype(BF16), (grad_in[...] * carry).astype(BF16)],
        0,
    )
    inputs = jnp.concatenate([full[128 * j : 128 * j + 64, :] for j in range(4)], 0)
    cotangent = jnp.concatenate([full[128 * j + 64 : 128 * j + 128, :] for j in range(4)], 0)
    first = ((0,), (0,))
    last = ((1,), (1,))
    mixed = dot(out_proj[...], gated, first)
    grad_inputs = dot(in_proj[...], scaled_grad, first)
    even = place[0] % 2 == 0
    for at in range(2):
        for to, values in enumerate([mixed, grad_inputs]):
            low = values[128 * at : 128 * at + 64, :]
            high = values[128 * at + 64 : 128 * at + 128, :]
            rows = slice(128 * at + 64 * to, 128 * at + 64 * to + 64)
            given[rows, :] = jnp.where(even, high, low).astype(BF16)
            kept[rows, :] = jnp.where(even, low, high)
    in_weight = dot(scaled_grad, inputs, last)
    out_weight = dot(gated, cotangent, last)
    shape_grads = jnp.concatenate([signal(1, 1), signal(0, 1)], 0) * window[...]
    padded = jnp.concatenate([hidden[...], jnp.zeros((LOCAL, CHUNK), F32)], 0)
    filter_grad = dot(shape_grads, padded, last, HIGHEST)
    for at in range(32):
        source, row = (in_weight, at) if at < 24 else (out_weight, at - 24)
        for half in range(2):
            weights[2 * at + half] = source[
                8 * row : 8 * row + 8, 128 * half : 128 * half + 128
            ].astype(BF16)
    for at in range(16):
        weights[64 + at] = filter_grad[8 * at : 8 * at + 8, :].astype(BF16)
    for at in range(80, 128):
        weights[at] = jnp.zeros((8, 128), BF16)
    lane = lax.broadcasted_iota(jnp.int32, (8, 128), 1)
    pick = jnp.where(lane < 3, 1.0, 0.0).astype(BF16)
    for role in range(2):
        total = dot(pick, plane(role, 6).astype(BF16), last)[:1, :]
        skip_out[1 - role : 2 - role, :] = total * TOTAL ** (-0.5)


def core_kernel(place, received, kept, given, left):
    total = kept[...] + received[...].astype(F32)
    near = place[0] < 2
    given[...] = jnp.where(near, total[128:, :], total[:128, :]).astype(BF16)
    left[...] = jnp.where(near, total[:128, :], total[128:, :])


def chip_kernel(received, left, mixed, grad_inputs):
    total = (left[...] + received[...].astype(F32)).astype(BF16)
    mixed[...] = total[:64, :]
    grad_inputs[...] = total[64:, :]


def sum_kernel(received, spread):
    total = jnp.sum(received[...].astype(F32), 0, keepdims=True) * TOTAL ** (-0.5)
    spread[...] = jnp.broadcast_to(total, (SEQ, 8, 128)).astype(BF16)


def last_kernel(received, in_weight, out_weight, filter_grad):
    for at in range(32):
        target, row = (in_weight, at) if at < 24 else (out_weight, at - 24)
        for half in range(2):
            target[8 * row : 8 * row + 8, 128 * half : 128 * half + 128] = received[
                2 * at + half
            ].astype(F32)
    for at in range(16):
        filter_grad[8 * at : 8 * at + 8, :] = received[64 + at].astype(F32)[:, :HIDDEN]


def call(kernel, name, outs, scalars, arrays, scratch=()):
    def vmem():
        return pl.BlockSpec(memory_space=pltpu.VMEM)

    return pl.pallas_call(
        kernel,
        name=name,
        out_shape=[jax.ShapeDtypeStruct(shape, kind) for shape, kind in outs],
        in_specs=[pl.BlockSpec(memory_space=pltpu.SMEM)] * scalars + [vmem() for _ in range(arrays)],
        out_specs=[vmem() for _ in outs],
        scratch_shapes=[pltpu.VMEM(shape, F32) for shape in scratch],
        compiler_params=pltpu.CompilerParams(vmem_limit_bytes=32 * 1024 * 1024),
    )


def shaping():
    return call(
        shape_kernel,
        "shape",
        [
            ((SEQ * SHAPE_ROWS, 128), BF16),
            ((HIDDEN, CHUNK), F32),
            ((2 * LOCAL, CHUNK), F32),
        ],
        1,
        3,
        [(LOCAL * SHAPE_ROWS, 128)],
    )


def front():
    return call(
        front_kernel,
        "project",
        [((SEQ * SEND_ROWS, 128), BF16), ((LOCAL, CHUNK), F32), ((LOCAL, CHUNK), F32)],
        3,
        3,
        [(LOCAL * SEND_ROWS, 128)],
    )


def filters():
    return call(
        filter_kernel, "filters", [((512, CHUNK), F32)], 0, 7, [(SEQ * SHAPE_ROWS, 128)]
    )


def series():
    return call(
        series_kernel,
        "convolve",
        [((SEQ * BACK_ROWS, 128), BF16)],
        4,
        10,
        [(SEQ * SEND_ROWS, 128), (SEQ * BACK_ROWS, 128)],
    )


def rear():
    return call(
        back_kernel,
        "weigh",
        [
            ((256, CHUNK), BF16),
            ((256, CHUNK), F32),
            ((SEQ, 8, 128), BF16),
            ((2, LOCAL), F32),
        ],
        1,
        8,
        [(SEQ * BACK_ROWS, 128)],
    )


def core_sum():
    return call(core_kernel, "add_core", [((128, CHUNK), BF16), ((128, CHUNK), F32)], 1, 2)


def chip_sum():
    return call(chip_kernel, "add_chip", [((64, CHUNK), BF16), ((64, CHUNK), BF16)], 0, 2)


def total():
    return call(sum_kernel, "add_up", [((SEQ, 8, 128), BF16)], 0, 1)


def finish():
    return call(
        last_kernel,
        "unpack",
        [((3 * LOCAL, WIDTH), F32), ((LOCAL, WIDTH), F32), ((2 * LOCAL, HIDDEN), F32)],
        0,
        1,
    )


def swap(values):
    return lax.all_to_all(values, "seq", split_axis=0, concat_axis=0, tiled=True)


def shards(
    inputs,
    clip_len,
    clip_order,
    in_proj,
    out_proj,
    filt_in,
    filt_out,
    decay_rate,
    skip_gain,
    cotangent,
):
    rank = lax.axis_index("seq").astype(jnp.int32).reshape(1)
    place = lax.axis_index("ch").astype(jnp.int32).reshape(1)
    in_rows = in_proj.reshape(3 * LOCAL, WIDTH)
    out_rows = out_proj.T
    analysis_high, analysis_low, *rest = [jnp.asarray(x) for x in tables()]
    synthesis_high, synthesis_low, inner_high, inner_low, twist_cos, twist_sin = rest
    shapes, hidden, window = shaping()(
        rank, filt_in, filt_out.reshape(2 * LOCAL, HIDDEN), decay_rate
    )
    shapes = swap(shapes.reshape(SEQ, SHAPE_ROWS, 128)).reshape(SEQ * SHAPE_ROWS, 128)
    full = lax.all_gather(jnp.concatenate([inputs, cotangent], 0), "ch", axis=0, tiled=True)
    send, gate_two, out_grad = front()(rank, clip_len, clip_order, full, in_rows, out_rows)
    received = swap(send.reshape(SEQ, SEND_ROWS, 128)).reshape(SEQ * SEND_ROWS, 128)
    (spectra,) = filters()(
        shapes, analysis_high, analysis_low, inner_high, inner_low, twist_cos, twist_sin
    )
    (back,) = series()(
        rank, clip_len, clip_order, skip_gain, received, spectra,
        analysis_high, analysis_low, *rest,
    )
    returned = swap(back.reshape(SEQ, BACK_ROWS, 128)).reshape(SEQ * BACK_ROWS, 128)
    given, kept, weights, grad_skip = rear()(
        place, returned, full, in_rows, out_rows, gate_two, out_grad, hidden, window
    )
    over_cores = lax.ppermute(given, "ch", [(0, 1), (1, 0), (2, 3), (3, 2)])
    given, left = core_sum()(place, over_cores, kept)
    over_chips = lax.ppermute(given, "ch", [(0, 2), (2, 0), (1, 3), (3, 1)])
    mixed, grad_inputs = chip_sum()(over_chips, left)
    (spread,) = total()(swap(weights))
    in_weight, out_weight, filter_grad = finish()(swap(spread))
    return (
        mixed,
        grad_inputs,
        in_weight.reshape(3, LOCAL, WIDTH),
        out_weight.T,
        filter_grad.reshape(2, LOCAL, HIDDEN),
        grad_skip,
    )


def solution(mesh):
    return jax.shard_map(
        shards,
        mesh=mesh,
        in_specs=(
            P("ch", "seq"),
            P(),
            P(),
            P(None, "ch", None),
            P(None, "ch"),
            P(),
            P(None, "ch", None),
            P(None, "ch"),
            P(None, "ch"),
            P("ch", "seq"),
        ),
        out_specs=(
            P("ch", "seq"),
            P("ch", "seq"),
            P(None, "ch", None),
            P(None, "ch"),
            P(None, "ch", None),
            P(None, "ch"),
        ),
        check_vma=False,
    )
```

```python
import functools
import math

import jax
import jax.numpy as jnp
import numpy as np
from jax import lax
from jax.experimental import pallas as pl
from jax.experimental.pallas import tpu as pltpu
from jax.sharding import PartitionSpec as P

EPSILON = 1e-05
HIGHEST = lax.Precision.HIGHEST
F32 = jnp.float32
BF16 = jnp.bfloat16

WIDTH = 256
TOTAL = 32768
SEQ = 128
CHUNK = 256
LOCAL = 64
HIDDEN = 64
BANDS = 16
CLIPS = 16
SEND_ROWS = 12
BACK_ROWS = 8


def halves(table):
    high = table.astype(BF16)
    low = (table - high.astype(np.float32)).astype(BF16)
    return high, low


def tables():
    k1 = np.arange(SEQ)[:, None] + 0.25
    s = np.arange(SEQ)[None, :]
    u = np.arange(CHUNK)[None, :]
    first = 2.0 * np.pi * k1 * s / SEQ
    analysis = np.concatenate([np.cos(first), -np.sin(first)], 0).astype(np.float32)
    synthesis = (np.concatenate([np.cos(first), -np.sin(first)], 0).T / TOTAL).astype(np.float32)
    twist = 2.0 * np.pi * k1 * u / TOTAL
    k2 = np.arange(CHUNK)
    second = 2.0 * np.pi * ((k2[:, None] * k2[None, :]) % CHUNK) / CHUNK
    inner = np.concatenate([np.cos(second), np.sin(second)], 1).astype(np.float32)
    return (
        *halves(analysis),
        *halves(synthesis),
        *halves(inner),
        np.cos(twist).astype(np.float32),
        np.sin(twist).astype(np.float32),
    )


def dot(a, b, dims=((1,), (0,)), precision=None):
    return lax.dot_general(a, b, (dims, ((), ())), precision=precision, preferred_element_type=F32)


def split(x):
    high = x.astype(BF16)
    return high, (x - high.astype(F32)).astype(BF16)


def clip_bounds(clip_len, clip_order):
    starts, lengths = [], []
    start = jnp.int32(0)
    for p in range(CLIPS):
        length = clip_len[clip_order[p]]
        starts.append(start)
        lengths.append(length)
        start = start + length
    return starts, lengths


def front_kernel(
    rank, clip_len, clip_order, full, in_proj, out_proj, filt_in, filt_out, decay,
    send, gate_out, grad_out, hidden_out, window_out, scratch,
):
    first = ((0,), (0,))
    inputs = jnp.concatenate([full[128 * j : 128 * j + 64, :] for j in range(4)], 0)
    cotangent = jnp.concatenate([full[128 * j + 64 : 128 * j + 128, :] for j in range(4)], 0)
    raw = dot(in_proj[...], inputs)
    out_grad = dot(out_proj[...], cotangent)
    gate_two = raw[2 * LOCAL :, :]
    gate_out[...] = gate_two
    grad_out[...] = out_grad

    offset = rank[0] * CHUNK
    starts, lengths = clip_bounds(clip_len, clip_order)
    time = offset + lax.broadcasted_iota(jnp.int32, (SEQ, CHUNK), 1)
    place = lax.broadcasted_iota(jnp.int32, (SEQ, CHUNK), 0)
    member = jnp.zeros((SEQ, CHUNK), F32)
    for p in range(CLIPS):
        inside = (time >= starts[p]) & (time < starts[p] + lengths[p]) & (place == p)
        member = jnp.where(inside, 1.0, member)
    wide = inputs.astype(F32)
    squares = jnp.sum(wide * wide, 0, keepdims=True)
    power = dot(jnp.broadcast_to(squares, (8, CHUNK)), member, ((1,), (1,)), HIGHEST)[:1, :]
    high, low = split(power)

    step = offset + lax.broadcasted_iota(jnp.int32, (BANDS, CHUNK), 1)
    band = 1 + lax.broadcasted_iota(jnp.int32, (BANDS, CHUNK), 0)
    phases = ((step * band) & (TOTAL - 1)).astype(F32) * (2.0 * math.pi / TOTAL)
    ramp = (offset + lax.broadcasted_iota(jnp.int32, (8, CHUNK), 1)).astype(F32) * (1.0 / TOTAL)
    first_row = lax.broadcasted_iota(jnp.int32, (8, HIDDEN), 0) == 0
    ramp_weight = jnp.where(first_row, filt_in[:8, :], 0.0)
    hidden = jnp.sin(
        dot(ramp_weight, ramp, first, HIGHEST)
        + dot(filt_in[1 : 1 + BANDS, :], jnp.cos(phases), first, HIGHEST)
        + dot(filt_in[1 + BANDS : 1 + 2 * BANDS, :], jnp.sin(phases), first, HIGHEST)
    )
    hidden_out[...] = hidden
    rows = lax.broadcasted_iota(jnp.int32, (LOCAL, LOCAL), 0)
    columns = lax.broadcasted_iota(jnp.int32, (LOCAL, LOCAL), 1)
    shapes = []
    for i in range(2):
        spread = jnp.broadcast_to(decay[i : i + 1, :], (LOCAL, LOCAL))
        rate = jnp.sum(jnp.where(rows == columns, spread, 0.0), 1, keepdims=True)
        window = jnp.exp(-rate * ramp[:1, :]) * TOTAL ** (-0.5)
        window_out[i * LOCAL : (i + 1) * LOCAL, :] = window
        weights = filt_out[i * LOCAL : (i + 1) * LOCAL, :]
        shapes.append(dot(weights, hidden, precision=HIGHEST) * window)

    arrays = [raw[:LOCAL, :], raw[LOCAL : 2 * LOCAL, :], gate_two * out_grad, *shapes]
    for at, values in enumerate(arrays):
        scratch[pl.ds(2 * at, LOCAL, stride=SEND_ROWS), :] = values[:, :128]
        scratch[pl.ds(2 * at + 1, LOCAL, stride=SEND_ROWS), :] = values[:, 128:]
    for at, values in enumerate([high, low]):
        scratch[pl.ds(10 + at, LOCAL, stride=SEND_ROWS), :] = jnp.broadcast_to(
            values.astype(F32), (LOCAL, 128)
        )
    packed = scratch[...].astype(BF16)
    send[: LOCAL * SEND_ROWS, :] = packed
    send[LOCAL * SEND_ROWS :, :] = packed


def turn(values, count, inner_high, inner_low):
    high, low = split(values)
    product = dot(high, inner_high[...]) + dot(low, inner_high[...]) + dot(high, inner_low[...])
    pieces = []
    for at in range(count):
        real = product[256 * at : 256 * at + 128, :]
        imag = product[256 * at + 128 : 256 * at + 256, :]
        pieces.append((real[:, :256], real[:, 256:], imag[:, :256], imag[:, 256:]))
    return pieces


def to_spectrum(signals, cosines, sines, analysis_high, analysis_low, inner_high, inner_low):
    high, low = split(jnp.concatenate(signals, 1))
    rows = (
        dot(analysis_high[...], high)
        + dot(analysis_high[...], low)
        + dot(analysis_low[...], high)
    )
    twisted = []
    for at in range(len(signals)):
        real = rows[:128, 256 * at : 256 * at + 256]
        imag = rows[128:, 256 * at : 256 * at + 256]
        twisted.append(cosines * real + sines * imag)
        twisted.append(cosines * imag - sines * real)
    pieces = turn(jnp.concatenate(twisted, 0), len(signals), inner_high, inner_low)
    return [(rc + is_, ic - rs) for rc, rs, ic, is_ in pieces]


def to_signal(spectra, cosines, sines, synthesis_high, synthesis_low, inner_high, inner_low):
    stacked = jnp.concatenate([part for pair in spectra for part in pair], 0)
    columns = []
    for rc, rs, ic, is_ in turn(stacked, len(spectra), inner_high, inner_low):
        real = rc - is_
        imag = ic + rs
        columns.append(
            jnp.concatenate([cosines * real - sines * imag, cosines * imag + sines * real], 0)
        )
    high, low = split(jnp.concatenate(columns, 1))
    rows = (
        dot(synthesis_high[...], high)
        + dot(synthesis_high[...], low)
        + dot(synthesis_low[...], high)
    )
    return [rows[:, 256 * at : 256 * at + 256] for at in range(len(spectra))]


def series_kernel(
    rank, clip_len, clip_order, skip_gain, received,
    analysis_high, analysis_low, synthesis_high, synthesis_low, inner_high, inner_low,
    twist_cos, twist_sin, back, scratch, packed,
):
    role = rank[0] // LOCAL
    channel = rank[0] % LOCAL
    forward = role == 0
    skip_one = skip_gain[0, channel]
    skip_two = skip_gain[1, channel]
    scratch[...] = received[...].astype(F32)

    def plane(row):
        return scratch[pl.ds(row, SEQ, stride=SEND_ROWS), :]

    def signal(at):
        return jnp.concatenate([plane(2 * at), plane(2 * at + 1)], 1)

    power = jnp.sum(plane(10) + plane(11), 0, keepdims=True)
    starts, lengths = clip_bounds(clip_len, clip_order)
    time = lax.broadcasted_iota(jnp.int32, (SEQ, CHUNK), 0) * CHUNK + lax.broadcasted_iota(
        jnp.int32, (SEQ, CHUNK), 1
    )
    lane = lax.broadcasted_iota(jnp.int32, (1, 128), 1)
    counts = jnp.ones((1, 128), F32)
    for p in range(CLIPS):
        counts = jnp.where(lane == p, lengths[p].astype(F32), counts)
    inverse_rms = lax.rsqrt(power / (WIDTH * counts) + EPSILON)
    scale = jnp.zeros((SEQ, CHUNK), F32)
    for p in range(CLIPS):
        scale = jnp.where(time >= starts[p], inverse_rms[:, p : p + 1], scale)

    cosines = twist_cos[...]
    sines = twist_sin[...]

    def analyse(signals):
        return to_spectrum(
            signals, cosines, sines, analysis_high, analysis_low, inner_high, inner_low
        )

    def synthesise(parts):
        return to_signal(
            parts, cosines, sines, synthesis_high, synthesis_low, inner_high, inner_low
        )

    def times(a, b, sign):
        return (a[0] * b[0] - sign * (a[1] * b[1]), a[1] * b[0] + sign * (a[0] * b[1]))

    def choose(a, b):
        return jnp.where(forward, a, b)

    def choose_spectrum(a, b):
        return tuple(choose(x, y) for x, y in zip(a, b))

    value = signal(0) * scale
    gate_one = signal(1) * scale
    scaled_two = signal(2) * scale
    value_spec, second_spec, filter_one, filter_two = analyse(
        [value, scaled_two, signal(3), signal(4)]
    )
    carry_one, level_grad = synthesise(
        [times(value_spec, filter_one, 1.0), times(second_spec, filter_two, -1.0)]
    )
    carry_one = carry_one + skip_one * value
    level_grad = level_grad + skip_two * scaled_two
    level_one = gate_one * carry_one
    scaled_one = gate_one * level_grad
    level_spec, first_spec = analyse([level_one, scaled_one])
    sign = choose(jnp.float32(1.0), jnp.float32(-1.0))
    chain, shape_grad = synthesise(
        [
            times(
                choose_spectrum(level_spec, first_spec),
                choose_spectrum(filter_two, filter_one),
                sign,
            ),
            times(
                choose_spectrum(second_spec, first_spec),
                choose_spectrum(level_spec, value_spec),
                -1.0,
            ),
        ]
    )
    source = choose(level_one, scaled_one)
    chain = scale * (chain + choose(skip_two, skip_one) * source)
    gate_grad = scale * (level_grad * carry_one)
    partner = choose(scaled_two, value)
    skip_grad = jnp.sum(jnp.sum(source * partner, 0, keepdims=True), 1, keepdims=True)
    high, low = split(skip_grad)
    mid = low.astype(F32)
    low = skip_grad - high.astype(F32) - mid
    high = high.astype(F32)
    skip_row = jnp.where(
        lane == 0, high, jnp.where(lane == 1, mid, jnp.where(lane == 2, low, 0.0))
    )
    for at, values in enumerate([chain, shape_grad, gate_grad]):
        packed[pl.ds(2 * at, SEQ, stride=BACK_ROWS), :] = values[:, :128]
        packed[pl.ds(2 * at + 1, SEQ, stride=BACK_ROWS), :] = values[:, 128:]
    packed[pl.ds(6, SEQ, stride=BACK_ROWS), :] = jnp.broadcast_to(skip_row, (SEQ, 128))
    packed[pl.ds(7, SEQ, stride=BACK_ROWS), :] = jnp.zeros((SEQ, 128), F32)
    back[...] = packed[...].astype(BF16)


def back_kernel(
    place, received, full, in_proj, out_proj, gate_in, grad_in, hidden, window,
    given, kept, weights, skip_out, scratch,
):
    scratch[...] = received[...].astype(F32)

    def plane(role, row):
        return scratch[pl.ds(role * LOCAL * BACK_ROWS + row, LOCAL, stride=BACK_ROWS), :]

    def signal(role, at):
        return jnp.concatenate([plane(role, 2 * at), plane(role, 2 * at + 1)], 1)

    carry = signal(0, 0)
    gated = (gate_in[...] * carry).astype(BF16)
    scaled_grad = jnp.concatenate(
        [signal(1, 0).astype(BF16), signal(1, 2).astype(BF16), (grad_in[...] * carry).astype(BF16)],
        0,
    )
    inputs = jnp.concatenate([full[128 * j : 128 * j + 64, :] for j in range(4)], 0)
    cotangent = jnp.concatenate([full[128 * j + 64 : 128 * j + 128, :] for j in range(4)], 0)
    first = ((0,), (0,))
    last = ((1,), (1,))
    mixed = dot(out_proj[...], gated, first)
    grad_inputs = dot(in_proj[...], scaled_grad, first)
    even = place[0] % 2 == 0
    for at in range(2):
        for to, values in enumerate([mixed, grad_inputs]):
            low = values[128 * at : 128 * at + 64, :]
            high = values[128 * at + 64 : 128 * at + 128, :]
            rows = slice(128 * at + 64 * to, 128 * at + 64 * to + 64)
            given[rows, :] = jnp.where(even, high, low).astype(BF16)
            kept[rows, :] = jnp.where(even, low, high)
    in_weight = dot(scaled_grad, inputs, last)
    out_weight = dot(gated, cotangent, last)
    shape_grads = jnp.concatenate([signal(1, 1), signal(0, 1)], 0) * window[...]
    padded = jnp.concatenate([hidden[...], jnp.zeros((LOCAL, CHUNK), F32)], 0)
    filter_grad = dot(shape_grads, padded, last, HIGHEST)
    for at in range(32):
        source, row = (in_weight, at) if at < 24 else (out_weight, at - 24)
        for half in range(2):
            weights[2 * at + half] = source[
                8 * row : 8 * row + 8, 128 * half : 128 * half + 128
            ].astype(BF16)
    for at in range(16):
        weights[64 + at] = filter_grad[8 * at : 8 * at + 8, :].astype(BF16)
    for at in range(80, 128):
        weights[at] = jnp.zeros((8, 128), BF16)
    lane = lax.broadcasted_iota(jnp.int32, (8, 128), 1)
    pick = jnp.where(lane < 3, 1.0, 0.0).astype(BF16)
    for role in range(2):
        total = dot(pick, plane(role, 6).astype(BF16), last)[:1, :]
        skip_out[1 - role : 2 - role, :] = total * TOTAL ** (-0.5)


def core_kernel(place, received, kept, given, left):
    total = kept[...] + received[...].astype(F32)
    near = place[0] < 2
    given[...] = jnp.where(near, total[128:, :], total[:128, :]).astype(BF16)
    left[...] = jnp.where(near, total[:128, :], total[128:, :])


def chip_kernel(received, left, mixed, grad_inputs):
    total = (left[...] + received[...].astype(F32)).astype(BF16)
    mixed[...] = total[:64, :]
    grad_inputs[...] = total[64:, :]


def sum_kernel(received, spread):
    total = jnp.sum(received[...].astype(F32), 0, keepdims=True) * TOTAL ** (-0.5)
    spread[...] = jnp.broadcast_to(total, (SEQ, 8, 128)).astype(BF16)


def last_kernel(received, in_weight, out_weight, filter_grad):
    for at in range(32):
        target, row = (in_weight, at) if at < 24 else (out_weight, at - 24)
        for half in range(2):
            target[8 * row : 8 * row + 8, 128 * half : 128 * half + 128] = received[
                2 * at + half
            ].astype(F32)
    for at in range(16):
        filter_grad[8 * at : 8 * at + 8, :] = received[64 + at].astype(F32)[:, :HIDDEN]


def call(kernel, name, outs, scalars, arrays, scratch=()):
    def vmem():
        return pl.BlockSpec(memory_space=pltpu.VMEM)

    return pl.pallas_call(
        kernel,
        name=name,
        out_shape=[jax.ShapeDtypeStruct(shape, kind) for shape, kind in outs],
        in_specs=[pl.BlockSpec(memory_space=pltpu.SMEM)] * scalars + [vmem() for _ in range(arrays)],
        out_specs=[vmem() for _ in outs],
        scratch_shapes=[pltpu.VMEM(shape, F32) for shape in scratch],
        compiler_params=pltpu.CompilerParams(vmem_limit_bytes=32 * 1024 * 1024),
    )


def front():
    return call(
        front_kernel,
        "project",
        [
            ((SEQ * SEND_ROWS, 128), BF16),
            ((LOCAL, CHUNK), F32),
            ((LOCAL, CHUNK), F32),
            ((HIDDEN, CHUNK), F32),
            ((2 * LOCAL, CHUNK), F32),
        ],
        3,
        6,
        [(LOCAL * SEND_ROWS, 128)],
    )


def series():
    return call(
        series_kernel,
        "convolve",
        [((SEQ * BACK_ROWS, 128), BF16)],
        4,
        9,
        [(SEQ * SEND_ROWS, 128), (SEQ * BACK_ROWS, 128)],
    )


def rear():
    return call(
        back_kernel,
        "weigh",
        [
            ((256, CHUNK), BF16),
            ((256, CHUNK), F32),
            ((SEQ, 8, 128), BF16),
            ((2, LOCAL), F32),
        ],
        1,
        8,
        [(SEQ * BACK_ROWS, 128)],
    )


def core_sum():
    return call(core_kernel, "add_core", [((128, CHUNK), BF16), ((128, CHUNK), F32)], 1, 2)


def chip_sum():
    return call(chip_kernel, "add_chip", [((64, CHUNK), BF16), ((64, CHUNK), BF16)], 0, 2)


def total():
    return call(sum_kernel, "add_up", [((SEQ, 8, 128), BF16)], 0, 1)


def finish():
    return call(
        last_kernel,
        "unpack",
        [((3 * LOCAL, WIDTH), F32), ((LOCAL, WIDTH), F32), ((2 * LOCAL, HIDDEN), F32)],
        0,
        1,
    )


def swap(values):
    return lax.all_to_all(values, "seq", split_axis=0, concat_axis=0, tiled=True)


def shards(
    inputs,
    clip_len,
    clip_order,
    in_proj,
    out_proj,
    filt_in,
    filt_out,
    decay_rate,
    skip_gain,
    cotangent,
):
    rank = lax.axis_index("seq").astype(jnp.int32).reshape(1)
    place = lax.axis_index("ch").astype(jnp.int32).reshape(1)
    in_rows = in_proj.reshape(3 * LOCAL, WIDTH)
    out_rows = out_proj.T
    full = lax.all_gather(jnp.concatenate([inputs, cotangent], 0), "ch", axis=0, tiled=True)
    send, gate_two, out_grad, hidden, window = front()(
        rank, clip_len, clip_order, full, in_rows, out_rows, filt_in,
        filt_out.reshape(2 * LOCAL, HIDDEN), decay_rate,
    )
    received = swap(send.reshape(SEQ * SEND_ROWS // 4, 4, 128)).reshape(SEQ * SEND_ROWS, 128)
    (back,) = series()(
        rank, clip_len, clip_order, skip_gain, received, *[jnp.asarray(x) for x in tables()]
    )
    returned = swap(back.reshape(SEQ, BACK_ROWS, 128)).reshape(SEQ * BACK_ROWS, 128)
    given, kept, weights, grad_skip = rear()(
        place, returned, full, in_rows, out_rows, gate_two, out_grad, hidden, window
    )
    over_cores = lax.ppermute(given, "ch", [(0, 1), (1, 0), (2, 3), (3, 2)])
    given, left = core_sum()(place, over_cores, kept)
    (spread,) = total()(swap(weights))
    spread, given = lax.optimization_barrier((spread, given))
    over_chips = lax.ppermute(given, "ch", [(0, 2), (2, 0), (1, 3), (3, 1)])
    mixed, grad_inputs = chip_sum()(over_chips, left)
    in_weight, out_weight, filter_grad = finish()(swap(spread))
    return (
        mixed,
        grad_inputs,
        in_weight.reshape(3, LOCAL, WIDTH),
        out_weight.T,
        filter_grad.reshape(2, LOCAL, HIDDEN),
        grad_skip,
    )


def solution(mesh):
    return jax.shard_map(
        shards,
        mesh=mesh,
        in_specs=(
            P("ch", "seq"),
            P(),
            P(),
            P(None, "ch", None),
            P(None, "ch"),
            P(),
            P(None, "ch", None),
            P(None, "ch"),
            P(None, "ch"),
            P("ch", "seq"),
        ),
        out_specs=(
            P("ch", "seq"),
            P("ch", "seq"),
            P(None, "ch", None),
            P(None, "ch"),
            P(None, "ch", None),
            P(None, "ch"),
        ),
        check_vma=False,
    )
```

```python
import functools
import math

import jax
import jax.numpy as jnp
import numpy as np
from jax import lax
from jax.experimental import pallas as pl
from jax.experimental.pallas import tpu as pltpu
from jax.sharding import PartitionSpec as P

EPSILON = 1e-05
HIGHEST = lax.Precision.HIGHEST
F32 = jnp.float32
BF16 = jnp.bfloat16

WIDTH = 256
TOTAL = 32768
SEQ = 128
CHUNK = 256
LOCAL = 64
HIDDEN = 64
BANDS = 16
CLIPS = 16
SEND_ROWS = 12
BACK_ROWS = 6


def tables():
    k1 = np.arange(SEQ)[:, None] + 0.25
    s = np.arange(SEQ)[None, :]
    u = np.arange(CHUNK)[None, :]
    first = 2.0 * np.pi * k1 * s / SEQ
    analysis = np.concatenate([np.cos(first), -np.sin(first)], 0).astype(np.float32)
    synthesis = (np.concatenate([np.cos(first), -np.sin(first)], 0).T / TOTAL).astype(np.float32)
    twist = 2.0 * np.pi * k1 * u / TOTAL
    k2 = np.arange(CHUNK)
    second = 2.0 * np.pi * ((k2[:, None] * k2[None, :]) % CHUNK) / CHUNK
    inner = np.concatenate([np.cos(second), np.sin(second)], 1).astype(np.float32)
    return (
        analysis.astype(BF16),
        synthesis.astype(BF16),
        inner.astype(BF16),
        np.cos(twist).astype(np.float32),
        np.sin(twist).astype(np.float32),
    )


def dot(a, b, dims=((1,), (0,)), precision=None):
    return lax.dot_general(a, b, (dims, ((), ())), precision=precision, preferred_element_type=F32)


def split(x):
    high = x.astype(BF16)
    return high, (x - high.astype(F32)).astype(BF16)


def clip_bounds(clip_len, clip_order):
    starts, lengths = [], []
    start = jnp.int32(0)
    for p in range(CLIPS):
        length = clip_len[clip_order[p]]
        starts.append(start)
        lengths.append(length)
        start = start + length
    return starts, lengths


def front_kernel(
    rank, clip_len, clip_order, full, in_proj, out_proj, filt_in, filt_out, decay,
    send, gate_out, grad_out, hidden_out, window_out, scratch,
):
    first = ((0,), (0,))
    inputs = jnp.concatenate([full[128 * j : 128 * j + 64, :] for j in range(4)], 0)
    cotangent = jnp.concatenate([full[128 * j + 64 : 128 * j + 128, :] for j in range(4)], 0)
    raw = dot(in_proj[...], inputs)
    out_grad = dot(out_proj[...], cotangent)
    gate_two = raw[2 * LOCAL :, :]
    gate_out[...] = gate_two
    grad_out[...] = out_grad

    offset = rank[0] * CHUNK
    starts, lengths = clip_bounds(clip_len, clip_order)
    time = offset + lax.broadcasted_iota(jnp.int32, (SEQ, CHUNK), 1)
    place = lax.broadcasted_iota(jnp.int32, (SEQ, CHUNK), 0)
    member = jnp.zeros((SEQ, CHUNK), F32)
    for p in range(CLIPS):
        inside = (time >= starts[p]) & (time < starts[p] + lengths[p]) & (place == p)
        member = jnp.where(inside, 1.0, member)
    wide = inputs.astype(F32)
    squares = jnp.sum(wide * wide, 0, keepdims=True)
    power = dot(jnp.broadcast_to(squares, (8, CHUNK)), member, ((1,), (1,)), HIGHEST)[:1, :]
    high, low = split(power)

    step = offset + lax.broadcasted_iota(jnp.int32, (BANDS, CHUNK), 1)
    band = 1 + lax.broadcasted_iota(jnp.int32, (BANDS, CHUNK), 0)
    phases = ((step * band) & (TOTAL - 1)).astype(F32) * (2.0 * math.pi / TOTAL)
    ramp = (offset + lax.broadcasted_iota(jnp.int32, (8, CHUNK), 1)).astype(F32) * (1.0 / TOTAL)
    first_row = lax.broadcasted_iota(jnp.int32, (8, HIDDEN), 0) == 0
    ramp_weight = jnp.where(first_row, filt_in[:8, :], 0.0)
    hidden = jnp.sin(
        dot(ramp_weight, ramp, first, HIGHEST)
        + dot(filt_in[1 : 1 + BANDS, :], jnp.cos(phases), first, HIGHEST)
        + dot(filt_in[1 + BANDS : 1 + 2 * BANDS, :], jnp.sin(phases), first, HIGHEST)
    )
    hidden_out[...] = hidden
    rows = lax.broadcasted_iota(jnp.int32, (LOCAL, LOCAL), 0)
    columns = lax.broadcasted_iota(jnp.int32, (LOCAL, LOCAL), 1)
    shapes = []
    for i in range(2):
        spread = jnp.broadcast_to(decay[i : i + 1, :], (LOCAL, LOCAL))
        rate = jnp.sum(jnp.where(rows == columns, spread, 0.0), 1, keepdims=True)
        window = jnp.exp(-rate * ramp[:1, :]) * TOTAL ** (-0.5)
        window_out[i * LOCAL : (i + 1) * LOCAL, :] = window
        weights = filt_out[i * LOCAL : (i + 1) * LOCAL, :]
        shapes.append(dot(weights, hidden, precision=HIGHEST) * window)

    arrays = [raw[:LOCAL, :], raw[LOCAL : 2 * LOCAL, :], gate_two * out_grad, *shapes]
    for at, values in enumerate(arrays):
        scratch[pl.ds(2 * at, LOCAL, stride=SEND_ROWS), :] = values[:, :128]
        scratch[pl.ds(2 * at + 1, LOCAL, stride=SEND_ROWS), :] = values[:, 128:]
    for at, values in enumerate([high, low]):
        scratch[pl.ds(10 + at, LOCAL, stride=SEND_ROWS), :] = jnp.broadcast_to(
            values.astype(F32), (LOCAL, 128)
        )
    packed = scratch[...].astype(BF16)
    send[: LOCAL * SEND_ROWS, :] = packed
    send[LOCAL * SEND_ROWS :, :] = packed


def turn(values, count, inner):
    product = dot(values.astype(BF16), inner[...])
    pieces = []
    for at in range(count):
        real = product[256 * at : 256 * at + 128, :]
        imag = product[256 * at + 128 : 256 * at + 256, :]
        pieces.append((real[:, :256], real[:, 256:], imag[:, :256], imag[:, 256:]))
    return pieces


def to_spectrum(signals, cosines, sines, analysis, inner):
    rows = dot(analysis[...], jnp.concatenate(signals, 1).astype(BF16))
    twisted = []
    for at in range(len(signals)):
        real = rows[:128, 256 * at : 256 * at + 256]
        imag = rows[128:, 256 * at : 256 * at + 256]
        twisted.append(cosines * real + sines * imag)
        twisted.append(cosines * imag - sines * real)
    pieces = turn(jnp.concatenate(twisted, 0), len(signals), inner)
    return [(rc + is_, ic - rs) for rc, rs, ic, is_ in pieces]


def to_signal(spectra, cosines, sines, synthesis, inner):
    stacked = jnp.concatenate([part for pair in spectra for part in pair], 0)
    columns = []
    for rc, rs, ic, is_ in turn(stacked, len(spectra), inner):
        real = rc - is_
        imag = ic + rs
        columns.append(
            jnp.concatenate([cosines * real - sines * imag, cosines * imag + sines * real], 0)
        )
    rows = dot(synthesis[...], jnp.concatenate(columns, 1).astype(BF16))
    return [rows[:, 256 * at : 256 * at + 256] for at in range(len(spectra))]


def series_kernel(
    rank, clip_len, clip_order, skip_gain, received,
    analysis, synthesis, inner, twist_cos, twist_sin, back, scratch, packed,
):
    role = rank[0] // LOCAL
    channel = rank[0] % LOCAL
    forward = role == 0
    skip_one = skip_gain[0, channel]
    skip_two = skip_gain[1, channel]
    scratch[...] = received[...].astype(F32)

    def plane(row):
        return scratch[pl.ds(row, SEQ, stride=SEND_ROWS), :]

    def signal(at):
        return jnp.concatenate([plane(2 * at), plane(2 * at + 1)], 1)

    power = jnp.sum(plane(10) + plane(11), 0, keepdims=True)
    starts, lengths = clip_bounds(clip_len, clip_order)
    time = lax.broadcasted_iota(jnp.int32, (SEQ, CHUNK), 0) * CHUNK + lax.broadcasted_iota(
        jnp.int32, (SEQ, CHUNK), 1
    )
    lane = lax.broadcasted_iota(jnp.int32, (1, 128), 1)
    counts = jnp.ones((1, 128), F32)
    for p in range(CLIPS):
        counts = jnp.where(lane == p, lengths[p].astype(F32), counts)
    inverse_rms = lax.rsqrt(power / (WIDTH * counts) + EPSILON)
    scale = jnp.zeros((SEQ, CHUNK), F32)
    for p in range(CLIPS):
        scale = jnp.where(time >= starts[p], inverse_rms[:, p : p + 1], scale)

    cosines = twist_cos[...]
    sines = twist_sin[...]

    def analyse(signals):
        return to_spectrum(signals, cosines, sines, analysis, inner)

    def synthesise(parts):
        return to_signal(parts, cosines, sines, synthesis, inner)

    def times(a, b, sign):
        return (a[0] * b[0] - sign * (a[1] * b[1]), a[1] * b[0] + sign * (a[0] * b[1]))

    def choose(a, b):
        return jnp.where(forward, a, b)

    def choose_spectrum(a, b):
        return tuple(choose(x, y) for x, y in zip(a, b))

    value = signal(0) * scale
    gate_one = signal(1) * scale
    scaled_two = signal(2) * scale
    value_spec, second_spec, filter_one, filter_two = analyse(
        [value, scaled_two, signal(3), signal(4)]
    )
    carry_one, level_grad = synthesise(
        [times(value_spec, filter_one, 1.0), times(second_spec, filter_two, -1.0)]
    )
    carry_one = carry_one + skip_one * value
    level_grad = level_grad + skip_two * scaled_two
    level_one = gate_one * carry_one
    scaled_one = gate_one * level_grad
    level_spec, first_spec = analyse([level_one, scaled_one])
    sign = choose(jnp.float32(1.0), jnp.float32(-1.0))
    chain, shape_grad = synthesise(
        [
            times(
                choose_spectrum(level_spec, first_spec),
                choose_spectrum(filter_two, filter_one),
                sign,
            ),
            times(
                choose_spectrum(second_spec, first_spec),
                choose_spectrum(level_spec, value_spec),
                -1.0,
            ),
        ]
    )
    source = choose(level_one, scaled_one)
    chain = scale * (chain + choose(skip_two, skip_one) * source)
    gate_grad = scale * (level_grad * carry_one)
    partner = choose(scaled_two, value)
    skip_grad = jnp.sum(jnp.sum(source * partner, 0, keepdims=True), 1, keepdims=True)
    high, low = split(skip_grad)
    mid = low.astype(F32)
    low = skip_grad - high.astype(F32) - mid
    high = high.astype(F32)
    skip_row = jnp.where(
        lane == 0, high, jnp.where(lane == 1, mid, jnp.where(lane == 2, low, 0.0))
    )
    for at, values in enumerate([chain, shape_grad]):
        packed[pl.ds(2 * at, SEQ, stride=BACK_ROWS), :] = values[:, :128]
        packed[pl.ds(2 * at + 1, SEQ, stride=BACK_ROWS), :] = values[:, 128:]
    packed[pl.ds(4, SEQ, stride=BACK_ROWS), :] = choose(gate_grad[:, :128], gate_grad[:, 128:])
    packed[pl.ds(5, SEQ, stride=BACK_ROWS), :] = jnp.broadcast_to(skip_row, (SEQ, 128))
    back[...] = packed[...].astype(BF16)


def back_kernel(
    place, received, full, in_proj, out_proj, gate_in, grad_in, hidden, window,
    given, kept, weights, skip_out, scratch, packed,
):
    scratch[...] = received[...].astype(F32)

    def plane(role, row):
        return scratch[pl.ds(role * LOCAL * BACK_ROWS + row, LOCAL, stride=BACK_ROWS), :]

    def signal(role, at):
        return jnp.concatenate([plane(role, 2 * at), plane(role, 2 * at + 1)], 1)

    carry = signal(0, 0)
    gated = (gate_in[...] * carry).astype(BF16)
    scaled_grad = jnp.concatenate(
        [
            signal(1, 0).astype(BF16),
            jnp.concatenate([plane(0, 4), plane(1, 4)], 1).astype(BF16),
            (grad_in[...] * carry).astype(BF16),
        ],
        0,
    )
    inputs = jnp.concatenate([full[128 * j : 128 * j + 64, :] for j in range(4)], 0)
    cotangent = jnp.concatenate([full[128 * j + 64 : 128 * j + 128, :] for j in range(4)], 0)
    first = ((0,), (0,))
    last = ((1,), (1,))
    mixed = dot(out_proj[...], gated, first)
    grad_inputs = dot(in_proj[...], scaled_grad, first)
    even = place[0] % 2 == 0
    for at in range(2):
        for to, values in enumerate([mixed, grad_inputs]):
            low = values[128 * at : 128 * at + 64, :]
            high = values[128 * at + 64 : 128 * at + 128, :]
            rows = slice(128 * at + 64 * to, 128 * at + 64 * to + 64)
            given[rows, :] = jnp.where(even, high, low).astype(BF16)
            kept[rows, :] = jnp.where(even, low, high)
    in_weight = dot(scaled_grad, inputs, last)
    out_weight = dot(gated, cotangent, last)
    shape_grads = jnp.concatenate([signal(1, 1), signal(0, 1)], 0) * window[...]
    padded = jnp.concatenate([hidden[...], jnp.zeros((LOCAL, CHUNK), F32)], 0)
    filter_grad = dot(shape_grads, padded, last, HIGHEST)
    rows = [
        in_weight[:128, :128],
        jnp.concatenate([in_weight[128:, :128], in_weight[:64, 128:]], 0),
        in_weight[64:, 128:],
        jnp.concatenate([out_weight[:, :128], out_weight[:, 128:]], 0),
        filter_grad,
        jnp.zeros((SEQ, 128), F32),
    ]
    for at, values in enumerate(rows):
        packed[pl.ds(at, SEQ, stride=BACK_ROWS), :] = values
    weights[...] = packed[...].astype(BF16)
    lane = lax.broadcasted_iota(jnp.int32, (8, 128), 1)
    pick = jnp.where(lane < 3, 1.0, 0.0).astype(BF16)
    for role in range(2):
        total = dot(pick, plane(role, 5).astype(BF16), last)[:1, :]
        skip_out[1 - role : 2 - role, :] = total * TOTAL ** (-0.5)


def core_kernel(place, received, kept, given, left):
    total = kept[...] + received[...].astype(F32)
    near = place[0] < 2
    given[...] = jnp.where(near, total[128:, :], total[:128, :]).astype(BF16)
    left[...] = jnp.where(near, total[:128, :], total[128:, :])


def chip_kernel(received, left, mixed, grad_inputs):
    total = (left[...] + received[...].astype(F32)).astype(BF16)
    mixed[...] = total[:64, :]
    grad_inputs[...] = total[64:, :]


def sum_kernel(received, spread):
    four = 4 * BACK_ROWS
    parts = jnp.sum(received[...].astype(F32).reshape(SEQ // 4, four, 128), 0)
    total = sum(parts[BACK_ROWS * at : BACK_ROWS * at + BACK_ROWS, :] for at in range(4))
    total = jnp.concatenate([total * TOTAL ** (-0.5)] * 4, 0)
    total = jnp.broadcast_to(total[None], (SEQ // 4, four, 128)).reshape(SEQ * BACK_ROWS, 128)
    spread[...] = total.astype(BF16)


def last_kernel(received, in_weight, out_weight, filter_grad, scratch):
    scratch[...] = received[...].astype(F32)
    rows = [scratch[pl.ds(at, SEQ, stride=BACK_ROWS), :] for at in range(5)]
    in_weight[:128, :128] = rows[0]
    in_weight[128:, :128] = rows[1][:64, :]
    in_weight[:64, 128:] = rows[1][64:, :]
    in_weight[64:, 128:] = rows[2]
    out_weight[:, :128] = rows[3][:64, :]
    out_weight[:, 128:] = rows[3][64:, :]
    filter_grad[...] = rows[4][:, :HIDDEN]


def call(kernel, name, outs, scalars, arrays, scratch=()):
    def vmem():
        return pl.BlockSpec(memory_space=pltpu.VMEM)

    return pl.pallas_call(
        kernel,
        name=name,
        out_shape=[jax.ShapeDtypeStruct(shape, kind) for shape, kind in outs],
        in_specs=[pl.BlockSpec(memory_space=pltpu.SMEM)] * scalars + [vmem() for _ in range(arrays)],
        out_specs=[vmem() for _ in outs],
        scratch_shapes=[pltpu.VMEM(shape, F32) for shape in scratch],
        compiler_params=pltpu.CompilerParams(vmem_limit_bytes=32 * 1024 * 1024),
    )


def front():
    return call(
        front_kernel,
        "project",
        [
            ((SEQ * SEND_ROWS, 128), BF16),
            ((LOCAL, CHUNK), F32),
            ((LOCAL, CHUNK), F32),
            ((HIDDEN, CHUNK), F32),
            ((2 * LOCAL, CHUNK), F32),
        ],
        3,
        6,
        [(LOCAL * SEND_ROWS, 128)],
    )


def series():
    return call(
        series_kernel,
        "convolve",
        [((SEQ * BACK_ROWS, 128), BF16)],
        4,
        6,
        [(SEQ * SEND_ROWS, 128), (SEQ * BACK_ROWS, 128)],
    )


def rear():
    return call(
        back_kernel,
        "weigh",
        [
            ((256, CHUNK), BF16),
            ((256, CHUNK), F32),
            ((SEQ * BACK_ROWS, 128), BF16),
            ((2, LOCAL), F32),
        ],
        1,
        8,
        [(SEQ * BACK_ROWS, 128), (SEQ * BACK_ROWS, 128)],
    )


def core_sum():
    return call(core_kernel, "add_core", [((128, CHUNK), BF16), ((128, CHUNK), F32)], 1, 2)


def chip_sum():
    return call(chip_kernel, "add_chip", [((64, CHUNK), BF16), ((64, CHUNK), BF16)], 0, 2)


def total():
    return call(sum_kernel, "add_up", [((SEQ * BACK_ROWS, 128), BF16)], 0, 1)


def finish():
    return call(
        last_kernel,
        "unpack",
        [((3 * LOCAL, WIDTH), F32), ((LOCAL, WIDTH), F32), ((2 * LOCAL, HIDDEN), F32)],
        0,
        1,
        [(SEQ * BACK_ROWS, 128)],
    )


def swap(values, group):
    tiles = values.reshape(values.shape[0] // group, group, 128)
    tiles = lax.all_to_all(tiles, "seq", split_axis=0, concat_axis=0, tiled=True)
    return tiles.reshape(values.shape)


def shards(
    inputs,
    clip_len,
    clip_order,
    in_proj,
    out_proj,
    filt_in,
    filt_out,
    decay_rate,
    skip_gain,
    cotangent,
):
    rank = lax.axis_index("seq").astype(jnp.int32).reshape(1)
    place = lax.axis_index("ch").astype(jnp.int32).reshape(1)
    rank, place = lax.optimization_barrier((rank, place))
    in_rows = in_proj.reshape(3 * LOCAL, WIDTH)
    out_rows = out_proj.T
    full = lax.all_gather(jnp.concatenate([inputs, cotangent], 0), "ch", axis=0, tiled=True)
    send, gate_two, out_grad, hidden, window = front()(
        rank, clip_len, clip_order, full, in_rows, out_rows, filt_in,
        filt_out.reshape(2 * LOCAL, HIDDEN), decay_rate,
    )
    received = swap(send, 4)
    (back,) = series()(
        rank, clip_len, clip_order, skip_gain, received, *[jnp.asarray(x) for x in tables()]
    )
    returned = swap(back, 2)
    given, kept, weights, grad_skip = rear()(
        place, returned, full, in_rows, out_rows, gate_two, out_grad, hidden, window
    )
    over_cores = lax.ppermute(given, "ch", [(0, 1), (1, 0), (2, 3), (3, 2)])
    given, left = core_sum()(place, over_cores, kept)
    (spread,) = total()(swap(weights, 2))
    spread, given = lax.optimization_barrier((spread, given))
    over_chips = lax.ppermute(given, "ch", [(0, 2), (2, 0), (1, 3), (3, 1)])
    mixed, grad_inputs = chip_sum()(over_chips, left)
    in_weight, out_weight, filter_grad = finish()(swap(spread, 2))
    return (
        mixed,
        grad_inputs,
        in_weight.reshape(3, LOCAL, WIDTH),
        out_weight.T,
        filter_grad.reshape(2, LOCAL, HIDDEN),
        grad_skip,
    )


def solution(mesh):
    return jax.shard_map(
        shards,
        mesh=mesh,
        in_specs=(
            P("ch", "seq"),
            P(),
            P(),
            P(None, "ch", None),
            P(None, "ch"),
            P(),
            P(None, "ch", None),
            P(None, "ch"),
            P(None, "ch"),
            P("ch", "seq"),
        ),
        out_specs=(
            P("ch", "seq"),
            P("ch", "seq"),
            P(None, "ch", None),
            P(None, "ch"),
            P(None, "ch", None),
            P(None, "ch"),
        ),
        check_vma=False,
    )
```

```python
import functools
import math

import jax
import jax.numpy as jnp
import numpy as np
from jax import lax
from jax.experimental import pallas as pl
from jax.experimental.pallas import tpu as pltpu
from jax.sharding import PartitionSpec as P

EPSILON = 1e-05
HIGHEST = lax.Precision.HIGHEST
F32 = jnp.float32
BF16 = jnp.bfloat16

WIDTH = 256
TOTAL = 32768
SEQ = 128
CHUNK = 256
LOCAL = 64
HIDDEN = 64
BANDS = 16
CLIPS = 16
SEND_ROWS = 12
BACK_ROWS = 12
PART_ROWS = 10
PARTS = 64


def tables():
    k1 = np.arange(SEQ)[:, None] + 0.25
    s = np.arange(SEQ)[None, :]
    u = np.arange(CHUNK)[None, :]
    first = 2.0 * np.pi * k1 * s / SEQ
    analysis = np.concatenate([np.cos(first), -np.sin(first)], 0).astype(np.float32)
    synthesis = (np.concatenate([np.cos(first), -np.sin(first)], 0).T / TOTAL).astype(np.float32)
    twist = 2.0 * np.pi * k1 * u / TOTAL
    k2 = np.arange(CHUNK)
    second = 2.0 * np.pi * ((k2[:, None] * k2[None, :]) % CHUNK) / CHUNK
    inner = np.concatenate([np.cos(second), np.sin(second)], 1).astype(np.float32)
    return (
        analysis.astype(BF16),
        synthesis.astype(BF16),
        inner.astype(BF16),
        np.cos(twist).astype(np.float32),
        np.sin(twist).astype(np.float32),
    )


def dot(a, b, dims=((1,), (0,)), precision=None):
    return lax.dot_general(a, b, (dims, ((), ())), precision=precision, preferred_element_type=F32)


def split(x):
    high = x.astype(BF16)
    return high, (x - high.astype(F32)).astype(BF16)


def to_column(row, count):
    shape = (count, count)
    rows = lax.broadcasted_iota(jnp.int32, shape, 0)
    columns = lax.broadcasted_iota(jnp.int32, shape, 1)
    spread = jnp.broadcast_to(row, shape)
    return jnp.sum(jnp.where(rows == columns, spread, jnp.zeros_like(spread)), 1, keepdims=True)


def clip_bounds(clip_len, clip_order):
    shape = (CLIPS, CLIPS)
    rows = lax.broadcasted_iota(jnp.int32, shape, 0)
    columns = lax.broadcasted_iota(jnp.int32, shape, 1)
    sizes = to_column(clip_len.astype(F32), CLIPS)
    lengths = jnp.sum(jnp.where(rows == clip_order, sizes, 0.0), 0, keepdims=True)
    starts = jnp.sum(
        jnp.where(rows < columns, to_column(lengths, CLIPS), 0.0), 0, keepdims=True
    )
    return starts, lengths


def front_kernel(
    rank, clip_len, clip_order, skip_gain, full, in_proj, out_proj, filt_in, filt_out, decay,
    send, gate_out, grad_out, hidden_out, window_out, notes, scratch,
):
    first = ((0,), (0,))
    inputs = jnp.concatenate([full[128 * j : 128 * j + 64, :] for j in range(4)], 0)
    cotangent = jnp.concatenate([full[128 * j + 64 : 128 * j + 128, :] for j in range(4)], 0)
    raw = dot(in_proj[...], inputs)
    out_grad = dot(out_proj[...], cotangent)
    gate_two = raw[2 * LOCAL :, :]
    gate_out[...] = gate_two
    grad_out[...] = out_grad

    offset = rank[0] * CHUNK
    starts, lengths = clip_bounds(clip_len[...], clip_order[...])
    begin = to_column(starts, CLIPS)
    end = begin + to_column(lengths, CLIPS)
    time = (offset + lax.broadcasted_iota(jnp.int32, (CLIPS, CHUNK), 1)).astype(F32)
    member = jnp.where((time >= begin) & (time < end), 1.0, 0.0)
    member = jnp.concatenate([member, jnp.zeros((128 - CLIPS, CHUNK), F32)], 0)
    wide = inputs.astype(F32)
    squares = jnp.sum(wide * wide, 0, keepdims=True)
    power = dot(jnp.broadcast_to(squares, (8, CHUNK)), member, ((1,), (1,)), HIGHEST)[:1, :]
    high, low = split(power)

    step = offset + lax.broadcasted_iota(jnp.int32, (BANDS, CHUNK), 1)
    band = 1 + lax.broadcasted_iota(jnp.int32, (BANDS, CHUNK), 0)
    phases = ((step * band) & (TOTAL - 1)).astype(F32) * (2.0 * math.pi / TOTAL)
    ramp = (offset + lax.broadcasted_iota(jnp.int32, (8, CHUNK), 1)).astype(F32) * (1.0 / TOTAL)
    first_row = lax.broadcasted_iota(jnp.int32, (8, HIDDEN), 0) == 0
    ramp_weight = jnp.where(first_row, filt_in[:8, :], 0.0)
    hidden = jnp.sin(
        dot(ramp_weight, ramp, first, HIGHEST)
        + dot(filt_in[1 : 1 + BANDS, :], jnp.cos(phases), first, HIGHEST)
        + dot(filt_in[1 + BANDS : 1 + 2 * BANDS, :], jnp.sin(phases), first, HIGHEST)
    )
    hidden_out[...] = hidden
    rows = lax.broadcasted_iota(jnp.int32, (LOCAL, LOCAL), 0)
    columns = lax.broadcasted_iota(jnp.int32, (LOCAL, LOCAL), 1)
    shapes = []
    for i in range(2):
        spread = jnp.broadcast_to(decay[i : i + 1, :], (LOCAL, LOCAL))
        rate = jnp.sum(jnp.where(rows == columns, spread, 0.0), 1, keepdims=True)
        window = jnp.exp(-rate * ramp[:1, :]) * TOTAL ** (-0.5)
        window_out[i * LOCAL : (i + 1) * LOCAL, :] = window
        weights = filt_out[i * LOCAL : (i + 1) * LOCAL, :]
        shapes.append(dot(weights, hidden, precision=HIGHEST) * window)

    channel = lax.broadcasted_iota(jnp.int32, (1, LOCAL), 1) == rank[0] % LOCAL
    skips = jnp.sum(jnp.where(channel, skip_gain[...], 0.0), 1, keepdims=True)
    empty = jnp.zeros((1, 128 - CLIPS), F32)
    backward = jnp.full((1, 128), rank[0] // LOCAL, jnp.int32).astype(F32)
    rows = [
        jnp.concatenate([starts, empty], 1),
        jnp.concatenate([lengths, empty], 1),
        jnp.broadcast_to(skips[:1, :], (1, 128)),
        jnp.broadcast_to(skips[1:, :], (1, 128)),
        backward,
        jnp.zeros((3, 128), F32),
    ]
    notes[...] = jnp.concatenate(rows, 0)

    arrays = [raw[:LOCAL, :], raw[LOCAL : 2 * LOCAL, :], gate_two * out_grad, *shapes]
    for at, values in enumerate(arrays):
        scratch[pl.ds(2 * at, LOCAL, stride=SEND_ROWS), :] = values[:, :128]
        scratch[pl.ds(2 * at + 1, LOCAL, stride=SEND_ROWS), :] = values[:, 128:]
    for at, values in enumerate([high, low]):
        scratch[pl.ds(10 + at, LOCAL, stride=SEND_ROWS), :] = jnp.broadcast_to(
            values.astype(F32), (LOCAL, 128)
        )
    packed = scratch[...].astype(BF16)
    send[: LOCAL * SEND_ROWS, :] = packed
    send[LOCAL * SEND_ROWS :, :] = packed


def turn(values, count, inner):
    product = dot(values.astype(BF16), inner[...])
    pieces = []
    for at in range(count):
        real = product[256 * at : 256 * at + 128, :]
        imag = product[256 * at + 128 : 256 * at + 256, :]
        pieces.append((real[:, :256], real[:, 256:], imag[:, :256], imag[:, 256:]))
    return pieces


def to_spectrum(signals, cosines, sines, analysis, inner):
    rows = dot(analysis[...], jnp.concatenate(signals, 1).astype(BF16))
    twisted = []
    for at in range(len(signals)):
        real = rows[:128, 256 * at : 256 * at + 256]
        imag = rows[128:, 256 * at : 256 * at + 256]
        twisted.append(cosines * real + sines * imag)
        twisted.append(cosines * imag - sines * real)
    pieces = turn(jnp.concatenate(twisted, 0), len(signals), inner)
    return [(rc + is_, ic - rs) for rc, rs, ic, is_ in pieces]


def to_signal(spectra, cosines, sines, synthesis, inner):
    stacked = jnp.concatenate([part for pair in spectra for part in pair], 0)
    columns = []
    for rc, rs, ic, is_ in turn(stacked, len(spectra), inner):
        real = rc - is_
        imag = ic + rs
        columns.append(
            jnp.concatenate([cosines * real - sines * imag, cosines * imag + sines * real], 0)
        )
    rows = dot(synthesis, jnp.concatenate(columns, 1).astype(BF16))
    return [rows[:, 256 * at : 256 * at + 256] for at in range(len(spectra))]


def series_kernel(
    notes, received, analysis, synthesis, inner, twist_cos, twist_sin, back, scratch, packed
):
    starts = notes[:1, :]
    counts = jnp.maximum(notes[1:2, :], 1.0)
    skip_one = notes[2:3, :1]
    skip_two = notes[3:4, :1]
    role = notes[4:5, :1]
    scratch[...] = received[...].astype(F32)

    def plane(row):
        return scratch[pl.ds(row, SEQ, stride=SEND_ROWS), :]

    def signal(at):
        return jnp.concatenate([plane(2 * at), plane(2 * at + 1)], 1)

    power = jnp.sum(plane(10) + plane(11), 0, keepdims=True)
    time = lax.broadcasted_iota(jnp.int32, (SEQ, CHUNK), 0) * CHUNK + lax.broadcasted_iota(
        jnp.int32, (SEQ, CHUNK), 1
    )
    time = time.astype(F32)
    lane = lax.broadcasted_iota(jnp.int32, (1, 128), 1)
    inverse_rms = lax.rsqrt(power / (WIDTH * counts) + EPSILON)
    scale = jnp.zeros((SEQ, CHUNK), F32)
    for p in range(CLIPS):
        scale = jnp.where(time >= starts[:, p : p + 1], inverse_rms[:, p : p + 1], scale)

    cosines = twist_cos[...]
    sines = twist_sin[...]

    def analyse(signals):
        return to_spectrum(signals, cosines, sines, analysis, inner)

    def synthesise(parts, table):
        return to_signal(parts, cosines, sines, table, inner)

    def times(a, b, sign):
        return (a[0] * b[0] - sign * (a[1] * b[1]), a[1] * b[0] + sign * (a[0] * b[1]))

    def half(values):
        lower = values[:PARTS, :]
        upper = values[PARTS:, :]
        return jnp.where(jnp.broadcast_to(role, lower.shape) == 0.0, lower, upper)

    value = signal(0) * scale
    gate_one = signal(1) * scale
    scaled_two = signal(2) * scale
    value_spec, second_spec, filter_one, filter_two = analyse(
        [value, scaled_two, signal(3), signal(4)]
    )
    carry_one, level_grad = synthesise(
        [times(value_spec, filter_one, 1.0), times(second_spec, filter_two, -1.0)],
        synthesis[...],
    )
    carry_one = carry_one + skip_one * value
    level_grad = level_grad + skip_two * scaled_two
    level_one = gate_one * carry_one
    scaled_one = gate_one * level_grad
    level_spec, first_spec = analyse([level_one, scaled_one])
    carry_two, shape_two, value_grad, shape_one = synthesise(
        [
            times(level_spec, filter_two, 1.0),
            times(second_spec, level_spec, -1.0),
            times(first_spec, filter_one, -1.0),
            times(first_spec, value_spec, -1.0),
        ],
        half(synthesis[...].astype(F32)).astype(BF16),
    )
    scale_half = half(scale)
    carry_two = scale_half * (carry_two + skip_two * half(level_one))
    value_grad = scale_half * (value_grad + skip_one * half(scaled_one))
    gate_grad = scale_half * half(level_grad * carry_one)

    def total(values):
        return jnp.sum(jnp.sum(values, 0, keepdims=True), 1, keepdims=True)

    skip_row = jnp.zeros((1, 128), F32)
    for at, skip_grad in enumerate([total(scaled_one * value), total(scaled_two * level_one)]):
        high, low = split(skip_grad)
        mid = low.astype(F32)
        low = skip_grad - high.astype(F32) - mid
        for to, part in enumerate([high.astype(F32), mid, low]):
            skip_row = jnp.where(lane == 3 * at + to, part, skip_row)
    for at, values in enumerate([carry_two, shape_two, value_grad, shape_one, gate_grad]):
        packed[pl.ds(2 * at, PARTS, stride=BACK_ROWS), :] = values[:, :128]
        packed[pl.ds(2 * at + 1, PARTS, stride=BACK_ROWS), :] = values[:, 128:]
    packed[pl.ds(10, PARTS, stride=BACK_ROWS), :] = jnp.broadcast_to(skip_row, (PARTS, 128))
    packed[pl.ds(11, PARTS, stride=BACK_ROWS), :] = jnp.zeros((PARTS, 128), F32)
    back[...] = packed[...].astype(BF16)


def back_kernel(
    place, received, full, in_proj, out_proj, gate_in, grad_in, hidden, window,
    given, kept, weights, skip_out, scratch, packed,
):
    scratch[...] = received[...].astype(F32)

    def plane(row):
        return scratch[pl.ds(row, LOCAL, stride=BACK_ROWS), :]

    def signal(at):
        return jnp.concatenate([plane(2 * at), plane(2 * at + 1)], 1)

    carry = signal(0)
    gated = (gate_in[...] * carry).astype(BF16)
    scaled_grad = jnp.concatenate(
        [signal(2).astype(BF16), signal(4).astype(BF16), (grad_in[...] * carry).astype(BF16)], 0
    )
    inputs = jnp.concatenate([full[128 * j : 128 * j + 64, :] for j in range(4)], 0)
    cotangent = jnp.concatenate([full[128 * j + 64 : 128 * j + 128, :] for j in range(4)], 0)
    first = ((0,), (0,))
    last = ((1,), (1,))
    mixed = dot(out_proj[...], gated, first)
    grad_inputs = dot(in_proj[...], scaled_grad, first)
    even = place[0] % 2 == 0
    for at in range(2):
        for to, values in enumerate([mixed, grad_inputs]):
            low = values[128 * at : 128 * at + 64, :]
            high = values[128 * at + 64 : 128 * at + 128, :]
            rows = slice(128 * at + 64 * to, 128 * at + 64 * to + 64)
            given[rows, :] = jnp.where(even, high, low).astype(BF16)
            kept[rows, :] = jnp.where(even, low, high)
    in_weight = dot(scaled_grad, inputs, last)
    out_weight = dot(gated, cotangent, last)
    blank = jnp.zeros((LOCAL, CHUNK), F32)
    shape_one = signal(3) * window[:LOCAL, :]
    shape_two = signal(1) * window[LOCAL:, :]
    filter_grad = dot(
        shape_one, jnp.concatenate([hidden[...], blank], 0), last, HIGHEST
    ) + dot(shape_two, jnp.concatenate([blank, hidden[...]], 0), last, HIGHEST)
    rows = [
        in_weight[64 * at : 64 * at + 64, 128 * half : 128 * half + 128]
        for at in range(3)
        for half in range(2)
    ]
    rows += [out_weight[:, :128], out_weight[:, 128:], filter_grad, jnp.zeros((PARTS, 128), F32)]
    for at, values in enumerate(rows):
        packed[pl.ds(at, PARTS, stride=PART_ROWS), :] = values
    weights[...] = packed[...].astype(BF16)
    lane = lax.broadcasted_iota(jnp.int32, (8, 128), 1)
    order = lax.broadcasted_iota(jnp.int32, (8, 128), 0)
    pick = jnp.where((lane >= 3 * order) & (lane < 3 * order + 3), 1.0, 0.0).astype(BF16)
    skip_out[...] = dot(pick, plane(10).astype(BF16), last)[:2, :] * TOTAL ** (-0.5)


def core_kernel(place, received, kept, given, left):
    total = kept[...] + received[...].astype(F32)
    near = place[0] < 2
    given[...] = jnp.where(near, total[128:, :], total[:128, :]).astype(BF16)
    left[...] = jnp.where(near, total[:128, :], total[128:, :])


def sum_kernel(received, spread):
    four = 4 * PART_ROWS
    parts = jnp.sum(received[...].astype(F32).reshape(PARTS // 4, four, 128), 0)
    total = sum(parts[PART_ROWS * at : PART_ROWS * at + PART_ROWS, :] for at in range(4))
    total = jnp.concatenate([total * TOTAL ** (-0.5)] * 4, 0)
    total = jnp.broadcast_to(total[None], (SEQ // 4, four, 128)).reshape(SEQ * PART_ROWS, 128)
    spread[...] = total.astype(BF16)


def last_kernel(
    received, over_chips, left, mixed, grad_inputs, in_weight, out_weight, filter_grad, scratch
):
    summed = (left[...] + over_chips[...].astype(F32)).astype(BF16)
    mixed[...] = summed[:64, :]
    grad_inputs[...] = summed[64:, :]
    scratch[...] = received[...].astype(F32)

    def block(at):
        first = scratch[pl.ds(at, PARTS, stride=PART_ROWS), :]
        return first + scratch[pl.ds(PARTS * PART_ROWS + at, PARTS, stride=PART_ROWS), :]

    for half in range(2):
        for at in range(3):
            in_weight[64 * at : 64 * at + 64, 128 * half : 128 * half + 128] = block(2 * at + half)
        out_weight[:, 128 * half : 128 * half + 128] = block(6 + half)
    filters = block(8)
    filter_grad[:LOCAL, :] = filters[:, :HIDDEN]
    filter_grad[LOCAL:, :] = filters[:, HIDDEN:]


def call(kernel, name, outs, scalars, arrays, scratch=()):
    def vmem():
        return pl.BlockSpec(memory_space=pltpu.VMEM)

    return pl.pallas_call(
        kernel,
        name=name,
        out_shape=[jax.ShapeDtypeStruct(shape, kind) for shape, kind in outs],
        in_specs=[pl.BlockSpec(memory_space=pltpu.SMEM)] * scalars + [vmem() for _ in range(arrays)],
        out_specs=[vmem() for _ in outs],
        scratch_shapes=[pltpu.VMEM(shape, F32) for shape in scratch],
        compiler_params=pltpu.CompilerParams(vmem_limit_bytes=32 * 1024 * 1024),
    )


def front():
    return call(
        front_kernel,
        "project",
        [
            ((SEQ * SEND_ROWS, 128), BF16),
            ((LOCAL, CHUNK), F32),
            ((LOCAL, CHUNK), F32),
            ((HIDDEN, CHUNK), F32),
            ((2 * LOCAL, CHUNK), F32),
            ((8, 128), F32),
        ],
        1,
        9,
        [(LOCAL * SEND_ROWS, 128)],
    )


def series():
    return call(
        series_kernel,
        "convolve",
        [((PARTS * BACK_ROWS, 128), BF16)],
        0,
        7,
        [(SEQ * SEND_ROWS, 128), (PARTS * BACK_ROWS, 128)],
    )


def rear():
    return call(
        back_kernel,
        "weigh",
        [
            ((256, CHUNK), BF16),
            ((256, CHUNK), F32),
            ((PARTS * PART_ROWS, 128), BF16),
            ((2, LOCAL), F32),
        ],
        1,
        8,
        [(PARTS * BACK_ROWS, 128), (PARTS * PART_ROWS, 128)],
    )


def core_sum():
    return call(core_kernel, "add_core", [((128, CHUNK), BF16), ((128, CHUNK), F32)], 1, 2)


def total():
    return call(sum_kernel, "add_up", [((SEQ * PART_ROWS, 128), BF16)], 0, 1)


def finish():
    return call(
        last_kernel,
        "unpack",
        [
            ((64, CHUNK), BF16),
            ((64, CHUNK), BF16),
            ((3 * LOCAL, WIDTH), F32),
            ((LOCAL, WIDTH), F32),
            ((2 * LOCAL, HIDDEN), F32),
        ],
        0,
        3,
        [(SEQ * PART_ROWS, 128)],
    )


def swap(values, group, among=None):
    tiles = values.reshape(values.shape[0] // group, group, 128)
    tiles = lax.all_to_all(
        tiles, "seq", split_axis=0, concat_axis=0, axis_index_groups=among, tiled=True
    )
    return tiles.reshape(values.shape)


def shards(
    inputs,
    clip_len,
    clip_order,
    in_proj,
    out_proj,
    filt_in,
    filt_out,
    decay_rate,
    skip_gain,
    cotangent,
):
    rank = lax.axis_index("seq").astype(jnp.int32).reshape(1)
    place = lax.axis_index("ch").astype(jnp.int32).reshape(1)
    rank, place = lax.optimization_barrier((rank, place))
    halves = [list(range(at * PARTS, at * PARTS + PARTS)) for at in range(SEQ // PARTS)]
    in_rows = in_proj.reshape(3 * LOCAL, WIDTH)
    out_rows = out_proj.T
    full = lax.all_gather(jnp.concatenate([inputs, cotangent], 0), "ch", axis=0, tiled=True)
    send, gate_two, out_grad, hidden, window, notes = front()(
        rank, clip_len.reshape(1, CLIPS), clip_order.reshape(1, CLIPS), skip_gain, full, in_rows,
        out_rows, filt_in, filt_out.reshape(2 * LOCAL, HIDDEN), decay_rate,
    )
    received = swap(send, 4)
    (back,) = series()(notes, received, *[jnp.asarray(x) for x in tables()])
    returned = swap(back, 4, halves)
    given, kept, weights, grad_skip = rear()(
        place, returned, full, in_rows, out_rows, gate_two, out_grad, hidden, window
    )
    over_cores = lax.ppermute(given, "ch", [(0, 1), (1, 0), (2, 3), (3, 2)])
    given, left = core_sum()(place, over_cores, kept)
    (spread,) = total()(swap(weights, 2, halves))
    spread, given = lax.optimization_barrier((spread, given))
    over_chips = lax.ppermute(given, "ch", [(0, 2), (2, 0), (1, 3), (3, 1)])
    mixed, grad_inputs, in_weight, out_weight, filter_grad = finish()(
        swap(spread, 2), over_chips, left
    )
    return (
        mixed,
        grad_inputs,
        in_weight.reshape(3, LOCAL, WIDTH),
        out_weight.T,
        filter_grad.reshape(2, LOCAL, HIDDEN),
        grad_skip,
    )


def solution(mesh):
    return jax.shard_map(
        shards,
        mesh=mesh,
        in_specs=(
            P("ch", "seq"),
            P(),
            P(),
            P(None, "ch", None),
            P(None, "ch"),
            P(),
            P(None, "ch", None),
            P(None, "ch"),
            P(None, "ch"),
            P("ch", "seq"),
        ),
        out_specs=(
            P("ch", "seq"),
            P("ch", "seq"),
            P(None, "ch", None),
            P(None, "ch"),
            P(None, "ch", None),
            P(None, "ch"),
        ),
        check_vma=False,
    )
```

```python
import functools
import math

import jax
import jax.numpy as jnp
import numpy as np
from jax import lax
from jax.experimental import pallas as pl
from jax.experimental.pallas import tpu as pltpu
from jax.sharding import PartitionSpec as P

EPSILON = 1e-05
HIGHEST = lax.Precision.HIGHEST
F32 = jnp.float32
BF16 = jnp.bfloat16

WIDTH = 256
TOTAL = 32768
SEQ = 128
CHUNK = 256
LOCAL = 64
HIDDEN = 64
BANDS = 16
CLIPS = 16
SEND_ROWS = 12
BACK_ROWS = 10
PART_ROWS = 10
PARTS = 64


def tables():
    k1 = np.arange(SEQ)[:, None] + 0.25
    s = np.arange(SEQ)[None, :]
    u = np.arange(CHUNK)[None, :]
    first = 2.0 * np.pi * k1 * s / SEQ
    analysis = np.concatenate([np.cos(first), -np.sin(first)], 0).astype(np.float32)
    synthesis = (np.concatenate([np.cos(first), -np.sin(first)], 0).T / TOTAL).astype(np.float32)
    twist = 2.0 * np.pi * k1 * u / TOTAL
    k2 = np.arange(CHUNK)
    second = 2.0 * np.pi * ((k2[:, None] * k2[None, :]) % CHUNK) / CHUNK
    cosines, sines = np.cos(second), np.sin(second)
    forward = np.block([[cosines, -sines], [sines, cosines]]).astype(np.float32)
    return (
        analysis.astype(BF16),
        synthesis.astype(BF16),
        forward.astype(BF16),
        forward.T.astype(BF16),
        np.cos(twist).astype(np.float32),
        np.sin(twist).astype(np.float32),
    )


def dot(a, b, dims=((1,), (0,)), precision=None):
    return lax.dot_general(a, b, (dims, ((), ())), precision=precision, preferred_element_type=F32)


def split(x):
    high = x.astype(BF16)
    return high, (x - high.astype(F32)).astype(BF16)


def to_column(row, count):
    shape = (count, count)
    rows = lax.broadcasted_iota(jnp.int32, shape, 0)
    columns = lax.broadcasted_iota(jnp.int32, shape, 1)
    spread = jnp.broadcast_to(row, shape)
    return jnp.sum(jnp.where(rows == columns, spread, jnp.zeros_like(spread)), 1, keepdims=True)


def clip_bounds(clip_len, clip_order):
    shape = (CLIPS, CLIPS)
    rows = lax.broadcasted_iota(jnp.int32, shape, 0)
    columns = lax.broadcasted_iota(jnp.int32, shape, 1)
    sizes = to_column(clip_len.astype(F32), CLIPS)
    lengths = jnp.sum(jnp.where(rows == clip_order, sizes, 0.0), 0, keepdims=True)
    starts = jnp.sum(
        jnp.where(rows < columns, to_column(lengths, CLIPS), 0.0), 0, keepdims=True
    )
    return starts, lengths


def front_kernel(
    rank, clip_len, clip_order, skip_gain, full, in_proj, out_proj, filt_in, filt_out, decay,
    send, gate_out, grad_out, hidden_out, window_out, notes, scratch,
):
    first = ((0,), (0,))
    inputs = jnp.concatenate([full[128 * j : 128 * j + 64, :] for j in range(4)], 0)
    cotangent = jnp.concatenate([full[128 * j + 64 : 128 * j + 128, :] for j in range(4)], 0)
    raw = dot(in_proj[...], inputs)
    out_grad = dot(out_proj[...], cotangent)
    gate_two = raw[2 * LOCAL :, :]
    gate_out[...] = gate_two
    grad_out[...] = out_grad

    offset = rank[0] * CHUNK
    starts, lengths = clip_bounds(clip_len[...], clip_order[...])
    begin = to_column(starts, CLIPS)
    end = begin + to_column(lengths, CLIPS)
    time = (offset + lax.broadcasted_iota(jnp.int32, (CLIPS, CHUNK), 1)).astype(F32)
    member = jnp.where((time >= begin) & (time < end), 1.0, 0.0)
    member = jnp.concatenate([member, jnp.zeros((128 - CLIPS, CHUNK), F32)], 0)
    wide = inputs.astype(F32)
    squares = jnp.sum(wide * wide, 0, keepdims=True)
    power = dot(jnp.broadcast_to(squares, (8, CHUNK)), member, ((1,), (1,)), HIGHEST)[:1, :]
    high, low = split(power)

    step = offset + lax.broadcasted_iota(jnp.int32, (BANDS, CHUNK), 1)
    band = 1 + lax.broadcasted_iota(jnp.int32, (BANDS, CHUNK), 0)
    phases = ((step * band) & (TOTAL - 1)).astype(F32) * (2.0 * math.pi / TOTAL)
    ramp = (offset + lax.broadcasted_iota(jnp.int32, (8, CHUNK), 1)).astype(F32) * (1.0 / TOTAL)
    first_row = lax.broadcasted_iota(jnp.int32, (8, HIDDEN), 0) == 0
    ramp_weight = jnp.where(first_row, filt_in[:8, :], 0.0)
    hidden = jnp.sin(
        dot(ramp_weight, ramp, first, HIGHEST)
        + dot(filt_in[1 : 1 + BANDS, :], jnp.cos(phases), first, HIGHEST)
        + dot(filt_in[1 + BANDS : 1 + 2 * BANDS, :], jnp.sin(phases), first, HIGHEST)
    )
    hidden_out[...] = hidden
    rows = lax.broadcasted_iota(jnp.int32, (LOCAL, LOCAL), 0)
    columns = lax.broadcasted_iota(jnp.int32, (LOCAL, LOCAL), 1)
    shapes = []
    for i in range(2):
        spread = jnp.broadcast_to(decay[i : i + 1, :], (LOCAL, LOCAL))
        rate = jnp.sum(jnp.where(rows == columns, spread, 0.0), 1, keepdims=True)
        window = jnp.exp(-rate * ramp[:1, :]) * TOTAL ** (-0.5)
        window_out[i * LOCAL : (i + 1) * LOCAL, :] = window
        weights = filt_out[i * LOCAL : (i + 1) * LOCAL, :]
        shapes.append(dot(weights, hidden, precision=HIGHEST) * window)

    channel = lax.broadcasted_iota(jnp.int32, (1, LOCAL), 1) == rank[0] % LOCAL
    skips = jnp.sum(jnp.where(channel, skip_gain[...], 0.0), 1, keepdims=True)
    empty = jnp.zeros((1, 128 - CLIPS), F32)
    backward = jnp.full((1, 128), rank[0] // LOCAL, jnp.int32).astype(F32)
    rows = [
        jnp.concatenate([starts, empty], 1),
        jnp.concatenate([lengths, empty], 1),
        jnp.broadcast_to(skips[:1, :], (1, 128)),
        jnp.broadcast_to(skips[1:, :], (1, 128)),
        backward,
        jnp.zeros((3, 128), F32),
    ]
    notes[...] = jnp.concatenate(rows, 0)

    arrays = [raw[:LOCAL, :], raw[LOCAL : 2 * LOCAL, :], gate_two * out_grad, *shapes]
    for at, values in enumerate(arrays):
        scratch[pl.ds(2 * at, LOCAL, stride=SEND_ROWS), :] = values[:, :128]
        scratch[pl.ds(2 * at + 1, LOCAL, stride=SEND_ROWS), :] = values[:, 128:]
    for at, values in enumerate([high, low]):
        scratch[pl.ds(10 + at, LOCAL, stride=SEND_ROWS), :] = jnp.broadcast_to(
            values.astype(F32), (LOCAL, 128)
        )
    packed = scratch[...].astype(BF16)
    send[: LOCAL * SEND_ROWS, :] = packed
    send[LOCAL * SEND_ROWS :, :] = packed


def to_spectrum(signals, cosines, sines, analysis, inner):
    rows = dot(analysis[...], jnp.concatenate(signals, 1).astype(BF16))
    twisted = []
    for at in range(len(signals)):
        real = rows[:128, 256 * at : 256 * at + 256]
        imag = rows[128:, 256 * at : 256 * at + 256]
        parts = [cosines * real + sines * imag, cosines * imag - sines * real]
        twisted.append(jnp.concatenate(parts, 1).astype(BF16))
    spectra = dot(jnp.concatenate(twisted, 0), inner[...])
    pairs = [spectra[128 * at : 128 * at + 128, :] for at in range(len(signals))]
    return [(pair[:, :256], pair[:, 256:]) for pair in pairs]


def to_signal(spectra, cosines, sines, synthesis, inner):
    stacked = [jnp.concatenate(pair, 1).astype(BF16) for pair in spectra]
    rows = dot(jnp.concatenate(stacked, 0), inner[...])
    columns = []
    for at in range(len(spectra)):
        real = rows[128 * at : 128 * at + 128, :256]
        imag = rows[128 * at : 128 * at + 128, 256:]
        parts = [cosines * real - sines * imag, cosines * imag + sines * real]
        columns.append(jnp.concatenate(parts, 0).astype(BF16))
    signals = dot(synthesis, jnp.concatenate(columns, 1))
    return [signals[:, 256 * at : 256 * at + 256] for at in range(len(spectra))]


def series_kernel(
    notes, received, analysis, synthesis, forward, backward, twist_cos, twist_sin,
    back, skips, scratch, packed,
):
    starts = notes[:1, :]
    counts = jnp.maximum(notes[1:2, :], 1.0)
    skip_one = notes[2:3, :1]
    skip_two = notes[3:4, :1]
    role = notes[4:5, :1]
    scratch[...] = received[...].astype(F32)

    def plane(row):
        return scratch[pl.ds(row, SEQ, stride=SEND_ROWS), :]

    def signal(at):
        return jnp.concatenate([plane(2 * at), plane(2 * at + 1)], 1)

    power = jnp.sum(plane(10) + plane(11), 0, keepdims=True)
    time = lax.broadcasted_iota(jnp.int32, (SEQ, CHUNK), 0) * CHUNK + lax.broadcasted_iota(
        jnp.int32, (SEQ, CHUNK), 1
    )
    time = time.astype(F32)
    lane = lax.broadcasted_iota(jnp.int32, (1, 128), 1)
    inverse_rms = lax.rsqrt(power / (WIDTH * counts) + EPSILON)
    scale = jnp.zeros((SEQ, CHUNK), F32)
    for p in range(CLIPS):
        scale = jnp.where(time >= starts[:, p : p + 1], inverse_rms[:, p : p + 1], scale)

    cosines = twist_cos[...]
    sines = twist_sin[...]

    def analyse(signals):
        return to_spectrum(signals, cosines, sines, analysis, forward)

    def synthesise(parts, table):
        return to_signal(parts, cosines, sines, table, backward)

    def times(a, b, sign):
        return (a[0] * b[0] - sign * (a[1] * b[1]), a[1] * b[0] + sign * (a[0] * b[1]))

    def half(values):
        lower = values[:PARTS, :]
        upper = values[PARTS:, :]
        return jnp.where(jnp.broadcast_to(role, lower.shape) == 0.0, lower, upper)

    value = signal(0) * scale
    gate_one = signal(1) * scale
    scaled_two = signal(2) * scale
    value_spec, second_spec, filter_one, filter_two = analyse(
        [value, scaled_two, signal(3), signal(4)]
    )
    carry_one, level_grad = synthesise(
        [times(value_spec, filter_one, 1.0), times(second_spec, filter_two, -1.0)],
        synthesis[...],
    )
    carry_one = carry_one + skip_one * value
    level_grad = level_grad + skip_two * scaled_two
    level_one = gate_one * carry_one
    scaled_one = gate_one * level_grad
    level_spec, first_spec = analyse([level_one, scaled_one])
    carry_two, shape_two, value_grad, shape_one = synthesise(
        [
            times(level_spec, filter_two, 1.0),
            times(second_spec, level_spec, -1.0),
            times(first_spec, filter_one, -1.0),
            times(first_spec, value_spec, -1.0),
        ],
        half(synthesis[...].astype(F32)).astype(BF16),
    )
    scale_half = half(scale)
    carry_two = scale_half * (carry_two + skip_two * half(level_one))
    value_grad = scale_half * (value_grad + skip_one * half(scaled_one))
    gate_grad = scale_half * half(level_grad * carry_one)

    def total(values):
        return jnp.sum(jnp.sum(values, 0, keepdims=True), 1, keepdims=True)

    skip_row = jnp.zeros((1, 128), F32)
    for at, skip_grad in enumerate([total(scaled_one * value), total(scaled_two * level_one)]):
        high, low = split(skip_grad)
        mid = low.astype(F32)
        low = skip_grad - high.astype(F32) - mid
        for to, part in enumerate([high.astype(F32), mid, low]):
            skip_row = jnp.where(lane == 3 * at + to, part, skip_row)
    for at, values in enumerate([carry_two, shape_two, value_grad, shape_one, gate_grad]):
        packed[pl.ds(2 * at, PARTS, stride=BACK_ROWS), :] = values[:, :128]
        packed[pl.ds(2 * at + 1, PARTS, stride=BACK_ROWS), :] = values[:, 128:]
    skips[...] = jnp.broadcast_to(skip_row, (8, 128))
    back[...] = packed[...].astype(BF16)


def returned_signal(scratch, at):
    rows = [scratch[pl.ds(2 * at + half, LOCAL, stride=BACK_ROWS), :] for half in range(2)]
    return jnp.concatenate(rows, 1)


def weight_kernel(
    received, full, gate_in, grad_in, hidden, window, weights, gated_out, scaled_out,
    scratch, packed,
):
    scratch[...] = received[...].astype(F32)
    carry = returned_signal(scratch, 0)
    gated = (gate_in[...] * carry).astype(BF16)
    scaled_grad = jnp.concatenate(
        [
            returned_signal(scratch, 2).astype(BF16),
            returned_signal(scratch, 4).astype(BF16),
            (grad_in[...] * carry).astype(BF16),
        ],
        0,
    )
    gated_out[...] = gated
    scaled_out[...] = scaled_grad
    inputs = jnp.concatenate([full[128 * j : 128 * j + 64, :] for j in range(4)], 0)
    cotangent = jnp.concatenate([full[128 * j + 64 : 128 * j + 128, :] for j in range(4)], 0)
    last = ((1,), (1,))
    in_weight = dot(scaled_grad, inputs, last)
    out_weight = dot(gated, cotangent, last)
    blank = jnp.zeros((LOCAL, CHUNK), F32)
    shape_one = returned_signal(scratch, 3) * window[:LOCAL, :]
    shape_two = returned_signal(scratch, 1) * window[LOCAL:, :]
    filter_grad = dot(
        shape_one, jnp.concatenate([hidden[...], blank], 0), last, HIGHEST
    ) + dot(shape_two, jnp.concatenate([blank, hidden[...]], 0), last, HIGHEST)
    rows = [
        in_weight[64 * at : 64 * at + 64, 128 * half : 128 * half + 128]
        for at in range(3)
        for half in range(2)
    ]
    rows += [out_weight[:, :128], out_weight[:, 128:], filter_grad, jnp.zeros((PARTS, 128), F32)]
    for at, values in enumerate(rows):
        packed[pl.ds(at, PARTS, stride=PART_ROWS), :] = values
    weights[...] = packed[...].astype(BF16)


def channel_kernel(place, gated, scaled_grad, in_proj, out_proj, given, kept):
    first = ((0,), (0,))
    mixed = dot(out_proj[...], gated[...], first)
    grad_inputs = dot(in_proj[...], scaled_grad[...], first)
    even = place[0] % 2 == 0
    for at in range(2):
        for to, values in enumerate([mixed, grad_inputs]):
            low = values[128 * at : 128 * at + 64, :]
            high = values[128 * at + 64 : 128 * at + 128, :]
            rows = slice(128 * at + 64 * to, 128 * at + 64 * to + 64)
            given[rows, :] = jnp.where(even, high, low).astype(BF16)
            kept[rows, :] = jnp.where(even, low, high)


def core_kernel(place, received, kept, given, left):
    total = kept[...] + received[...].astype(F32)
    near = place[0] < 2
    given[...] = jnp.where(near, total[128:, :], total[:128, :]).astype(BF16)
    left[...] = jnp.where(near, total[:128, :], total[128:, :])


def sum_kernel(received, skips, spread):
    four = 4 * PART_ROWS
    parts = jnp.sum(received[...].astype(F32).reshape(PARTS // 4, four, 128), 0)
    total = sum(parts[PART_ROWS * at : PART_ROWS * at + PART_ROWS, :] for at in range(4))
    row = lax.broadcasted_iota(jnp.int32, (PART_ROWS, 128), 0)
    total = jnp.where(row == PART_ROWS - 1, skips[:1, :], total * TOTAL ** (-0.5))
    total = jnp.concatenate([total] * 4, 0)
    total = jnp.broadcast_to(total[None], (SEQ // 4, four, 128)).reshape(SEQ * PART_ROWS, 128)
    spread[...] = total.astype(BF16)


def last_kernel(
    received, over_chips, left, mixed, grad_inputs, in_weight, out_weight, filter_grad, skip_grad,
    scratch,
):
    summed = (left[...] + over_chips[...].astype(F32)).astype(BF16)
    mixed[...] = summed[:64, :]
    grad_inputs[...] = summed[64:, :]
    scratch[...] = received[...].astype(F32)

    def block(at):
        first = scratch[pl.ds(at, PARTS, stride=PART_ROWS), :]
        return first + scratch[pl.ds(PARTS * PART_ROWS + at, PARTS, stride=PART_ROWS), :]

    for half in range(2):
        for at in range(3):
            in_weight[64 * at : 64 * at + 64, 128 * half : 128 * half + 128] = block(2 * at + half)
        out_weight[:, 128 * half : 128 * half + 128] = block(6 + half)
    filters = block(8)
    filter_grad[:LOCAL, :] = filters[:, :HIDDEN]
    filter_grad[LOCAL:, :] = filters[:, HIDDEN:]
    lane = lax.broadcasted_iota(jnp.int32, (8, 128), 1)
    order = lax.broadcasted_iota(jnp.int32, (8, 128), 0)
    pick = jnp.where((lane >= 3 * order) & (lane < 3 * order + 3), 1.0, 0.0).astype(BF16)
    skips = scratch[pl.ds(PART_ROWS - 1, PARTS, stride=PART_ROWS), :].astype(BF16)
    skip_grad[...] = dot(pick, skips, ((1,), (1,)))[:2, :] * TOTAL ** (-0.5)


def call(kernel, name, outs, scalars, arrays, scratch=()):
    def vmem():
        return pl.BlockSpec(memory_space=pltpu.VMEM)

    return pl.pallas_call(
        kernel,
        name=name,
        out_shape=[jax.ShapeDtypeStruct(shape, kind) for shape, kind in outs],
        in_specs=[pl.BlockSpec(memory_space=pltpu.SMEM)] * scalars + [vmem() for _ in range(arrays)],
        out_specs=[vmem() for _ in outs],
        scratch_shapes=[pltpu.VMEM(shape, F32) for shape in scratch],
        compiler_params=pltpu.CompilerParams(vmem_limit_bytes=32 * 1024 * 1024),
    )


def front():
    return call(
        front_kernel,
        "project",
        [
            ((SEQ * SEND_ROWS, 128), BF16),
            ((LOCAL, CHUNK), F32),
            ((LOCAL, CHUNK), F32),
            ((HIDDEN, CHUNK), F32),
            ((2 * LOCAL, CHUNK), F32),
            ((8, 128), F32),
        ],
        1,
        9,
        [(LOCAL * SEND_ROWS, 128)],
    )


def series():
    return call(
        series_kernel,
        "convolve",
        [((PARTS * BACK_ROWS, 128), BF16), ((8, 128), F32)],
        0,
        8,
        [(SEQ * SEND_ROWS, 128), (PARTS * BACK_ROWS, 128)],
    )


def weighing():
    return call(
        weight_kernel,
        "weigh",
        [
            ((PARTS * PART_ROWS, 128), BF16),
            ((LOCAL, CHUNK), BF16),
            ((3 * LOCAL, CHUNK), BF16),
        ],
        0,
        6,
        [(PARTS * BACK_ROWS, 128), (PARTS * PART_ROWS, 128)],
    )


def channels():
    return call(channel_kernel, "mix", [((256, CHUNK), BF16), ((256, CHUNK), F32)], 1, 4)


def core_sum():
    return call(core_kernel, "add_core", [((128, CHUNK), BF16), ((128, CHUNK), F32)], 1, 2)


def total():
    return call(sum_kernel, "add_up", [((SEQ * PART_ROWS, 128), BF16)], 0, 2)


def finish():
    return call(
        last_kernel,
        "unpack",
        [
            ((64, CHUNK), BF16),
            ((64, CHUNK), BF16),
            ((3 * LOCAL, WIDTH), F32),
            ((LOCAL, WIDTH), F32),
            ((2 * LOCAL, HIDDEN), F32),
            ((2, LOCAL), F32),
        ],
        0,
        3,
        [(SEQ * PART_ROWS, 128)],
    )


def swap(values, group, among=None):
    tiles = values.reshape(values.shape[0] // group, group, 128)
    tiles = lax.all_to_all(
        tiles, "seq", split_axis=0, concat_axis=0, axis_index_groups=among, tiled=True
    )
    return tiles.reshape(values.shape)


def shards(
    inputs,
    clip_len,
    clip_order,
    in_proj,
    out_proj,
    filt_in,
    filt_out,
    decay_rate,
    skip_gain,
    cotangent,
):
    rank = lax.axis_index("seq").astype(jnp.int32).reshape(1)
    place = lax.axis_index("ch").astype(jnp.int32).reshape(1)
    rank, place = lax.optimization_barrier((rank, place))
    halves = [list(range(at * PARTS, at * PARTS + PARTS)) for at in range(SEQ // PARTS)]
    in_rows = in_proj.reshape(3 * LOCAL, WIDTH)
    out_rows = out_proj.T
    full = lax.all_gather(jnp.concatenate([inputs, cotangent], 0), "ch", axis=0, tiled=True)
    send, gate_two, out_grad, hidden, window, notes = front()(
        rank, clip_len.reshape(1, CLIPS), clip_order.reshape(1, CLIPS), skip_gain, full, in_rows,
        out_rows, filt_in, filt_out.reshape(2 * LOCAL, HIDDEN), decay_rate,
    )
    received = swap(send, 4)
    back, skips = series()(notes, received, *[jnp.asarray(x) for x in tables()])
    returned = swap(back, 2, halves)
    weights, gated, scaled_grad = weighing()(
        returned, full, gate_two, out_grad, hidden, window
    )
    given, kept = channels()(place, gated, scaled_grad, in_rows, out_rows)
    over_cores = lax.ppermute(given, "ch", [(0, 1), (1, 0), (2, 3), (3, 2)])
    given, left = core_sum()(place, over_cores, kept)
    (spread,) = total()(swap(weights, 2, halves), skips)
    spread, given = lax.optimization_barrier((spread, given))
    over_chips = lax.ppermute(given, "ch", [(0, 2), (2, 0), (1, 3), (3, 1)])
    mixed, grad_inputs, in_weight, out_weight, filter_grad, grad_skip = finish()(
        swap(spread, 2), over_chips, left
    )
    return (
        mixed,
        grad_inputs,
        in_weight.reshape(3, LOCAL, WIDTH),
        out_weight.T,
        filter_grad.reshape(2, LOCAL, HIDDEN),
        grad_skip,
    )


def solution(mesh):
    return jax.shard_map(
        shards,
        mesh=mesh,
        in_specs=(
            P("ch", "seq"),
            P(),
            P(),
            P(None, "ch", None),
            P(None, "ch"),
            P(),
            P(None, "ch", None),
            P(None, "ch"),
            P(None, "ch"),
            P("ch", "seq"),
        ),
        out_specs=(
            P("ch", "seq"),
            P("ch", "seq"),
            P(None, "ch", None),
            P(None, "ch"),
            P(None, "ch", None),
            P(None, "ch"),
        ),
        check_vma=False,
    )
```

```python
import functools
import math

import jax
import jax.numpy as jnp
import numpy as np
from jax import lax
from jax.experimental import pallas as pl
from jax.experimental.pallas import tpu as pltpu
from jax.sharding import PartitionSpec as P

EPSILON = 1e-05
HIGHEST = lax.Precision.HIGHEST
F32 = jnp.float32
BF16 = jnp.bfloat16

WIDTH = 256
TOTAL = 32768
SEQ = 128
CHUNK = 256
LOCAL = 64
HIDDEN = 64
BANDS = 16
CLIPS = 16
SEND_ROWS = 8
BACK_ROWS = 10
PART_ROWS = 10
PARTS = 64


def tables():
    k1 = np.arange(SEQ)[:, None] + 0.25
    s = np.arange(SEQ)[None, :]
    u = np.arange(CHUNK)[None, :]
    first = 2.0 * np.pi * k1 * s / SEQ
    analysis = np.concatenate([np.cos(first), -np.sin(first)], 0).astype(np.float32)
    synthesis = (np.concatenate([np.cos(first), -np.sin(first)], 0).T / TOTAL).astype(np.float32)
    twist = 2.0 * np.pi * k1 * u / TOTAL
    k2 = np.arange(CHUNK)
    second = 2.0 * np.pi * ((k2[:, None] * k2[None, :]) % CHUNK) / CHUNK
    cosines, sines = np.cos(second), np.sin(second)
    forward = np.block([[cosines, -sines], [sines, cosines]]).astype(np.float32)
    return (
        analysis.astype(BF16),
        synthesis.astype(BF16),
        forward.astype(BF16),
        forward.T.astype(BF16),
        np.cos(twist).astype(np.float32),
        np.sin(twist).astype(np.float32),
    )


def wave_tables():
    f = np.arange(1, BANDS + 1)
    count = 2 * BANDS + 2
    chunk = 2.0 * np.pi * (f[None, :] * np.arange(SEQ)[:, None] % SEQ) / SEQ
    sample = 2.0 * np.pi * f[:, None] * np.arange(CHUNK)[None, :] / TOTAL
    cosines, sines = np.cos(chunk), np.sin(chunk)
    ramp = np.arange(SEQ)[:, None] / SEQ
    ones = np.ones((SEQ, 1))
    first = np.concatenate([cosines, cosines, ramp, ones], 1)
    second = np.concatenate([sines, -sines, 0 * ones, 0 * ones], 1)
    inner = np.concatenate(
        [
            np.cos(sample),
            np.sin(sample),
            np.ones((1, CHUNK)),
            np.arange(CHUNK)[None, :] / TOTAL,
        ],
        0,
    ).astype(np.float32)
    high = inner.astype(BF16)
    low = (inner - high.astype(np.float32)).astype(BF16)
    pick_first = np.zeros((1 + 2 * BANDS, count))
    pick_second = np.zeros((1 + 2 * BANDS, count))
    for band in range(BANDS):
        pick_first[1 + band, band] = 1
        pick_first[1 + BANDS + band, BANDS + band] = 1
        pick_second[1 + BANDS + band, band] = 1
        pick_second[1 + band, BANDS + band] = 1
    pick_first[0, 2 * BANDS :] = 1

    def lanes(table):
        wide = np.zeros((table.shape[0], 128), np.float32)
        wide[:, : 3 * count] = np.concatenate([table] * 3, 1)
        return wide

    def rows(table):
        wide = np.zeros((40, 128), np.float32)
        wide[:32] = lanes(table)[:32]
        wide[39] = lanes(table)[32]
        return wide

    factors = np.zeros((128, CHUNK), BF16)
    factors[: 3 * count] = np.concatenate([high, low, high], 0)
    return lanes(first), lanes(second), rows(pick_first), rows(pick_second), factors


def dot(a, b, dims=((1,), (0,)), precision=None):
    return lax.dot_general(a, b, (dims, ((), ())), precision=precision, preferred_element_type=F32)


def split(x):
    high = x.astype(BF16)
    return high, (x - high.astype(F32)).astype(BF16)


def to_column(row, count):
    shape = (count, count)
    rows = lax.broadcasted_iota(jnp.int32, shape, 0)
    columns = lax.broadcasted_iota(jnp.int32, shape, 1)
    spread = jnp.broadcast_to(row, shape)
    return jnp.sum(jnp.where(rows == columns, spread, jnp.zeros_like(spread)), 1, keepdims=True)


def clip_bounds(clip_len, clip_order):
    shape = (CLIPS, CLIPS)
    rows = lax.broadcasted_iota(jnp.int32, shape, 0)
    columns = lax.broadcasted_iota(jnp.int32, shape, 1)
    sizes = to_column(clip_len.astype(F32), CLIPS)
    lengths = jnp.sum(jnp.where(rows == clip_order, sizes, 0.0), 0, keepdims=True)
    starts = jnp.sum(
        jnp.where(rows < columns, to_column(lengths, CLIPS), 0.0), 0, keepdims=True
    )
    return starts, lengths


def front_kernel(
    rank, clip_len, clip_order, skip_gain, full, in_proj, out_proj, filt_in, decay,
    send, gate_out, grad_out, hidden_out, window_out, notes, scratch,
):
    first = ((0,), (0,))
    inputs = jnp.concatenate([full[128 * j : 128 * j + 64, :] for j in range(4)], 0)
    cotangent = jnp.concatenate([full[128 * j + 64 : 128 * j + 128, :] for j in range(4)], 0)
    raw = dot(in_proj[...], inputs)
    out_grad = dot(out_proj[...], cotangent)
    gate_two = raw[2 * LOCAL :, :]
    gate_out[...] = gate_two
    grad_out[...] = out_grad

    offset = rank[0] * CHUNK
    starts, lengths = clip_bounds(clip_len[...], clip_order[...])
    begin = to_column(starts, CLIPS)
    end = begin + to_column(lengths, CLIPS)
    time = (offset + lax.broadcasted_iota(jnp.int32, (CLIPS, CHUNK), 1)).astype(F32)
    member = jnp.where((time >= begin) & (time < end), 1.0, 0.0)
    member = jnp.concatenate([member, jnp.zeros((128 - CLIPS, CHUNK), F32)], 0)
    wide = inputs.astype(F32)
    squares = jnp.sum(wide * wide, 0, keepdims=True)
    power = dot(jnp.broadcast_to(squares, (8, CHUNK)), member, ((1,), (1,)), HIGHEST)[:1, :]
    high, low = split(power)

    step = offset + lax.broadcasted_iota(jnp.int32, (BANDS, CHUNK), 1)
    band = 1 + lax.broadcasted_iota(jnp.int32, (BANDS, CHUNK), 0)
    phases = ((step * band) & (TOTAL - 1)).astype(F32) * (2.0 * math.pi / TOTAL)
    ramp = (offset + lax.broadcasted_iota(jnp.int32, (8, CHUNK), 1)).astype(F32) * (1.0 / TOTAL)
    first_row = lax.broadcasted_iota(jnp.int32, (8, HIDDEN), 0) == 0
    ramp_weight = jnp.where(first_row, filt_in[:8, :], 0.0)
    hidden = jnp.sin(
        dot(ramp_weight, ramp, first, HIGHEST)
        + dot(filt_in[1 : 1 + BANDS, :], jnp.cos(phases), first, HIGHEST)
        + dot(filt_in[1 + BANDS : 1 + 2 * BANDS, :], jnp.sin(phases), first, HIGHEST)
    )
    hidden_out[...] = hidden
    rows = lax.broadcasted_iota(jnp.int32, (LOCAL, LOCAL), 0)
    columns = lax.broadcasted_iota(jnp.int32, (LOCAL, LOCAL), 1)
    for i in range(2):
        spread = jnp.broadcast_to(decay[i : i + 1, :], (LOCAL, LOCAL))
        rate = jnp.sum(jnp.where(rows == columns, spread, 0.0), 1, keepdims=True)
        window = jnp.exp(-rate * ramp[:1, :]) * TOTAL ** (-0.5)
        window_out[i * LOCAL : (i + 1) * LOCAL, :] = window

    channel = lax.broadcasted_iota(jnp.int32, (1, LOCAL), 1) == rank[0] % LOCAL
    skips = jnp.sum(jnp.where(channel, skip_gain[...], 0.0), 1, keepdims=True)
    empty = jnp.zeros((1, 128 - CLIPS), F32)
    backward = jnp.full((1, 128), rank[0] // LOCAL, jnp.int32).astype(F32)
    rows = [
        jnp.concatenate([starts, empty], 1),
        jnp.concatenate([lengths, empty], 1),
        jnp.broadcast_to(skips[:1, :], (1, 128)),
        jnp.broadcast_to(skips[1:, :], (1, 128)),
        backward,
        jnp.zeros((3, 128), F32),
    ]
    notes[...] = jnp.concatenate(rows, 0)

    arrays = [raw[:LOCAL, :], raw[LOCAL : 2 * LOCAL, :], gate_two * out_grad]
    for at, values in enumerate(arrays):
        scratch[pl.ds(2 * at, LOCAL, stride=SEND_ROWS), :] = values[:, :128]
        scratch[pl.ds(2 * at + 1, LOCAL, stride=SEND_ROWS), :] = values[:, 128:]
    for at, values in enumerate([high, low]):
        scratch[pl.ds(6 + at, LOCAL, stride=SEND_ROWS), :] = jnp.broadcast_to(
            values.astype(F32), (LOCAL, 128)
        )
    packed = scratch[...].astype(BF16)
    send[: LOCAL * SEND_ROWS, :] = packed
    send[LOCAL * SEND_ROWS :, :] = packed


def to_spectrum(signals, cosines, sines, analysis, inner):
    rows = dot(analysis[...], jnp.concatenate(signals, 1).astype(BF16))
    twisted = []
    for at in range(len(signals)):
        real = rows[:128, 256 * at : 256 * at + 256]
        imag = rows[128:, 256 * at : 256 * at + 256]
        parts = [cosines * real + sines * imag, cosines * imag - sines * real]
        twisted.append(jnp.concatenate(parts, 1).astype(BF16))
    spectra = dot(jnp.concatenate(twisted, 0), inner[...])
    pairs = [spectra[128 * at : 128 * at + 128, :] for at in range(len(signals))]
    return [(pair[:, :256], pair[:, 256:]) for pair in pairs]


def to_signal(spectra, cosines, sines, synthesis, inner):
    stacked = [jnp.concatenate(pair, 1).astype(BF16) for pair in spectra]
    rows = dot(jnp.concatenate(stacked, 0), inner[...])
    columns = []
    for at in range(len(spectra)):
        real = rows[128 * at : 128 * at + 128, :256]
        imag = rows[128 * at : 128 * at + 128, 256:]
        parts = [cosines * real - sines * imag, cosines * imag + sines * real]
        columns.append(jnp.concatenate(parts, 0).astype(BF16))
    signals = dot(synthesis, jnp.concatenate(columns, 1))
    return [signals[:, 256 * at : 256 * at + 256] for at in range(len(spectra))]


WAVE = (6.2831826, -41.341423, 81.59618, -76.5801, 41.205395, -12.271262)


def sine(turns):
    rest = turns - jnp.floor(turns + 0.5)
    square = rest * rest
    value = jnp.full_like(rest, WAVE[-1])
    for factor in WAVE[-2::-1]:
        value = value * square + factor
    return value * rest


def filter_kernel(
    rank, filt_in, filt_out, decay, wave_first, wave_second, pick_first, pick_second, factors,
    analysis, forward, twist_cos, twist_sin, spectra, weight_one, weight_two, out_one, out_two,
    shapes,
):
    channel = rank[0] % LOCAL
    first = ((0,), (0,))
    groups = 8 * HIDDEN
    row = lax.broadcasted_iota(jnp.int32, (groups, HIDDEN), 0)
    column = lax.broadcasted_iota(jnp.int32, (groups, HIDDEN), 1)
    repeat = jnp.where(row // 8 == column, 1.0, 0.0)
    for pick, target in [(pick_first, weight_one), (pick_second, weight_two)]:
        weights = dot(filt_in[:32, :], pick[:32, :], first, HIGHEST) + dot(
            filt_in[25:33, :], pick[32:, :], first, HIGHEST
        )
        target[...] = dot(repeat, weights * (0.5 / math.pi), precision=HIGHEST)
    lane = lax.broadcasted_iota(jnp.int32, (1, LOCAL), 1)
    here = lax.broadcasted_iota(jnp.int32, (LOCAL, HIDDEN), 0) == channel
    for i, target in enumerate([out_one, out_two]):
        mine = jnp.where(here, filt_out[i * LOCAL : (i + 1) * LOCAL, :], 0.0)
        spread = jnp.broadcast_to(
            to_column(jnp.sum(mine, 0, keepdims=True), HIDDEN), (HIDDEN, 128)
        )
        target[...] = dot(repeat, spread, precision=HIGHEST)
    rates = jnp.sum(jnp.where(lane == channel, decay[...], 0.0), 1, keepdims=True)
    count = 2 * BANDS + 2
    exact = lax.broadcasted_iota(jnp.int32, (groups, 128), 1) < 2 * count

    def block(at, carry):
        rows = pl.ds(pl.multiple_of(at * 8, 8), 8)

        def repeated(values):
            return jnp.broadcast_to(values[None], (HIDDEN, 8, 128)).reshape(groups, 128)

        sums = repeated(wave_first[rows, :]) * weight_one[...]
        sums = sums + repeated(wave_second[rows, :]) * weight_two[...]
        high = sums.astype(BF16).astype(F32)
        hidden = sine(dot(jnp.where(exact, high, sums - high).astype(BF16), factors[...]))
        for i, target in enumerate([out_one, out_two]):
            factor = target[...]
            product = hidden * jnp.concatenate([factor, factor], 1)
            shapes[i, rows, :] = jnp.sum(product.reshape(HIDDEN, 8, CHUNK), 0)
        return carry

    lax.fori_loop(0, SEQ // 8, block, 0)
    time = lax.broadcasted_iota(jnp.int32, (SEQ, CHUNK), 0) * CHUNK + lax.broadcasted_iota(
        jnp.int32, (SEQ, CHUNK), 1
    )
    ramp = time.astype(F32) * (1.0 / TOTAL)
    windows = [jnp.exp(-rates[i : i + 1, :] * ramp) * TOTAL ** (-0.5) for i in range(2)]
    both = to_spectrum(
        [shapes[i] * windows[i] for i in range(2)], twist_cos[...], twist_sin[...], analysis, forward
    )
    for i, (real, imag) in enumerate(both):
        spectra[128 * i : 128 * i + 128, :256] = real
        spectra[128 * i : 128 * i + 128, 256:] = imag


def series_kernel(
    notes, received, filters, analysis, synthesis, forward, backward, twist_cos, twist_sin,
    back, skips, scratch, packed,
):
    starts = notes[:1, :]
    counts = jnp.maximum(notes[1:2, :], 1.0)
    skip_one = notes[2:3, :1]
    skip_two = notes[3:4, :1]
    role = notes[4:5, :1]
    scratch[...] = received[...].astype(F32)

    def plane(row):
        return scratch[pl.ds(row, SEQ, stride=SEND_ROWS), :]

    def signal(at):
        return jnp.concatenate([plane(2 * at), plane(2 * at + 1)], 1)

    power = jnp.sum(plane(6) + plane(7), 0, keepdims=True)
    time = lax.broadcasted_iota(jnp.int32, (SEQ, CHUNK), 0) * CHUNK + lax.broadcasted_iota(
        jnp.int32, (SEQ, CHUNK), 1
    )
    time = time.astype(F32)
    lane = lax.broadcasted_iota(jnp.int32, (1, 128), 1)
    inverse_rms = lax.rsqrt(power / (WIDTH * counts) + EPSILON)
    scale = jnp.zeros((SEQ, CHUNK), F32)
    for p in range(CLIPS):
        scale = jnp.where(time >= starts[:, p : p + 1], inverse_rms[:, p : p + 1], scale)

    cosines = twist_cos[...]
    sines = twist_sin[...]

    def analyse(signals):
        return to_spectrum(signals, cosines, sines, analysis, forward)

    def synthesise(parts, table):
        return to_signal(parts, cosines, sines, table, backward)

    def times(a, b, sign):
        return (a[0] * b[0] - sign * (a[1] * b[1]), a[1] * b[0] + sign * (a[0] * b[1]))

    def half(values):
        lower = values[:PARTS, :]
        upper = values[PARTS:, :]
        return jnp.where(jnp.broadcast_to(role, lower.shape) == 0.0, lower, upper)

    value = signal(0) * scale
    gate_one = signal(1) * scale
    scaled_two = signal(2) * scale
    value_spec, second_spec = analyse([value, scaled_two])
    filter_one, filter_two = [
        (filters[128 * i : 128 * i + 128, :256], filters[128 * i : 128 * i + 128, 256:])
        for i in range(2)
    ]
    carry_one, level_grad = synthesise(
        [times(value_spec, filter_one, 1.0), times(second_spec, filter_two, -1.0)],
        synthesis[...],
    )
    carry_one = carry_one + skip_one * value
    level_grad = level_grad + skip_two * scaled_two
    level_one = gate_one * carry_one
    scaled_one = gate_one * level_grad
    level_spec, first_spec = analyse([level_one, scaled_one])
    carry_two, shape_two, value_grad, shape_one = synthesise(
        [
            times(level_spec, filter_two, 1.0),
            times(second_spec, level_spec, -1.0),
            times(first_spec, filter_one, -1.0),
            times(first_spec, value_spec, -1.0),
        ],
        half(synthesis[...].astype(F32)).astype(BF16),
    )
    scale_half = half(scale)
    carry_two = scale_half * (carry_two + skip_two * half(level_one))
    value_grad = scale_half * (value_grad + skip_one * half(scaled_one))
    gate_grad = scale_half * half(level_grad * carry_one)

    def total(values):
        return jnp.sum(jnp.sum(values, 0, keepdims=True), 1, keepdims=True)

    skip_row = jnp.zeros((1, 128), F32)
    for at, skip_grad in enumerate([total(scaled_one * value), total(scaled_two * level_one)]):
        high, low = split(skip_grad)
        mid = low.astype(F32)
        low = skip_grad - high.astype(F32) - mid
        for to, part in enumerate([high.astype(F32), mid, low]):
            skip_row = jnp.where(lane == 3 * at + to, part, skip_row)
    for at, values in enumerate([carry_two, shape_two, value_grad, shape_one, gate_grad]):
        packed[pl.ds(2 * at, PARTS, stride=BACK_ROWS), :] = values[:, :128]
        packed[pl.ds(2 * at + 1, PARTS, stride=BACK_ROWS), :] = values[:, 128:]
    skips[...] = jnp.broadcast_to(skip_row, (8, 128))
    back[...] = packed[...].astype(BF16)


def returned_signal(scratch, at):
    rows = [scratch[pl.ds(2 * at + half, LOCAL, stride=BACK_ROWS), :] for half in range(2)]
    return jnp.concatenate(rows, 1)


def weight_kernel(
    received, full, gate_in, grad_in, hidden, window, weights, gated_out, scaled_out,
    scratch, packed,
):
    scratch[...] = received[...].astype(F32)
    carry = returned_signal(scratch, 0)
    gated = (gate_in[...] * carry).astype(BF16)
    scaled_grad = jnp.concatenate(
        [
            returned_signal(scratch, 2).astype(BF16),
            returned_signal(scratch, 4).astype(BF16),
            (grad_in[...] * carry).astype(BF16),
        ],
        0,
    )
    gated_out[...] = gated
    scaled_out[...] = scaled_grad
    inputs = jnp.concatenate([full[128 * j : 128 * j + 64, :] for j in range(4)], 0)
    cotangent = jnp.concatenate([full[128 * j + 64 : 128 * j + 128, :] for j in range(4)], 0)
    last = ((1,), (1,))
    in_weight = dot(scaled_grad, inputs, last)
    out_weight = dot(gated, cotangent, last)
    blank = jnp.zeros((LOCAL, CHUNK), F32)
    shape_one = returned_signal(scratch, 3) * window[:LOCAL, :]
    shape_two = returned_signal(scratch, 1) * window[LOCAL:, :]
    filter_grad = dot(
        shape_one, jnp.concatenate([hidden[...], blank], 0), last, HIGHEST
    ) + dot(shape_two, jnp.concatenate([blank, hidden[...]], 0), last, HIGHEST)
    rows = [
        in_weight[64 * at : 64 * at + 64, 128 * half : 128 * half + 128]
        for at in range(3)
        for half in range(2)
    ]
    rows += [out_weight[:, :128], out_weight[:, 128:], filter_grad, jnp.zeros((PARTS, 128), F32)]
    for at, values in enumerate(rows):
        packed[pl.ds(at, PARTS, stride=PART_ROWS), :] = values
    weights[...] = packed[...].astype(BF16)


def channel_kernel(place, gated, scaled_grad, in_proj, out_proj, given, kept):
    first = ((0,), (0,))
    mixed = dot(out_proj[...], gated[...], first)
    grad_inputs = dot(in_proj[...], scaled_grad[...], first)
    even = place[0] % 2 == 0
    for at in range(2):
        for to, values in enumerate([mixed, grad_inputs]):
            low = values[128 * at : 128 * at + 64, :]
            high = values[128 * at + 64 : 128 * at + 128, :]
            rows = slice(128 * at + 64 * to, 128 * at + 64 * to + 64)
            given[rows, :] = jnp.where(even, high, low).astype(BF16)
            kept[rows, :] = jnp.where(even, low, high)


def core_kernel(place, received, kept, given, left):
    total = kept[...] + received[...].astype(F32)
    near = place[0] < 2
    given[...] = jnp.where(near, total[128:, :], total[:128, :]).astype(BF16)
    left[...] = jnp.where(near, total[:128, :], total[128:, :])


def sum_kernel(received, skips, spread):
    four = 4 * PART_ROWS
    parts = jnp.sum(received[...].astype(F32).reshape(PARTS // 4, four, 128), 0)
    total = sum(parts[PART_ROWS * at : PART_ROWS * at + PART_ROWS, :] for at in range(4))
    row = lax.broadcasted_iota(jnp.int32, (PART_ROWS, 128), 0)
    total = jnp.where(row == PART_ROWS - 1, skips[:1, :], total * TOTAL ** (-0.5))
    total = jnp.concatenate([total] * 4, 0)
    total = jnp.broadcast_to(total[None], (SEQ // 4, four, 128)).reshape(SEQ * PART_ROWS, 128)
    spread[...] = total.astype(BF16)


def last_kernel(
    received, over_chips, left, mixed, grad_inputs, in_weight, out_weight, filter_grad, skip_grad,
    scratch,
):
    summed = (left[...] + over_chips[...].astype(F32)).astype(BF16)
    mixed[...] = summed[:64, :]
    grad_inputs[...] = summed[64:, :]
    scratch[...] = received[...].astype(F32)

    def block(at):
        first = scratch[pl.ds(at, PARTS, stride=PART_ROWS), :]
        return first + scratch[pl.ds(PARTS * PART_ROWS + at, PARTS, stride=PART_ROWS), :]

    for half in range(2):
        for at in range(3):
            in_weight[64 * at : 64 * at + 64, 128 * half : 128 * half + 128] = block(2 * at + half)
        out_weight[:, 128 * half : 128 * half + 128] = block(6 + half)
    filters = block(8)
    filter_grad[:LOCAL, :] = filters[:, :HIDDEN]
    filter_grad[LOCAL:, :] = filters[:, HIDDEN:]
    lane = lax.broadcasted_iota(jnp.int32, (8, 128), 1)
    order = lax.broadcasted_iota(jnp.int32, (8, 128), 0)
    pick = jnp.where((lane >= 3 * order) & (lane < 3 * order + 3), 1.0, 0.0).astype(BF16)
    skips = scratch[pl.ds(PART_ROWS - 1, PARTS, stride=PART_ROWS), :].astype(BF16)
    skip_grad[...] = dot(pick, skips, ((1,), (1,)))[:2, :] * TOTAL ** (-0.5)


def call(kernel, name, outs, scalars, arrays, scratch=()):
    def vmem():
        return pl.BlockSpec(memory_space=pltpu.VMEM)

    return pl.pallas_call(
        kernel,
        name=name,
        out_shape=[jax.ShapeDtypeStruct(shape, kind) for shape, kind in outs],
        in_specs=[pl.BlockSpec(memory_space=pltpu.SMEM)] * scalars + [vmem() for _ in range(arrays)],
        out_specs=[vmem() for _ in outs],
        scratch_shapes=[pltpu.VMEM(shape, F32) for shape in scratch],
        compiler_params=pltpu.CompilerParams(vmem_limit_bytes=32 * 1024 * 1024),
    )


def front():
    return call(
        front_kernel,
        "project",
        [
            ((SEQ * SEND_ROWS, 128), BF16),
            ((LOCAL, CHUNK), F32),
            ((LOCAL, CHUNK), F32),
            ((HIDDEN, CHUNK), F32),
            ((2 * LOCAL, CHUNK), F32),
            ((8, 128), F32),
        ],
        1,
        8,
        [(LOCAL * SEND_ROWS, 128)],
    )


def filtering():
    return call(
        filter_kernel,
        "filters",
        [((2 * SEQ, 2 * CHUNK), F32)],
        1,
        12,
        [(8 * HIDDEN, 128)] * 4 + [(2, SEQ, CHUNK)],
    )


def series():
    return call(
        series_kernel,
        "convolve",
        [((PARTS * BACK_ROWS, 128), BF16), ((8, 128), F32)],
        0,
        9,
        [(SEQ * SEND_ROWS, 128), (PARTS * BACK_ROWS, 128)],
    )


def weighing():
    return call(
        weight_kernel,
        "weigh",
        [
            ((PARTS * PART_ROWS, 128), BF16),
            ((LOCAL, CHUNK), BF16),
            ((3 * LOCAL, CHUNK), BF16),
        ],
        0,
        6,
        [(PARTS * BACK_ROWS, 128), (PARTS * PART_ROWS, 128)],
    )


def channels():
    return call(channel_kernel, "mix", [((256, CHUNK), BF16), ((256, CHUNK), F32)], 1, 4)


def core_sum():
    return call(core_kernel, "add_core", [((128, CHUNK), BF16), ((128, CHUNK), F32)], 1, 2)


def total():
    return call(sum_kernel, "add_up", [((SEQ * PART_ROWS, 128), BF16)], 0, 2)


def finish():
    return call(
        last_kernel,
        "unpack",
        [
            ((64, CHUNK), BF16),
            ((64, CHUNK), BF16),
            ((3 * LOCAL, WIDTH), F32),
            ((LOCAL, WIDTH), F32),
            ((2 * LOCAL, HIDDEN), F32),
            ((2, LOCAL), F32),
        ],
        0,
        3,
        [(SEQ * PART_ROWS, 128)],
    )


def swap(values, group, among=None):
    tiles = values.reshape(values.shape[0] // group, group, 128)
    tiles = lax.all_to_all(
        tiles, "seq", split_axis=0, concat_axis=0, axis_index_groups=among, tiled=True
    )
    return tiles.reshape(values.shape)


def shards(
    inputs,
    clip_len,
    clip_order,
    in_proj,
    out_proj,
    filt_in,
    filt_out,
    decay_rate,
    skip_gain,
    cotangent,
):
    rank = lax.axis_index("seq").astype(jnp.int32).reshape(1)
    place = lax.axis_index("ch").astype(jnp.int32).reshape(1)
    rank, place = lax.optimization_barrier((rank, place))
    halves = [list(range(at * PARTS, at * PARTS + PARTS)) for at in range(SEQ // PARTS)]
    in_rows = in_proj.reshape(3 * LOCAL, WIDTH)
    out_rows = out_proj.T
    full = lax.all_gather(jnp.concatenate([inputs, cotangent], 0), "ch", axis=0, tiled=True)
    send, gate_two, out_grad, hidden, window, notes = front()(
        rank, clip_len.reshape(1, CLIPS), clip_order.reshape(1, CLIPS), skip_gain, full, in_rows,
        out_rows, filt_in, decay_rate,
    )
    received = swap(send, 4)
    analysis, synthesis, forward, backward, twist_cos, twist_sin = [
        jnp.asarray(x) for x in tables()
    ]
    (spectra,) = filtering()(
        rank, filt_in, filt_out.reshape(2 * LOCAL, HIDDEN), decay_rate,
        *[jnp.asarray(x) for x in wave_tables()], analysis, forward, twist_cos, twist_sin,
    )
    back, skips = series()(
        notes, received, spectra, analysis, synthesis, forward, backward, twist_cos, twist_sin
    )
    returned = swap(back, 2, halves)
    weights, gated, scaled_grad = weighing()(
        returned, full, gate_two, out_grad, hidden, window
    )
    given, kept = channels()(place, gated, scaled_grad, in_rows, out_rows)
    over_cores = lax.ppermute(given, "ch", [(0, 1), (1, 0), (2, 3), (3, 2)])
    given, left = core_sum()(place, over_cores, kept)
    (spread,) = total()(swap(weights, 2, halves), skips)
    spread, given = lax.optimization_barrier((spread, given))
    over_chips = lax.ppermute(given, "ch", [(0, 2), (2, 0), (1, 3), (3, 1)])
    mixed, grad_inputs, in_weight, out_weight, filter_grad, grad_skip = finish()(
        swap(spread, 2), over_chips, left
    )
    return (
        mixed,
        grad_inputs,
        in_weight.reshape(3, LOCAL, WIDTH),
        out_weight.T,
        filter_grad.reshape(2, LOCAL, HIDDEN),
        grad_skip,
    )


def solution(mesh):
    return jax.shard_map(
        shards,
        mesh=mesh,
        in_specs=(
            P("ch", "seq"),
            P(),
            P(),
            P(None, "ch", None),
            P(None, "ch"),
            P(),
            P(None, "ch", None),
            P(None, "ch"),
            P(None, "ch"),
            P("ch", "seq"),
        ),
        out_specs=(
            P("ch", "seq"),
            P("ch", "seq"),
            P(None, "ch", None),
            P(None, "ch"),
            P(None, "ch", None),
            P(None, "ch"),
        ),
        check_vma=False,
    )
```

```python
import functools
import math

import jax
import jax.numpy as jnp
import numpy as np
from jax import lax
from jax.experimental import pallas as pl
from jax.experimental.pallas import tpu as pltpu
from jax.sharding import PartitionSpec as P

EPSILON = 1e-05
HIGHEST = lax.Precision.HIGHEST
F32 = jnp.float32
BF16 = jnp.bfloat16

WIDTH = 256
TOTAL = 32768
SEQ = 128
CHUNK = 256
LOCAL = 64
HIDDEN = 64
BANDS = 16
CLIPS = 16
SEND_ROWS = 8
BACK_ROWS = 10
SPARE = 16
PART_ROWS = 10
PARTS = 64


def tables():
    k1 = np.arange(SEQ)[:, None] + 0.25
    s = np.arange(SEQ)[None, :]
    u = np.arange(CHUNK)[None, :]
    first = 2.0 * np.pi * k1 * s / SEQ
    analysis = np.concatenate([np.cos(first), -np.sin(first)], 0).astype(np.float32)
    synthesis = (np.concatenate([np.cos(first), -np.sin(first)], 0).T / TOTAL).astype(np.float32)
    twist = 2.0 * np.pi * k1 * u / TOTAL
    k2 = np.arange(CHUNK)
    second = 2.0 * np.pi * ((k2[:, None] * k2[None, :]) % CHUNK) / CHUNK
    cosines, sines = np.cos(second), np.sin(second)
    forward = np.block([[cosines, -sines], [sines, cosines]]).astype(np.float32)
    return (
        analysis.astype(BF16),
        synthesis.astype(BF16),
        forward.astype(BF16),
        forward.T.astype(BF16),
        np.cos(twist).astype(np.float32),
        np.sin(twist).astype(np.float32),
    )


def wave_tables():
    f = np.arange(1, BANDS + 1)
    count = 2 * BANDS + 2
    chunk = 2.0 * np.pi * (f[None, :] * np.arange(SEQ)[:, None] % SEQ) / SEQ
    sample = 2.0 * np.pi * f[:, None] * np.arange(CHUNK)[None, :] / TOTAL
    cosines, sines = np.cos(chunk), np.sin(chunk)
    ramp = np.arange(SEQ)[:, None] / SEQ
    ones = np.ones((SEQ, 1))
    first = np.concatenate([cosines, cosines, ramp, ones], 1)
    second = np.concatenate([sines, -sines, 0 * ones, 0 * ones], 1)
    inner = np.concatenate(
        [
            np.cos(sample),
            np.sin(sample),
            np.ones((1, CHUNK)),
            np.arange(CHUNK)[None, :] / TOTAL,
        ],
        0,
    ).astype(np.float32)
    high = inner.astype(BF16)
    low = (inner - high.astype(np.float32)).astype(BF16)
    pick_first = np.zeros((1 + 2 * BANDS, count))
    pick_second = np.zeros((1 + 2 * BANDS, count))
    for band in range(BANDS):
        pick_first[1 + band, band] = 1
        pick_first[1 + BANDS + band, BANDS + band] = 1
        pick_second[1 + BANDS + band, band] = 1
        pick_second[1 + band, BANDS + band] = 1
    pick_first[0, 2 * BANDS :] = 1

    def lanes(table):
        wide = np.zeros((table.shape[0], 128), np.float32)
        wide[:, : 3 * count] = np.concatenate([table] * 3, 1)
        return wide

    def rows(table):
        wide = np.zeros((40, 128), np.float32)
        wide[:32] = lanes(table)[:32]
        wide[39] = lanes(table)[32]
        return wide

    factors = np.zeros((128, CHUNK), BF16)
    factors[: 3 * count] = np.concatenate([high, low, high], 0)
    return lanes(first), lanes(second), rows(pick_first), rows(pick_second), factors


def dot(a, b, dims=((1,), (0,)), precision=None):
    return lax.dot_general(a, b, (dims, ((), ())), precision=precision, preferred_element_type=F32)


def split(x):
    high = x.astype(BF16)
    return high, (x - high.astype(F32)).astype(BF16)


def to_column(row, count):
    shape = (count, count)
    rows = lax.broadcasted_iota(jnp.int32, shape, 0)
    columns = lax.broadcasted_iota(jnp.int32, shape, 1)
    spread = jnp.broadcast_to(row, shape)
    return jnp.sum(jnp.where(rows == columns, spread, jnp.zeros_like(spread)), 1, keepdims=True)


def clip_bounds(clip_len, clip_order):
    shape = (CLIPS, CLIPS)
    rows = lax.broadcasted_iota(jnp.int32, shape, 0)
    columns = lax.broadcasted_iota(jnp.int32, shape, 1)
    sizes = to_column(clip_len.astype(F32), CLIPS)
    lengths = jnp.sum(jnp.where(rows == clip_order, sizes, 0.0), 0, keepdims=True)
    starts = jnp.sum(
        jnp.where(rows < columns, to_column(lengths, CLIPS), 0.0), 0, keepdims=True
    )
    return starts, lengths


def front_kernel(
    rank, clip_len, clip_order, skip_gain, full, in_proj, out_proj, filt_in, decay,
    send, gate_out, grad_out, hidden_out, window_out, notes, scratch,
):
    first = ((0,), (0,))
    inputs = jnp.concatenate([full[128 * j : 128 * j + 64, :] for j in range(4)], 0)
    cotangent = jnp.concatenate([full[128 * j + 64 : 128 * j + 128, :] for j in range(4)], 0)
    raw = dot(in_proj[...], inputs)
    out_grad = dot(out_proj[...], cotangent)
    gate_two = raw[2 * LOCAL :, :]
    gate_out[...] = gate_two
    grad_out[...] = out_grad

    offset = rank[0] * CHUNK
    starts, lengths = clip_bounds(clip_len[...], clip_order[...])
    begin = to_column(starts, CLIPS)
    end = begin + to_column(lengths, CLIPS)
    time = (offset + lax.broadcasted_iota(jnp.int32, (CLIPS, CHUNK), 1)).astype(F32)
    member = jnp.where((time >= begin) & (time < end), 1.0, 0.0)
    member = jnp.concatenate([member, jnp.zeros((128 - CLIPS, CHUNK), F32)], 0)
    wide = inputs.astype(F32)
    squares = jnp.sum(wide * wide, 0, keepdims=True)
    power = dot(jnp.broadcast_to(squares, (8, CHUNK)), member, ((1,), (1,)), HIGHEST)[:1, :]
    high, low = split(power)

    step = offset + lax.broadcasted_iota(jnp.int32, (BANDS, CHUNK), 1)
    band = 1 + lax.broadcasted_iota(jnp.int32, (BANDS, CHUNK), 0)
    phases = ((step * band) & (TOTAL - 1)).astype(F32) * (2.0 * math.pi / TOTAL)
    ramp = (offset + lax.broadcasted_iota(jnp.int32, (8, CHUNK), 1)).astype(F32) * (1.0 / TOTAL)
    first_row = lax.broadcasted_iota(jnp.int32, (8, HIDDEN), 0) == 0
    ramp_weight = jnp.where(first_row, filt_in[:8, :], 0.0)
    hidden = jnp.sin(
        dot(ramp_weight, ramp, first, HIGHEST)
        + dot(filt_in[1 : 1 + BANDS, :], jnp.cos(phases), first, HIGHEST)
        + dot(filt_in[1 + BANDS : 1 + 2 * BANDS, :], jnp.sin(phases), first, HIGHEST)
    )
    hidden_out[...] = hidden
    rows = lax.broadcasted_iota(jnp.int32, (LOCAL, LOCAL), 0)
    columns = lax.broadcasted_iota(jnp.int32, (LOCAL, LOCAL), 1)
    for i in range(2):
        spread = jnp.broadcast_to(decay[i : i + 1, :], (LOCAL, LOCAL))
        rate = jnp.sum(jnp.where(rows == columns, spread, 0.0), 1, keepdims=True)
        window = jnp.exp(-rate * ramp[:1, :]) * TOTAL ** (-0.5)
        window_out[i * LOCAL : (i + 1) * LOCAL, :] = window

    channel = lax.broadcasted_iota(jnp.int32, (1, LOCAL), 1) == rank[0] % LOCAL
    skips = jnp.sum(jnp.where(channel, skip_gain[...], 0.0), 1, keepdims=True)
    empty = jnp.zeros((1, 128 - CLIPS), F32)
    backward = jnp.full((1, 128), rank[0] // LOCAL, jnp.int32).astype(F32)
    rows = [
        jnp.concatenate([starts, empty], 1),
        jnp.concatenate([lengths, empty], 1),
        jnp.broadcast_to(skips[:1, :], (1, 128)),
        jnp.broadcast_to(skips[1:, :], (1, 128)),
        backward,
        jnp.zeros((3, 128), F32),
    ]
    notes[...] = jnp.concatenate(rows, 0)

    arrays = [raw[:LOCAL, :], raw[LOCAL : 2 * LOCAL, :], gate_two * out_grad]
    for at, values in enumerate(arrays):
        scratch[pl.ds(2 * at, LOCAL, stride=SEND_ROWS), :] = values[:, :128]
        scratch[pl.ds(2 * at + 1, LOCAL, stride=SEND_ROWS), :] = values[:, 128:]
    for at, values in enumerate([high, low]):
        scratch[pl.ds(6 + at, LOCAL, stride=SEND_ROWS), :] = jnp.broadcast_to(
            values.astype(F32), (LOCAL, 128)
        )
    packed = scratch[: LOCAL * SEND_ROWS, :].astype(BF16)
    send[: LOCAL * SEND_ROWS, :] = packed
    send[LOCAL * SEND_ROWS :, :] = packed


def to_spectrum(signals, cosines, sines, analysis, inner):
    rows = dot(analysis[...], jnp.concatenate(signals, 1).astype(BF16))
    twisted = []
    for at in range(len(signals)):
        real = rows[:128, 256 * at : 256 * at + 256]
        imag = rows[128:, 256 * at : 256 * at + 256]
        parts = [cosines * real + sines * imag, cosines * imag - sines * real]
        twisted.append(jnp.concatenate(parts, 1).astype(BF16))
    spectra = dot(jnp.concatenate(twisted, 0), inner[...])
    pairs = [spectra[128 * at : 128 * at + 128, :] for at in range(len(signals))]
    return [(pair[:, :256], pair[:, 256:]) for pair in pairs]


def to_signal(spectra, cosines, sines, synthesis, inner):
    stacked = [jnp.concatenate(pair, 1).astype(BF16) for pair in spectra]
    rows = dot(jnp.concatenate(stacked, 0), inner[...])
    columns = []
    for at in range(len(spectra)):
        real = rows[128 * at : 128 * at + 128, :256]
        imag = rows[128 * at : 128 * at + 128, 256:]
        parts = [cosines * real - sines * imag, cosines * imag + sines * real]
        columns.append(jnp.concatenate(parts, 0).astype(BF16))
    signals = dot(synthesis, jnp.concatenate(columns, 1))
    return [signals[:, 256 * at : 256 * at + 256] for at in range(len(spectra))]


WAVE = (6.2831826, -41.341423, 81.59618, -76.5801, 41.205395, -12.271262)


def sine(turns):
    rest = turns - jnp.floor(turns + 0.5)
    square = rest * rest
    value = jnp.full_like(rest, WAVE[-1])
    for factor in WAVE[-2::-1]:
        value = value * square + factor
    return value * rest


def filter_kernel(
    rank, filt_in, filt_out, decay, wave_first, wave_second, pick_first, pick_second, factors,
    analysis, forward, twist_cos, twist_sin, spectra, weight_one, weight_two, out_one, out_two,
    shapes,
):
    channel = rank[0] % LOCAL
    first = ((0,), (0,))
    groups = 8 * HIDDEN
    row = lax.broadcasted_iota(jnp.int32, (groups, HIDDEN), 0)
    column = lax.broadcasted_iota(jnp.int32, (groups, HIDDEN), 1)
    repeat = jnp.where(row // 8 == column, 1.0, 0.0)
    for pick, target in [(pick_first, weight_one), (pick_second, weight_two)]:
        weights = dot(filt_in[:32, :], pick[:32, :], first, HIGHEST) + dot(
            filt_in[25:33, :], pick[32:, :], first, HIGHEST
        )
        target[...] = dot(repeat, weights * (0.5 / math.pi), precision=HIGHEST)
    lane = lax.broadcasted_iota(jnp.int32, (1, LOCAL), 1)
    here = lax.broadcasted_iota(jnp.int32, (LOCAL, HIDDEN), 0) == channel
    for i, target in enumerate([out_one, out_two]):
        mine = jnp.where(here, filt_out[i * LOCAL : (i + 1) * LOCAL, :], 0.0)
        spread = jnp.broadcast_to(
            to_column(jnp.sum(mine, 0, keepdims=True), HIDDEN), (HIDDEN, 128)
        )
        target[...] = dot(repeat, spread, precision=HIGHEST)
    rates = jnp.sum(jnp.where(lane == channel, decay[...], 0.0), 1, keepdims=True)
    count = 2 * BANDS + 2
    exact = lax.broadcasted_iota(jnp.int32, (groups, 128), 1) < 2 * count

    def block(at, carry):
        rows = pl.ds(pl.multiple_of(at * 8, 8), 8)

        def repeated(values):
            return jnp.broadcast_to(values[None], (HIDDEN, 8, 128)).reshape(groups, 128)

        sums = repeated(wave_first[rows, :]) * weight_one[...]
        sums = sums + repeated(wave_second[rows, :]) * weight_two[...]
        high = sums.astype(BF16).astype(F32)
        hidden = sine(dot(jnp.where(exact, high, sums - high).astype(BF16), factors[...]))
        for i, target in enumerate([out_one, out_two]):
            factor = target[...]
            product = hidden * jnp.concatenate([factor, factor], 1)
            shapes[i, rows, :] = jnp.sum(product.reshape(HIDDEN, 8, CHUNK), 0)
        return carry

    lax.fori_loop(0, SEQ // 8, block, 0)
    time = lax.broadcasted_iota(jnp.int32, (SEQ, CHUNK), 0) * CHUNK + lax.broadcasted_iota(
        jnp.int32, (SEQ, CHUNK), 1
    )
    ramp = time.astype(F32) * (1.0 / TOTAL)
    windows = [jnp.exp(-rates[i : i + 1, :] * ramp) * TOTAL ** (-0.5) for i in range(2)]
    both = to_spectrum(
        [shapes[i] * windows[i] for i in range(2)], twist_cos[...], twist_sin[...], analysis, forward
    )
    for i, (real, imag) in enumerate(both):
        spectra[128 * i : 128 * i + 128, :256] = real
        spectra[128 * i : 128 * i + 128, 256:] = imag


def series_kernel(
    notes, received, filters, analysis, synthesis, forward, backward, twist_cos, twist_sin,
    back, skips, scratch, packed,
):
    starts = notes[:1, :]
    counts = jnp.maximum(notes[1:2, :], 1.0)
    skip_one = notes[2:3, :1]
    skip_two = notes[3:4, :1]
    role = notes[4:5, :1]
    scratch[: received.shape[0], :] = received[...].astype(F32)

    def plane(row):
        return scratch[pl.ds(row, SEQ, stride=SEND_ROWS), :]

    def signal(at):
        return jnp.concatenate([plane(2 * at), plane(2 * at + 1)], 1)

    power = jnp.sum(plane(6) + plane(7), 0, keepdims=True)
    time = lax.broadcasted_iota(jnp.int32, (SEQ, CHUNK), 0) * CHUNK + lax.broadcasted_iota(
        jnp.int32, (SEQ, CHUNK), 1
    )
    time = time.astype(F32)
    lane = lax.broadcasted_iota(jnp.int32, (1, 128), 1)
    inverse_rms = lax.rsqrt(power / (WIDTH * counts) + EPSILON)
    scale = jnp.zeros((SEQ, CHUNK), F32)
    for p in range(CLIPS):
        scale = jnp.where(time >= starts[:, p : p + 1], inverse_rms[:, p : p + 1], scale)

    cosines = twist_cos[...]
    sines = twist_sin[...]

    def analyse(signals):
        return to_spectrum(signals, cosines, sines, analysis, forward)

    def synthesise(parts, table):
        return to_signal(parts, cosines, sines, table, backward)

    def times(a, b, sign):
        return (a[0] * b[0] - sign * (a[1] * b[1]), a[1] * b[0] + sign * (a[0] * b[1]))

    def half(values):
        lower = values[:PARTS, :]
        upper = values[PARTS:, :]
        return jnp.where(jnp.broadcast_to(role, lower.shape) == 0.0, lower, upper)

    value = signal(0) * scale
    gate_one = signal(1) * scale
    scaled_two = signal(2) * scale
    value_spec, second_spec = analyse([value, scaled_two])
    filter_one, filter_two = [
        (filters[128 * i : 128 * i + 128, :256], filters[128 * i : 128 * i + 128, 256:])
        for i in range(2)
    ]
    carry_one, level_grad = synthesise(
        [times(value_spec, filter_one, 1.0), times(second_spec, filter_two, -1.0)],
        synthesis[...],
    )
    carry_one = carry_one + skip_one * value
    level_grad = level_grad + skip_two * scaled_two
    level_one = gate_one * carry_one
    scaled_one = gate_one * level_grad
    level_spec, first_spec = analyse([level_one, scaled_one])
    carry_two, shape_two, value_grad, shape_one = synthesise(
        [
            times(level_spec, filter_two, 1.0),
            times(second_spec, level_spec, -1.0),
            times(first_spec, filter_one, -1.0),
            times(first_spec, value_spec, -1.0),
        ],
        half(synthesis[...].astype(F32)).astype(BF16),
    )
    scale_half = half(scale)
    carry_two = scale_half * (carry_two + skip_two * half(level_one))
    value_grad = scale_half * (value_grad + skip_one * half(scaled_one))
    gate_grad = scale_half * half(level_grad * carry_one)

    def total(values):
        return jnp.sum(jnp.sum(values, 0, keepdims=True), 1, keepdims=True)

    skip_row = jnp.zeros((1, 128), F32)
    for at, skip_grad in enumerate([total(scaled_one * value), total(scaled_two * level_one)]):
        high, low = split(skip_grad)
        mid = low.astype(F32)
        low = skip_grad - high.astype(F32) - mid
        for to, part in enumerate([high.astype(F32), mid, low]):
            skip_row = jnp.where(lane == 3 * at + to, part, skip_row)
    for at, values in enumerate([carry_two, shape_two, value_grad, shape_one, gate_grad]):
        packed[pl.ds(2 * at, PARTS, stride=BACK_ROWS), :] = values[:, :128]
        packed[pl.ds(2 * at + 1, PARTS, stride=BACK_ROWS), :] = values[:, 128:]
    skips[...] = jnp.broadcast_to(skip_row, (8, 128))
    back[...] = packed[: back.shape[0], :].astype(BF16)


def returned_signal(scratch, at):
    rows = [scratch[pl.ds(2 * at + half, LOCAL, stride=BACK_ROWS), :] for half in range(2)]
    return jnp.concatenate(rows, 1)


def weight_kernel(
    received, full, gate_in, grad_in, hidden, window, weights, gated_out, scaled_out,
    scratch, packed,
):
    scratch[: received.shape[0], :] = received[...].astype(F32)
    carry = returned_signal(scratch, 0)
    gated = (gate_in[...] * carry).astype(BF16)
    scaled_grad = jnp.concatenate(
        [
            returned_signal(scratch, 2).astype(BF16),
            returned_signal(scratch, 4).astype(BF16),
            (grad_in[...] * carry).astype(BF16),
        ],
        0,
    )
    gated_out[...] = gated
    scaled_out[...] = scaled_grad
    inputs = jnp.concatenate([full[128 * j : 128 * j + 64, :] for j in range(4)], 0)
    cotangent = jnp.concatenate([full[128 * j + 64 : 128 * j + 128, :] for j in range(4)], 0)
    last = ((1,), (1,))
    in_weight = dot(scaled_grad, inputs, last)
    out_weight = dot(gated, cotangent, last)
    blank = jnp.zeros((LOCAL, CHUNK), F32)
    shape_one = returned_signal(scratch, 3) * window[:LOCAL, :]
    shape_two = returned_signal(scratch, 1) * window[LOCAL:, :]
    filter_grad = dot(
        shape_one, jnp.concatenate([hidden[...], blank], 0), last, HIGHEST
    ) + dot(shape_two, jnp.concatenate([blank, hidden[...]], 0), last, HIGHEST)
    rows = [
        in_weight[64 * at : 64 * at + 64, 128 * half : 128 * half + 128]
        for at in range(3)
        for half in range(2)
    ]
    rows += [out_weight[:, :128], out_weight[:, 128:], filter_grad, jnp.zeros((PARTS, 128), F32)]
    for at, values in enumerate(rows):
        packed[pl.ds(at, PARTS, stride=PART_ROWS), :] = values
    weights[...] = packed[: weights.shape[0], :].astype(BF16)


def channel_kernel(place, gated, scaled_grad, in_proj, out_proj, given, kept):
    first = ((0,), (0,))
    mixed = dot(out_proj[...], gated[...], first)
    grad_inputs = dot(in_proj[...], scaled_grad[...], first)
    even = place[0] % 2 == 0
    for at in range(2):
        for to, values in enumerate([mixed, grad_inputs]):
            low = values[128 * at : 128 * at + 64, :]
            high = values[128 * at + 64 : 128 * at + 128, :]
            rows = slice(128 * at + 64 * to, 128 * at + 64 * to + 64)
            given[rows, :] = jnp.where(even, high, low).astype(BF16)
            kept[rows, :] = jnp.where(even, low, high)


def core_kernel(place, received, kept, given, left):
    total = kept[...] + received[...].astype(F32)
    near = place[0] < 2
    given[...] = jnp.where(near, total[128:, :], total[:128, :]).astype(BF16)
    left[...] = jnp.where(near, total[:128, :], total[128:, :])


def sum_kernel(received, skips, spread):
    four = 4 * PART_ROWS
    parts = jnp.sum(received[...].astype(F32).reshape(PARTS // 4, four, 128), 0)
    total = sum(parts[PART_ROWS * at : PART_ROWS * at + PART_ROWS, :] for at in range(4))
    row = lax.broadcasted_iota(jnp.int32, (PART_ROWS, 128), 0)
    total = jnp.where(row == PART_ROWS - 1, skips[:1, :], total * TOTAL ** (-0.5))
    total = jnp.concatenate([total] * 4, 0)
    total = jnp.broadcast_to(total[None], (SEQ // 4, four, 128)).reshape(SEQ * PART_ROWS, 128)
    spread[...] = total.astype(BF16)


def last_kernel(
    received, over_chips, left, mixed, grad_inputs, in_weight, out_weight, filter_grad, skip_grad,
    scratch,
):
    summed = (left[...] + over_chips[...].astype(F32)).astype(BF16)
    mixed[...] = summed[:64, :]
    grad_inputs[...] = summed[64:, :]
    scratch[: received.shape[0], :] = received[...].astype(F32)

    def block(at):
        first = scratch[pl.ds(at, PARTS, stride=PART_ROWS), :]
        return first + scratch[pl.ds(PARTS * PART_ROWS + at, PARTS, stride=PART_ROWS), :]

    for half in range(2):
        for at in range(3):
            in_weight[64 * at : 64 * at + 64, 128 * half : 128 * half + 128] = block(2 * at + half)
        out_weight[:, 128 * half : 128 * half + 128] = block(6 + half)
    filters = block(8)
    filter_grad[:LOCAL, :] = filters[:, :HIDDEN]
    filter_grad[LOCAL:, :] = filters[:, HIDDEN:]
    lane = lax.broadcasted_iota(jnp.int32, (8, 128), 1)
    order = lax.broadcasted_iota(jnp.int32, (8, 128), 0)
    pick = jnp.where((lane >= 3 * order) & (lane < 3 * order + 3), 1.0, 0.0).astype(BF16)
    skips = scratch[pl.ds(PART_ROWS - 1, PARTS, stride=PART_ROWS), :].astype(BF16)
    skip_grad[...] = dot(pick, skips, ((1,), (1,)))[:2, :] * TOTAL ** (-0.5)


def call(kernel, name, outs, scalars, arrays, scratch=(), spare=SPARE):
    def vmem():
        return pl.BlockSpec(memory_space=pltpu.VMEM)

    return pl.pallas_call(
        kernel,
        name=name,
        out_shape=[jax.ShapeDtypeStruct(shape, kind) for shape, kind in outs],
        in_specs=[pl.BlockSpec(memory_space=pltpu.SMEM)] * scalars + [vmem() for _ in range(arrays)],
        out_specs=[vmem() for _ in outs],
        scratch_shapes=[
            pltpu.VMEM((*shape[:-2], shape[-2] + spare, shape[-1]), F32) for shape in scratch
        ],
        compiler_params=pltpu.CompilerParams(vmem_limit_bytes=32 * 1024 * 1024),
    )


def front():
    return call(
        front_kernel,
        "project",
        [
            ((SEQ * SEND_ROWS, 128), BF16),
            ((LOCAL, CHUNK), F32),
            ((LOCAL, CHUNK), F32),
            ((HIDDEN, CHUNK), F32),
            ((2 * LOCAL, CHUNK), F32),
            ((8, 128), F32),
        ],
        1,
        8,
        [(LOCAL * SEND_ROWS, 128)],
    )


def filtering():
    return call(
        filter_kernel,
        "filters",
        [((2 * SEQ, 2 * CHUNK), F32)],
        1,
        12,
        [(8 * HIDDEN, 128)] * 4 + [(2, SEQ, CHUNK)],
        spare=0,
    )


def series():
    return call(
        series_kernel,
        "convolve",
        [((PARTS * BACK_ROWS, 128), BF16), ((8, 128), F32)],
        0,
        9,
        [(SEQ * SEND_ROWS, 128), (PARTS * BACK_ROWS, 128)],
    )


def weighing():
    return call(
        weight_kernel,
        "weigh",
        [
            ((PARTS * PART_ROWS, 128), BF16),
            ((LOCAL, CHUNK), BF16),
            ((3 * LOCAL, CHUNK), BF16),
        ],
        0,
        6,
        [(PARTS * BACK_ROWS, 128), (PARTS * PART_ROWS, 128)],
    )


def channels():
    return call(channel_kernel, "mix", [((256, CHUNK), BF16), ((256, CHUNK), F32)], 1, 4)


def core_sum():
    return call(core_kernel, "add_core", [((128, CHUNK), BF16), ((128, CHUNK), F32)], 1, 2)


def total():
    return call(sum_kernel, "add_up", [((SEQ * PART_ROWS, 128), BF16)], 0, 2)


def finish():
    return call(
        last_kernel,
        "unpack",
        [
            ((64, CHUNK), BF16),
            ((64, CHUNK), BF16),
            ((3 * LOCAL, WIDTH), F32),
            ((LOCAL, WIDTH), F32),
            ((2 * LOCAL, HIDDEN), F32),
            ((2, LOCAL), F32),
        ],
        0,
        3,
        [(SEQ * PART_ROWS, 128)],
    )


def swap(values, group, among=None):
    tiles = values.reshape(values.shape[0] // group, group, 128)
    tiles = lax.all_to_all(
        tiles, "seq", split_axis=0, concat_axis=0, axis_index_groups=among, tiled=True
    )
    return tiles.reshape(values.shape)


def shards(
    inputs,
    clip_len,
    clip_order,
    in_proj,
    out_proj,
    filt_in,
    filt_out,
    decay_rate,
    skip_gain,
    cotangent,
):
    rank = lax.axis_index("seq").astype(jnp.int32).reshape(1)
    place = lax.axis_index("ch").astype(jnp.int32).reshape(1)
    rank, place = lax.optimization_barrier((rank, place))
    halves = [list(range(at * PARTS, at * PARTS + PARTS)) for at in range(SEQ // PARTS)]
    in_rows = in_proj.reshape(3 * LOCAL, WIDTH)
    out_rows = out_proj.T
    full = lax.all_gather(jnp.concatenate([inputs, cotangent], 0), "ch", axis=0, tiled=True)
    send, gate_two, out_grad, hidden, window, notes = front()(
        rank, clip_len.reshape(1, CLIPS), clip_order.reshape(1, CLIPS), skip_gain, full, in_rows,
        out_rows, filt_in, decay_rate,
    )
    received = swap(send, 4)
    analysis, synthesis, forward, backward, twist_cos, twist_sin = [
        jnp.asarray(x) for x in tables()
    ]
    (spectra,) = filtering()(
        rank, filt_in, filt_out.reshape(2 * LOCAL, HIDDEN), decay_rate,
        *[jnp.asarray(x) for x in wave_tables()], analysis, forward, twist_cos, twist_sin,
    )
    back, skips = series()(
        notes, received, spectra, analysis, synthesis, forward, backward, twist_cos, twist_sin
    )
    returned = swap(back, 2, halves)
    weights, gated, scaled_grad = weighing()(
        returned, full, gate_two, out_grad, hidden, window
    )
    given, kept = channels()(place, gated, scaled_grad, in_rows, out_rows)
    over_cores = lax.ppermute(given, "ch", [(0, 1), (1, 0), (2, 3), (3, 2)])
    given, left = core_sum()(place, over_cores, kept)
    (spread,) = total()(swap(weights, 2, halves), skips)
    spread, given = lax.optimization_barrier((spread, given))
    over_chips = lax.ppermute(given, "ch", [(0, 2), (2, 0), (1, 3), (3, 1)])
    mixed, grad_inputs, in_weight, out_weight, filter_grad, grad_skip = finish()(
        swap(spread, 2), over_chips, left
    )
    return (
        mixed,
        grad_inputs,
        in_weight.reshape(3, LOCAL, WIDTH),
        out_weight.T,
        filter_grad.reshape(2, LOCAL, HIDDEN),
        grad_skip,
    )


def solution(mesh):
    return jax.shard_map(
        shards,
        mesh=mesh,
        in_specs=(
            P("ch", "seq"),
            P(),
            P(),
            P(None, "ch", None),
            P(None, "ch"),
            P(),
            P(None, "ch", None),
            P(None, "ch"),
            P(None, "ch"),
            P("ch", "seq"),
        ),
        out_specs=(
            P("ch", "seq"),
            P("ch", "seq"),
            P(None, "ch", None),
            P(None, "ch"),
            P(None, "ch", None),
            P(None, "ch"),
        ),
        check_vma=False,
    )
```

```python
import functools
import math

import jax
import jax.numpy as jnp
import numpy as np
from jax import lax
from jax.experimental import pallas as pl
from jax.experimental.pallas import tpu as pltpu
from jax.sharding import PartitionSpec as P

EPSILON = 1e-05
HIGHEST = lax.Precision.HIGHEST
F32 = jnp.float32
BF16 = jnp.bfloat16

WIDTH = 256
TOTAL = 32768
SEQ = 128
CHUNK = 256
LOCAL = 64
HIDDEN = 64
BANDS = 16
CLIPS = 16
SEND_ROWS = 8
BACK_ROWS = 10
SPARE = 16
PART_ROWS = 10
PARTS = 64


def tables():
    k1 = np.arange(SEQ)[:, None] + 0.25
    s = np.arange(SEQ)[None, :]
    u = np.arange(CHUNK)[None, :]
    first = 2.0 * np.pi * k1 * s / SEQ
    analysis = np.concatenate([np.cos(first), -np.sin(first)], 0).astype(np.float32)
    synthesis = (np.concatenate([np.cos(first), -np.sin(first)], 0).T / TOTAL).astype(np.float32)
    twist = 2.0 * np.pi * k1 * u / TOTAL
    k2 = np.arange(CHUNK)
    second = 2.0 * np.pi * ((k2[:, None] * k2[None, :]) % CHUNK) / CHUNK
    cosines, sines = np.cos(second), np.sin(second)
    forward = np.block([[cosines, -sines], [sines, cosines]]).astype(np.float32)
    return (
        analysis.astype(BF16),
        synthesis.astype(BF16),
        forward.astype(BF16),
        forward.T.astype(BF16),
        np.cos(twist).astype(np.float32),
        np.sin(twist).astype(np.float32),
    )


def wave_tables():
    f = np.arange(1, BANDS + 1)
    count = 2 * BANDS + 2
    chunk = 2.0 * np.pi * (f[None, :] * np.arange(SEQ)[:, None] % SEQ) / SEQ
    sample = 2.0 * np.pi * f[:, None] * np.arange(CHUNK)[None, :] / TOTAL
    cosines, sines = np.cos(chunk), np.sin(chunk)
    ramp = np.arange(SEQ)[:, None] / SEQ
    ones = np.ones((SEQ, 1))
    first = np.concatenate([cosines, cosines, ramp, ones], 1)
    second = np.concatenate([sines, -sines, 0 * ones, 0 * ones], 1)
    inner = np.concatenate(
        [
            np.cos(sample),
            np.sin(sample),
            np.ones((1, CHUNK)),
            np.arange(CHUNK)[None, :] / TOTAL,
        ],
        0,
    ).astype(np.float32)
    high = inner.astype(BF16)
    low = (inner - high.astype(np.float32)).astype(BF16)
    pick_first = np.zeros((1 + 2 * BANDS, count))
    pick_second = np.zeros((1 + 2 * BANDS, count))
    for band in range(BANDS):
        pick_first[1 + band, band] = 1
        pick_first[1 + BANDS + band, BANDS + band] = 1
        pick_second[1 + BANDS + band, band] = 1
        pick_second[1 + band, BANDS + band] = 1
    pick_first[0, 2 * BANDS :] = 1

    def lanes(table):
        wide = np.zeros((table.shape[0], 128), np.float32)
        wide[:, : 3 * count] = np.concatenate([table] * 3, 1)
        return wide

    def rows(table):
        wide = np.zeros((40, 128), np.float32)
        wide[:32] = lanes(table)[:32]
        wide[39] = lanes(table)[32]
        return wide

    factors = np.zeros((128, CHUNK), BF16)
    factors[: 3 * count] = np.concatenate([high, low, high], 0)
    return lanes(first), lanes(second), rows(pick_first), rows(pick_second), factors


def dot(a, b, dims=((1,), (0,)), precision=None):
    return lax.dot_general(a, b, (dims, ((), ())), precision=precision, preferred_element_type=F32)


def split(x):
    high = x.astype(BF16)
    return high, (x - high.astype(F32)).astype(BF16)


def to_column(row, count):
    shape = (count, count)
    rows = lax.broadcasted_iota(jnp.int32, shape, 0)
    columns = lax.broadcasted_iota(jnp.int32, shape, 1)
    spread = jnp.broadcast_to(row, shape)
    return jnp.sum(jnp.where(rows == columns, spread, jnp.zeros_like(spread)), 1, keepdims=True)


def clip_bounds(clip_len, clip_order):
    shape = (CLIPS, CLIPS)
    rows = lax.broadcasted_iota(jnp.int32, shape, 0)
    columns = lax.broadcasted_iota(jnp.int32, shape, 1)
    sizes = to_column(clip_len.astype(F32), CLIPS)
    lengths = jnp.sum(jnp.where(rows == clip_order, sizes, 0.0), 0, keepdims=True)
    starts = jnp.sum(
        jnp.where(rows < columns, to_column(lengths, CLIPS), 0.0), 0, keepdims=True
    )
    return starts, lengths


def front_kernel(
    rank, clip_len, clip_order, skip_gain, full, in_proj, out_proj, filt_in, decay,
    send, gate_out, grad_out, hidden_out, window_out, notes, scratch,
):
    first = ((0,), (0,))
    inputs = jnp.concatenate([full[128 * j : 128 * j + 64, :] for j in range(4)], 0)
    cotangent = jnp.concatenate([full[128 * j + 64 : 128 * j + 128, :] for j in range(4)], 0)
    raw = dot(in_proj[...], inputs)
    out_grad = dot(out_proj[...], cotangent)
    gate_two = raw[2 * LOCAL :, :]
    gate_out[...] = gate_two
    grad_out[...] = out_grad

    offset = rank[0] * CHUNK
    starts, lengths = clip_bounds(clip_len[...], clip_order[...])
    begin = to_column(starts, CLIPS)
    end = begin + to_column(lengths, CLIPS)
    time = (offset + lax.broadcasted_iota(jnp.int32, (CLIPS, CHUNK), 1)).astype(F32)
    member = jnp.where((time >= begin) & (time < end), 1.0, 0.0)
    member = jnp.concatenate([member, jnp.zeros((128 - CLIPS, CHUNK), F32)], 0)
    wide = inputs.astype(F32)
    squares = jnp.sum(wide * wide, 0, keepdims=True)
    power = dot(jnp.broadcast_to(squares, (8, CHUNK)), member, ((1,), (1,)), HIGHEST)[:1, :]
    high, low = split(power)

    step = offset + lax.broadcasted_iota(jnp.int32, (BANDS, CHUNK), 1)
    band = 1 + lax.broadcasted_iota(jnp.int32, (BANDS, CHUNK), 0)
    phases = ((step * band) & (TOTAL - 1)).astype(F32) * (2.0 * math.pi / TOTAL)
    ramp = (offset + lax.broadcasted_iota(jnp.int32, (8, CHUNK), 1)).astype(F32) * (1.0 / TOTAL)
    first_row = lax.broadcasted_iota(jnp.int32, (8, HIDDEN), 0) == 0
    ramp_weight = jnp.where(first_row, filt_in[:8, :], 0.0)
    hidden = jnp.sin(
        dot(ramp_weight, ramp, first, HIGHEST)
        + dot(filt_in[1 : 1 + BANDS, :], jnp.cos(phases), first, HIGHEST)
        + dot(filt_in[1 + BANDS : 1 + 2 * BANDS, :], jnp.sin(phases), first, HIGHEST)
    )
    hidden_out[...] = hidden
    rows = lax.broadcasted_iota(jnp.int32, (LOCAL, LOCAL), 0)
    columns = lax.broadcasted_iota(jnp.int32, (LOCAL, LOCAL), 1)
    for i in range(2):
        spread = jnp.broadcast_to(decay[i : i + 1, :], (LOCAL, LOCAL))
        rate = jnp.sum(jnp.where(rows == columns, spread, 0.0), 1, keepdims=True)
        window = jnp.exp(-rate * ramp[:1, :]) * TOTAL ** (-0.5)
        window_out[i * LOCAL : (i + 1) * LOCAL, :] = window

    channel = lax.broadcasted_iota(jnp.int32, (1, LOCAL), 1) == rank[0] % LOCAL
    skips = jnp.sum(jnp.where(channel, skip_gain[...], 0.0), 1, keepdims=True)
    empty = jnp.zeros((1, 128 - CLIPS), F32)
    backward = jnp.full((1, 128), rank[0] // LOCAL, jnp.int32).astype(F32)
    rows = [
        jnp.concatenate([starts, empty], 1),
        jnp.concatenate([lengths, empty], 1),
        jnp.broadcast_to(skips[:1, :], (1, 128)),
        jnp.broadcast_to(skips[1:, :], (1, 128)),
        backward,
        jnp.zeros((3, 128), F32),
    ]
    notes[...] = jnp.concatenate(rows, 0)

    arrays = [raw[:LOCAL, :], raw[LOCAL : 2 * LOCAL, :], gate_two * out_grad]
    for at, values in enumerate(arrays):
        scratch[pl.ds(2 * at, LOCAL, stride=SEND_ROWS), :] = values[:, :128]
        scratch[pl.ds(2 * at + 1, LOCAL, stride=SEND_ROWS), :] = values[:, 128:]
    for at, values in enumerate([high, low]):
        scratch[pl.ds(6 + at, LOCAL, stride=SEND_ROWS), :] = jnp.broadcast_to(
            values.astype(F32), (LOCAL, 128)
        )
    packed = scratch[: LOCAL * SEND_ROWS, :].astype(BF16)
    send[: LOCAL * SEND_ROWS, :] = packed
    send[LOCAL * SEND_ROWS :, :] = packed


def to_spectrum(signals, cosines, sines, analysis, inner):
    rows = dot(analysis[...], jnp.concatenate(signals, 1).astype(BF16))
    twisted = []
    for at in range(len(signals)):
        real = rows[:128, 256 * at : 256 * at + 256]
        imag = rows[128:, 256 * at : 256 * at + 256]
        parts = [cosines * real + sines * imag, cosines * imag - sines * real]
        twisted.append(jnp.concatenate(parts, 1).astype(BF16))
    spectra = dot(jnp.concatenate(twisted, 0), inner[...])
    pairs = [spectra[128 * at : 128 * at + 128, :] for at in range(len(signals))]
    return [(pair[:, :256], pair[:, 256:]) for pair in pairs]


def to_signal(spectra, cosines, sines, synthesis, inner):
    stacked = [jnp.concatenate(pair, 1).astype(BF16) for pair in spectra]
    rows = dot(jnp.concatenate(stacked, 0), inner[...])
    columns = []
    for at in range(len(spectra)):
        real = rows[128 * at : 128 * at + 128, :256]
        imag = rows[128 * at : 128 * at + 128, 256:]
        parts = [cosines * real - sines * imag, cosines * imag + sines * real]
        columns.append(jnp.concatenate(parts, 0).astype(BF16))
    signals = dot(synthesis, jnp.concatenate(columns, 1))
    return [signals[:, 256 * at : 256 * at + 256] for at in range(len(spectra))]


WAVE = (6.2831826, -41.341423, 81.59618, -76.5801, 41.205395, -12.271262)


def sine(turns):
    rest = turns - jnp.floor(turns + 0.5)
    square = rest * rest
    value = jnp.full_like(rest, WAVE[-1])
    for factor in WAVE[-2::-1]:
        value = value * square + factor
    return value * rest


def filter_kernel(
    rank, filt_in, filt_out, decay, wave_first, wave_second, pick_first, pick_second, factors,
    analysis, forward, twist_cos, twist_sin, spectra, weight_one, weight_two, out_one, out_two,
    shapes,
):
    channel = rank[0] % LOCAL
    first = ((0,), (0,))
    groups = 8 * HIDDEN
    row = lax.broadcasted_iota(jnp.int32, (groups, HIDDEN), 0)
    column = lax.broadcasted_iota(jnp.int32, (groups, HIDDEN), 1)
    repeat = jnp.where(row // 8 == column, 1.0, 0.0)
    for pick, target in [(pick_first, weight_one), (pick_second, weight_two)]:
        weights = dot(filt_in[:32, :], pick[:32, :], first, HIGHEST) + dot(
            filt_in[25:33, :], pick[32:, :], first, HIGHEST
        )
        target[...] = dot(repeat, weights * (0.5 / math.pi), precision=HIGHEST)
    lane = lax.broadcasted_iota(jnp.int32, (1, LOCAL), 1)
    here = lax.broadcasted_iota(jnp.int32, (LOCAL, HIDDEN), 0) == channel
    for i, target in enumerate([out_one, out_two]):
        mine = jnp.where(here, filt_out[i * LOCAL : (i + 1) * LOCAL, :], 0.0)
        spread = jnp.broadcast_to(
            to_column(jnp.sum(mine, 0, keepdims=True), HIDDEN), (HIDDEN, 128)
        )
        target[...] = dot(repeat, spread, precision=HIGHEST)
    rates = jnp.sum(jnp.where(lane == channel, decay[...], 0.0), 1, keepdims=True)
    count = 2 * BANDS + 2
    exact = lax.broadcasted_iota(jnp.int32, (groups, 128), 1) < 2 * count

    def block(at, carry):
        rows = pl.ds(pl.multiple_of(at * 8, 8), 8)

        def repeated(values):
            return jnp.broadcast_to(values[None], (HIDDEN, 8, 128)).reshape(groups, 128)

        sums = repeated(wave_first[rows, :]) * weight_one[...]
        sums = sums + repeated(wave_second[rows, :]) * weight_two[...]
        high = sums.astype(BF16).astype(F32)
        hidden = sine(dot(jnp.where(exact, high, sums - high).astype(BF16), factors[...]))
        for i, target in enumerate([out_one, out_two]):
            factor = target[...]
            product = hidden * jnp.concatenate([factor, factor], 1)
            shapes[i, rows, :] = jnp.sum(product.reshape(HIDDEN, 8, CHUNK), 0)
        return carry

    lax.fori_loop(0, SEQ // 8, block, 0, unroll=2)
    time = lax.broadcasted_iota(jnp.int32, (SEQ, CHUNK), 0) * CHUNK + lax.broadcasted_iota(
        jnp.int32, (SEQ, CHUNK), 1
    )
    ramp = time.astype(F32) * (1.0 / TOTAL)
    windows = [jnp.exp(-rates[i : i + 1, :] * ramp) * TOTAL ** (-0.5) for i in range(2)]
    both = to_spectrum(
        [shapes[i] * windows[i] for i in range(2)], twist_cos[...], twist_sin[...], analysis, forward
    )
    for i, (real, imag) in enumerate(both):
        spectra[128 * i : 128 * i + 128, :256] = real
        spectra[128 * i : 128 * i + 128, 256:] = imag


def series_kernel(
    notes, received, filters, analysis, synthesis, forward, backward, twist_cos, twist_sin,
    back, skips, scratch, packed,
):
    starts = notes[:1, :]
    counts = jnp.maximum(notes[1:2, :], 1.0)
    skip_one = notes[2:3, :1]
    skip_two = notes[3:4, :1]
    role = notes[4:5, :1]
    scratch[: received.shape[0], :] = received[...].astype(F32)

    def plane(row):
        return scratch[pl.ds(row, SEQ, stride=SEND_ROWS), :]

    def signal(at):
        return jnp.concatenate([plane(2 * at), plane(2 * at + 1)], 1)

    power = jnp.sum(plane(6) + plane(7), 0, keepdims=True)
    time = lax.broadcasted_iota(jnp.int32, (SEQ, CHUNK), 0) * CHUNK + lax.broadcasted_iota(
        jnp.int32, (SEQ, CHUNK), 1
    )
    time = time.astype(F32)
    lane = lax.broadcasted_iota(jnp.int32, (1, 128), 1)
    inverse_rms = lax.rsqrt(power / (WIDTH * counts) + EPSILON)
    scale = jnp.zeros((SEQ, CHUNK), F32)
    for p in range(CLIPS):
        scale = jnp.where(time >= starts[:, p : p + 1], inverse_rms[:, p : p + 1], scale)

    cosines = twist_cos[...]
    sines = twist_sin[...]

    def analyse(signals):
        return to_spectrum(signals, cosines, sines, analysis, forward)

    def synthesise(parts, table):
        return to_signal(parts, cosines, sines, table, backward)

    def times(a, b, sign):
        return (a[0] * b[0] - sign * (a[1] * b[1]), a[1] * b[0] + sign * (a[0] * b[1]))

    def half(values):
        lower = values[:PARTS, :]
        upper = values[PARTS:, :]
        return jnp.where(jnp.broadcast_to(role, lower.shape) == 0.0, lower, upper)

    value = signal(0) * scale
    gate_one = signal(1) * scale
    scaled_two = signal(2) * scale
    value_spec, second_spec = analyse([value, scaled_two])
    filter_one, filter_two = [
        (filters[128 * i : 128 * i + 128, :256], filters[128 * i : 128 * i + 128, 256:])
        for i in range(2)
    ]
    carry_one, level_grad = synthesise(
        [times(value_spec, filter_one, 1.0), times(second_spec, filter_two, -1.0)],
        synthesis[...],
    )
    carry_one = carry_one + skip_one * value
    level_grad = level_grad + skip_two * scaled_two
    level_one = gate_one * carry_one
    scaled_one = gate_one * level_grad
    level_spec, first_spec = analyse([level_one, scaled_one])
    carry_two, shape_two, value_grad, shape_one = synthesise(
        [
            times(level_spec, filter_two, 1.0),
            times(second_spec, level_spec, -1.0),
            times(first_spec, filter_one, -1.0),
            times(first_spec, value_spec, -1.0),
        ],
        half(synthesis[...].astype(F32)).astype(BF16),
    )
    scale_half = half(scale)
    carry_two = scale_half * (carry_two + skip_two * half(level_one))
    value_grad = scale_half * (value_grad + skip_one * half(scaled_one))
    gate_grad = scale_half * half(level_grad * carry_one)

    def total(values):
        return jnp.sum(jnp.sum(values, 0, keepdims=True), 1, keepdims=True)

    skip_row = jnp.zeros((1, 128), F32)
    for at, skip_grad in enumerate([total(scaled_one * value), total(scaled_two * level_one)]):
        high, low = split(skip_grad)
        mid = low.astype(F32)
        low = skip_grad - high.astype(F32) - mid
        for to, part in enumerate([high.astype(F32), mid, low]):
            skip_row = jnp.where(lane == 3 * at + to, part, skip_row)
    for at, values in enumerate([carry_two, shape_two, value_grad, shape_one, gate_grad]):
        packed[pl.ds(2 * at, PARTS, stride=BACK_ROWS), :] = values[:, :128]
        packed[pl.ds(2 * at + 1, PARTS, stride=BACK_ROWS), :] = values[:, 128:]
    skips[...] = jnp.broadcast_to(skip_row, (8, 128))
    back[...] = packed[: back.shape[0], :].astype(BF16)


def returned_signal(scratch, at):
    rows = [scratch[pl.ds(2 * at + half, LOCAL, stride=BACK_ROWS), :] for half in range(2)]
    return jnp.concatenate(rows, 1)


def weight_kernel(
    received, full, gate_in, grad_in, hidden, window, weights, gated_out, scaled_out,
    scratch, packed,
):
    scratch[: received.shape[0], :] = received[...].astype(F32)
    carry = returned_signal(scratch, 0)
    gated = (gate_in[...] * carry).astype(BF16)
    scaled_grad = jnp.concatenate(
        [
            returned_signal(scratch, 2).astype(BF16),
            returned_signal(scratch, 4).astype(BF16),
            (grad_in[...] * carry).astype(BF16),
        ],
        0,
    )
    gated_out[...] = gated
    scaled_out[...] = scaled_grad
    inputs = jnp.concatenate([full[128 * j : 128 * j + 64, :] for j in range(4)], 0)
    cotangent = jnp.concatenate([full[128 * j + 64 : 128 * j + 128, :] for j in range(4)], 0)
    last = ((1,), (1,))
    in_weight = dot(scaled_grad, inputs, last)
    out_weight = dot(gated, cotangent, last)
    blank = jnp.zeros((LOCAL, CHUNK), F32)
    shape_one = returned_signal(scratch, 3) * window[:LOCAL, :]
    shape_two = returned_signal(scratch, 1) * window[LOCAL:, :]
    filter_grad = dot(
        shape_one, jnp.concatenate([hidden[...], blank], 0), last, HIGHEST
    ) + dot(shape_two, jnp.concatenate([blank, hidden[...]], 0), last, HIGHEST)
    rows = [
        in_weight[64 * at : 64 * at + 64, 128 * half : 128 * half + 128]
        for at in range(3)
        for half in range(2)
    ]
    rows += [out_weight[:, :128], out_weight[:, 128:], filter_grad, jnp.zeros((PARTS, 128), F32)]
    for at, values in enumerate(rows):
        packed[pl.ds(at, PARTS, stride=PART_ROWS), :] = values
    weights[...] = packed[: weights.shape[0], :].astype(BF16)


def channel_kernel(place, gated, scaled_grad, in_proj, out_proj, given, kept):
    first = ((0,), (0,))
    mixed = dot(out_proj[...], gated[...], first)
    grad_inputs = dot(in_proj[...], scaled_grad[...], first)
    even = place[0] % 2 == 0
    for at in range(2):
        for to, values in enumerate([mixed, grad_inputs]):
            low = values[128 * at : 128 * at + 64, :]
            high = values[128 * at + 64 : 128 * at + 128, :]
            rows = slice(128 * at + 64 * to, 128 * at + 64 * to + 64)
            given[rows, :] = jnp.where(even, high, low).astype(BF16)
            kept[rows, :] = jnp.where(even, low, high)


def core_kernel(place, received, kept, given, left):
    total = kept[...] + received[...].astype(F32)
    near = place[0] < 2
    given[...] = jnp.where(near, total[128:, :], total[:128, :]).astype(BF16)
    left[...] = jnp.where(near, total[:128, :], total[128:, :])


def sum_kernel(received, skips, spread):
    four = 4 * PART_ROWS
    parts = jnp.sum(received[...].astype(F32).reshape(PARTS // 4, four, 128), 0)
    total = sum(parts[PART_ROWS * at : PART_ROWS * at + PART_ROWS, :] for at in range(4))
    row = lax.broadcasted_iota(jnp.int32, (PART_ROWS, 128), 0)
    total = jnp.where(row == PART_ROWS - 1, skips[:1, :], total * TOTAL ** (-0.5))
    total = jnp.concatenate([total] * 4, 0)
    total = jnp.broadcast_to(total[None], (SEQ // 4, four, 128)).reshape(SEQ * PART_ROWS, 128)
    spread[...] = total.astype(BF16)


def last_kernel(
    received, over_chips, left, mixed, grad_inputs, in_weight, out_weight, filter_grad, skip_grad,
    scratch,
):
    summed = (left[...] + over_chips[...].astype(F32)).astype(BF16)
    mixed[...] = summed[:64, :]
    grad_inputs[...] = summed[64:, :]
    scratch[: received.shape[0], :] = received[...].astype(F32)

    def block(at):
        first = scratch[pl.ds(at, PARTS, stride=PART_ROWS), :]
        return first + scratch[pl.ds(PARTS * PART_ROWS + at, PARTS, stride=PART_ROWS), :]

    for half in range(2):
        for at in range(3):
            in_weight[64 * at : 64 * at + 64, 128 * half : 128 * half + 128] = block(2 * at + half)
        out_weight[:, 128 * half : 128 * half + 128] = block(6 + half)
    filters = block(8)
    filter_grad[:LOCAL, :] = filters[:, :HIDDEN]
    filter_grad[LOCAL:, :] = filters[:, HIDDEN:]
    lane = lax.broadcasted_iota(jnp.int32, (8, 128), 1)
    order = lax.broadcasted_iota(jnp.int32, (8, 128), 0)
    pick = jnp.where((lane >= 3 * order) & (lane < 3 * order + 3), 1.0, 0.0).astype(BF16)
    skips = scratch[pl.ds(PART_ROWS - 1, PARTS, stride=PART_ROWS), :].astype(BF16)
    skip_grad[...] = dot(pick, skips, ((1,), (1,)))[:2, :] * TOTAL ** (-0.5)


def call(kernel, name, outs, scalars, arrays, scratch=(), spare=SPARE):
    def vmem():
        return pl.BlockSpec(memory_space=pltpu.VMEM)

    return pl.pallas_call(
        kernel,
        name=name,
        out_shape=[jax.ShapeDtypeStruct(shape, kind) for shape, kind in outs],
        in_specs=[pl.BlockSpec(memory_space=pltpu.SMEM)] * scalars + [vmem() for _ in range(arrays)],
        out_specs=[vmem() for _ in outs],
        scratch_shapes=[
            pltpu.VMEM((*shape[:-2], shape[-2] + spare, shape[-1]), F32) for shape in scratch
        ],
        compiler_params=pltpu.CompilerParams(vmem_limit_bytes=32 * 1024 * 1024),
    )


def front():
    return call(
        front_kernel,
        "project",
        [
            ((SEQ * SEND_ROWS, 128), BF16),
            ((LOCAL, CHUNK), F32),
            ((LOCAL, CHUNK), F32),
            ((HIDDEN, CHUNK), F32),
            ((2 * LOCAL, CHUNK), F32),
            ((8, 128), F32),
        ],
        1,
        8,
        [(LOCAL * SEND_ROWS, 128)],
    )


def filtering():
    return call(
        filter_kernel,
        "filters",
        [((2 * SEQ, 2 * CHUNK), F32)],
        1,
        12,
        [(8 * HIDDEN, 128)] * 4 + [(2, SEQ, CHUNK)],
        spare=0,
    )


def series():
    return call(
        series_kernel,
        "convolve",
        [((PARTS * BACK_ROWS, 128), BF16), ((8, 128), F32)],
        0,
        9,
        [(SEQ * SEND_ROWS, 128), (PARTS * BACK_ROWS, 128)],
    )


def weighing():
    return call(
        weight_kernel,
        "weigh",
        [
            ((PARTS * PART_ROWS, 128), BF16),
            ((LOCAL, CHUNK), BF16),
            ((3 * LOCAL, CHUNK), BF16),
        ],
        0,
        6,
        [(PARTS * BACK_ROWS, 128), (PARTS * PART_ROWS, 128)],
    )


def channels():
    return call(channel_kernel, "mix", [((256, CHUNK), BF16), ((256, CHUNK), F32)], 1, 4)


def core_sum():
    return call(core_kernel, "add_core", [((128, CHUNK), BF16), ((128, CHUNK), F32)], 1, 2)


def total():
    return call(sum_kernel, "add_up", [((SEQ * PART_ROWS, 128), BF16)], 0, 2)


def finish():
    return call(
        last_kernel,
        "unpack",
        [
            ((64, CHUNK), BF16),
            ((64, CHUNK), BF16),
            ((3 * LOCAL, WIDTH), F32),
            ((LOCAL, WIDTH), F32),
            ((2 * LOCAL, HIDDEN), F32),
            ((2, LOCAL), F32),
        ],
        0,
        3,
        [(SEQ * PART_ROWS, 128)],
    )


def swap(values, group, among=None):
    tiles = values.reshape(values.shape[0] // group, group, 128)
    tiles = lax.all_to_all(
        tiles, "seq", split_axis=0, concat_axis=0, axis_index_groups=among, tiled=True
    )
    return tiles.reshape(values.shape)


def shards(
    inputs,
    clip_len,
    clip_order,
    in_proj,
    out_proj,
    filt_in,
    filt_out,
    decay_rate,
    skip_gain,
    cotangent,
):
    rank = lax.axis_index("seq").astype(jnp.int32).reshape(1)
    place = lax.axis_index("ch").astype(jnp.int32).reshape(1)
    rank, place = lax.optimization_barrier((rank, place))
    halves = [list(range(at * PARTS, at * PARTS + PARTS)) for at in range(SEQ // PARTS)]
    in_rows = in_proj.reshape(3 * LOCAL, WIDTH)
    out_rows = out_proj.T
    full = lax.all_gather(jnp.concatenate([inputs, cotangent], 0), "ch", axis=0, tiled=True)
    send, gate_two, out_grad, hidden, window, notes = front()(
        rank, clip_len.reshape(1, CLIPS), clip_order.reshape(1, CLIPS), skip_gain, full, in_rows,
        out_rows, filt_in, decay_rate,
    )
    received = swap(send, 4)
    analysis, synthesis, forward, backward, twist_cos, twist_sin = [
        jnp.asarray(x) for x in tables()
    ]
    (spectra,) = filtering()(
        rank, filt_in, filt_out.reshape(2 * LOCAL, HIDDEN), decay_rate,
        *[jnp.asarray(x) for x in wave_tables()], analysis, forward, twist_cos, twist_sin,
    )
    back, skips = series()(
        notes, received, spectra, analysis, synthesis, forward, backward, twist_cos, twist_sin
    )
    returned = swap(back, 2, halves)
    weights, gated, scaled_grad = weighing()(
        returned, full, gate_two, out_grad, hidden, window
    )
    given, kept = channels()(place, gated, scaled_grad, in_rows, out_rows)
    over_cores = lax.ppermute(given, "ch", [(0, 1), (1, 0), (2, 3), (3, 2)])
    given, left = core_sum()(place, over_cores, kept)
    (spread,) = total()(swap(weights, 2, halves), skips)
    spread, given = lax.optimization_barrier((spread, given))
    over_chips = lax.ppermute(given, "ch", [(0, 2), (2, 0), (1, 3), (3, 1)])
    mixed, grad_inputs, in_weight, out_weight, filter_grad, grad_skip = finish()(
        swap(spread, 2), over_chips, left
    )
    return (
        mixed,
        grad_inputs,
        in_weight.reshape(3, LOCAL, WIDTH),
        out_weight.T,
        filter_grad.reshape(2, LOCAL, HIDDEN),
        grad_skip,
    )


def solution(mesh):
    return jax.shard_map(
        shards,
        mesh=mesh,
        in_specs=(
            P("ch", "seq"),
            P(),
            P(),
            P(None, "ch", None),
            P(None, "ch"),
            P(),
            P(None, "ch", None),
            P(None, "ch"),
            P(None, "ch"),
            P("ch", "seq"),
        ),
        out_specs=(
            P("ch", "seq"),
            P("ch", "seq"),
            P(None, "ch", None),
            P(None, "ch"),
            P(None, "ch", None),
            P(None, "ch"),
        ),
        check_vma=False,
    )
```

```python
import functools
import math

import jax
import jax.numpy as jnp
import numpy as np
from jax import lax
from jax.experimental import pallas as pl
from jax.experimental.pallas import tpu as pltpu
from jax.sharding import PartitionSpec as P

EPSILON = 1e-05
HIGHEST = lax.Precision.HIGHEST
F32 = jnp.float32
BF16 = jnp.bfloat16

WIDTH = 256
TOTAL = 32768
SEQ = 128
CHUNK = 256
LOCAL = 64
HIDDEN = 64
BANDS = 16
CLIPS = 16
SEND_ROWS = 8
BACK_ROWS = 10
SPARE = 16
PART_ROWS = 10
PARTS = 64


def tables():
    k1 = np.arange(SEQ)[:, None] + 0.25
    s = np.arange(SEQ)[None, :]
    u = np.arange(CHUNK)[None, :]
    first = 2.0 * np.pi * k1 * s / SEQ
    analysis = np.concatenate([np.cos(first), -np.sin(first)], 0).astype(np.float32)
    synthesis = (np.concatenate([np.cos(first), -np.sin(first)], 0).T / TOTAL).astype(np.float32)
    twist = 2.0 * np.pi * k1 * u / TOTAL
    k2 = np.arange(CHUNK)
    second = 2.0 * np.pi * ((k2[:, None] * k2[None, :]) % CHUNK) / CHUNK
    cosines, sines = np.cos(second), np.sin(second)
    forward = np.block([[cosines, -sines], [sines, cosines]]).astype(np.float32)
    return (
        analysis.astype(BF16),
        synthesis.astype(BF16),
        forward.astype(BF16),
        forward.T.astype(BF16),
        np.cos(twist).astype(np.float32),
        np.sin(twist).astype(np.float32),
    )


def wave_tables():
    f = np.arange(1, BANDS + 1)
    count = 2 * BANDS + 2
    chunk = 2.0 * np.pi * (f[None, :] * np.arange(SEQ)[:, None] % SEQ) / SEQ
    sample = 2.0 * np.pi * f[:, None] * np.arange(CHUNK)[None, :] / TOTAL
    cosines, sines = np.cos(chunk), np.sin(chunk)
    ramp = np.arange(SEQ)[:, None] / SEQ
    ones = np.ones((SEQ, 1))
    first = np.concatenate([cosines, cosines, ramp, ones], 1)
    second = np.concatenate([sines, -sines, 0 * ones, 0 * ones], 1)
    inner = np.concatenate(
        [
            np.cos(sample),
            np.sin(sample),
            np.ones((1, CHUNK)),
            np.arange(CHUNK)[None, :] / TOTAL,
        ],
        0,
    ).astype(np.float32)
    high = inner.astype(BF16)
    low = (inner - high.astype(np.float32)).astype(BF16)
    pick_first = np.zeros((1 + 2 * BANDS, count))
    pick_second = np.zeros((1 + 2 * BANDS, count))
    for band in range(BANDS):
        pick_first[1 + band, band] = 1
        pick_first[1 + BANDS + band, BANDS + band] = 1
        pick_second[1 + BANDS + band, band] = 1
        pick_second[1 + band, BANDS + band] = 1
    pick_first[0, 2 * BANDS :] = 1

    def lanes(table):
        wide = np.zeros((table.shape[0], 128), np.float32)
        wide[:, : 3 * count] = np.concatenate([table] * 3, 1)
        return wide

    def rows(table):
        wide = np.zeros((40, 128), np.float32)
        wide[:32] = lanes(table)[:32]
        wide[39] = lanes(table)[32]
        return wide

    factors = np.zeros((128, CHUNK), BF16)
    factors[: 3 * count] = np.concatenate([high, low, high], 0)
    return lanes(first), lanes(second), rows(pick_first), rows(pick_second), factors


def dot(a, b, dims=((1,), (0,)), precision=None):
    return lax.dot_general(a, b, (dims, ((), ())), precision=precision, preferred_element_type=F32)


def split(x):
    high = x.astype(BF16)
    return high, (x - high.astype(F32)).astype(BF16)


def to_column(row, count):
    shape = (count, count)
    rows = lax.broadcasted_iota(jnp.int32, shape, 0)
    columns = lax.broadcasted_iota(jnp.int32, shape, 1)
    spread = jnp.broadcast_to(row, shape)
    return jnp.sum(jnp.where(rows == columns, spread, jnp.zeros_like(spread)), 1, keepdims=True)


def clip_bounds(clip_len, clip_order):
    shape = (CLIPS, CLIPS)
    rows = lax.broadcasted_iota(jnp.int32, shape, 0)
    columns = lax.broadcasted_iota(jnp.int32, shape, 1)
    sizes = to_column(clip_len.astype(F32), CLIPS)
    lengths = jnp.sum(jnp.where(rows == clip_order, sizes, 0.0), 0, keepdims=True)
    starts = jnp.sum(
        jnp.where(rows < columns, to_column(lengths, CLIPS), 0.0), 0, keepdims=True
    )
    return starts, lengths


def front_kernel(
    rank, clip_len, clip_order, skip_gain, full, in_proj, out_proj, filt_in, decay,
    send, gate_out, grad_out, hidden_out, window_out, notes, scratch,
):
    first = ((0,), (0,))
    inputs = jnp.concatenate([full[128 * j : 128 * j + 64, :] for j in range(4)], 0)
    cotangent = jnp.concatenate([full[128 * j + 64 : 128 * j + 128, :] for j in range(4)], 0)
    raw = dot(in_proj[...], inputs)
    out_grad = dot(out_proj[...], cotangent)
    gate_two = raw[2 * LOCAL :, :]
    gate_out[...] = gate_two
    grad_out[...] = out_grad

    offset = rank[0] * CHUNK
    starts, lengths = clip_bounds(clip_len[...], clip_order[...])
    begin = to_column(starts, CLIPS)
    end = begin + to_column(lengths, CLIPS)
    time = (offset + lax.broadcasted_iota(jnp.int32, (CLIPS, CHUNK), 1)).astype(F32)
    member = jnp.where((time >= begin) & (time < end), 1.0, 0.0)
    member = jnp.concatenate([member, jnp.zeros((128 - CLIPS, CHUNK), F32)], 0)
    wide = inputs.astype(F32)
    squares = jnp.sum(wide * wide, 0, keepdims=True)
    power = dot(jnp.broadcast_to(squares, (8, CHUNK)), member, ((1,), (1,)), HIGHEST)[:1, :]
    high, low = split(power)

    step = offset + lax.broadcasted_iota(jnp.int32, (BANDS, CHUNK), 1)
    band = 1 + lax.broadcasted_iota(jnp.int32, (BANDS, CHUNK), 0)
    phases = ((step * band) & (TOTAL - 1)).astype(F32) * (2.0 * math.pi / TOTAL)
    ramp = (offset + lax.broadcasted_iota(jnp.int32, (8, CHUNK), 1)).astype(F32) * (1.0 / TOTAL)
    first_row = lax.broadcasted_iota(jnp.int32, (8, HIDDEN), 0) == 0
    ramp_weight = jnp.where(first_row, filt_in[:8, :], 0.0)
    hidden = jnp.sin(
        dot(ramp_weight, ramp, first, HIGHEST)
        + dot(filt_in[1 : 1 + BANDS, :], jnp.cos(phases), first, HIGHEST)
        + dot(filt_in[1 + BANDS : 1 + 2 * BANDS, :], jnp.sin(phases), first, HIGHEST)
    )
    hidden_out[...] = hidden
    rows = lax.broadcasted_iota(jnp.int32, (LOCAL, LOCAL), 0)
    columns = lax.broadcasted_iota(jnp.int32, (LOCAL, LOCAL), 1)
    for i in range(2):
        spread = jnp.broadcast_to(decay[i : i + 1, :], (LOCAL, LOCAL))
        rate = jnp.sum(jnp.where(rows == columns, spread, 0.0), 1, keepdims=True)
        window = jnp.exp(-rate * ramp[:1, :]) * TOTAL ** (-0.5)
        window_out[i * LOCAL : (i + 1) * LOCAL, :] = window

    channel = lax.broadcasted_iota(jnp.int32, (1, LOCAL), 1) == rank[0] % LOCAL
    skips = jnp.sum(jnp.where(channel, skip_gain[...], 0.0), 1, keepdims=True)
    empty = jnp.zeros((1, 128 - CLIPS), F32)
    backward = jnp.full((1, 128), rank[0] // LOCAL, jnp.int32).astype(F32)
    rows = [
        jnp.concatenate([starts, empty], 1),
        jnp.concatenate([lengths, empty], 1),
        jnp.broadcast_to(skips[:1, :], (1, 128)),
        jnp.broadcast_to(skips[1:, :], (1, 128)),
        backward,
        jnp.zeros((3, 128), F32),
    ]
    notes[...] = jnp.concatenate(rows, 0)

    arrays = [raw[:LOCAL, :], raw[LOCAL : 2 * LOCAL, :], gate_two * out_grad]
    for at, values in enumerate(arrays):
        scratch[pl.ds(2 * at, LOCAL, stride=SEND_ROWS), :] = values[:, :128]
        scratch[pl.ds(2 * at + 1, LOCAL, stride=SEND_ROWS), :] = values[:, 128:]
    for at, values in enumerate([high, low]):
        scratch[pl.ds(6 + at, LOCAL, stride=SEND_ROWS), :] = jnp.broadcast_to(
            values.astype(F32), (LOCAL, 128)
        )
    packed = scratch[: LOCAL * SEND_ROWS, :].astype(BF16)
    send[: LOCAL * SEND_ROWS, :] = packed
    send[LOCAL * SEND_ROWS :, :] = packed


def to_spectrum(signals, cosines, sines, analysis, inner):
    rows = dot(analysis[...], jnp.concatenate(signals, 1).astype(BF16))
    twisted = []
    for at in range(len(signals)):
        real = rows[:128, 256 * at : 256 * at + 256]
        imag = rows[128:, 256 * at : 256 * at + 256]
        parts = [cosines * real + sines * imag, cosines * imag - sines * real]
        twisted.append(jnp.concatenate(parts, 1).astype(BF16))
    spectra = dot(jnp.concatenate(twisted, 0), inner[...])
    pairs = [spectra[128 * at : 128 * at + 128, :] for at in range(len(signals))]
    return [(pair[:, :256], pair[:, 256:]) for pair in pairs]


def to_signal(spectra, cosines, sines, synthesis, inner):
    stacked = [jnp.concatenate(pair, 1).astype(BF16) for pair in spectra]
    rows = dot(jnp.concatenate(stacked, 0), inner[...])
    columns = []
    for at in range(len(spectra)):
        real = rows[128 * at : 128 * at + 128, :256]
        imag = rows[128 * at : 128 * at + 128, 256:]
        parts = [cosines * real - sines * imag, cosines * imag + sines * real]
        columns.append(jnp.concatenate(parts, 0).astype(BF16))
    signals = dot(synthesis, jnp.concatenate(columns, 1))
    return [signals[:, 256 * at : 256 * at + 256] for at in range(len(spectra))]


WAVE = (6.2831826, -41.341423, 81.59618, -76.5801, 41.205395, -12.271262)


def sine(turns):
    rest = turns - jnp.floor(turns + 0.5)
    square = rest * rest
    value = jnp.full_like(rest, WAVE[-1])
    for factor in WAVE[-2::-1]:
        value = value * square + factor
    return value * rest


def filter_kernel(
    rank, filt_in, filt_out, decay, wave_first, wave_second, pick_first, pick_second, factors,
    analysis, forward, twist_cos, twist_sin, spectra, weight_one, weight_two, out_one, out_two,
    shapes,
):
    channel = rank[0] % LOCAL
    first = ((0,), (0,))
    groups = 8 * HIDDEN
    row = lax.broadcasted_iota(jnp.int32, (groups, HIDDEN), 0)
    column = lax.broadcasted_iota(jnp.int32, (groups, HIDDEN), 1)
    repeat = jnp.where(row // 8 == column, 1.0, 0.0)
    for pick, target in [(pick_first, weight_one), (pick_second, weight_two)]:
        weights = dot(filt_in[:32, :], pick[:32, :], first, HIGHEST) + dot(
            filt_in[25:33, :], pick[32:, :], first, HIGHEST
        )
        target[...] = dot(repeat, weights * (0.5 / math.pi), precision=HIGHEST)
    lane = lax.broadcasted_iota(jnp.int32, (1, LOCAL), 1)
    here = lax.broadcasted_iota(jnp.int32, (LOCAL, HIDDEN), 0) == channel
    for i, target in enumerate([out_one, out_two]):
        mine = jnp.where(here, filt_out[i * LOCAL : (i + 1) * LOCAL, :], 0.0)
        spread = jnp.broadcast_to(
            to_column(jnp.sum(mine, 0, keepdims=True), HIDDEN), (HIDDEN, 128)
        )
        target[...] = dot(repeat, spread, precision=HIGHEST)
    rates = jnp.sum(jnp.where(lane == channel, decay[...], 0.0), 1, keepdims=True)
    count = 2 * BANDS + 2
    exact = lax.broadcasted_iota(jnp.int32, (groups, 128), 1) < 2 * count

    def block(at, carry):
        rows = pl.ds(pl.multiple_of(at * 8, 8), 8)

        def repeated(values):
            return jnp.broadcast_to(values[None], (HIDDEN, 8, 128)).reshape(groups, 128)

        sums = repeated(wave_first[rows, :]) * weight_one[...]
        sums = sums + repeated(wave_second[rows, :]) * weight_two[...]
        high = sums.astype(BF16).astype(F32)
        hidden = sine(dot(jnp.where(exact, high, sums - high).astype(BF16), factors[...]))
        for i, target in enumerate([out_one, out_two]):
            factor = target[...]
            product = hidden * jnp.concatenate([factor, factor], 1)
            shapes[i, rows, :] = jnp.sum(product.reshape(HIDDEN, 8, CHUNK), 0)
        return carry

    lax.fori_loop(0, SEQ // 8, block, 0, unroll=4)
    time = lax.broadcasted_iota(jnp.int32, (SEQ, CHUNK), 0) * CHUNK + lax.broadcasted_iota(
        jnp.int32, (SEQ, CHUNK), 1
    )
    ramp = time.astype(F32) * (1.0 / TOTAL)
    windows = [jnp.exp(-rates[i : i + 1, :] * ramp) * TOTAL ** (-0.5) for i in range(2)]
    both = to_spectrum(
        [shapes[i] * windows[i] for i in range(2)], twist_cos[...], twist_sin[...], analysis, forward
    )
    for i, (real, imag) in enumerate(both):
        spectra[128 * i : 128 * i + 128, :256] = real
        spectra[128 * i : 128 * i + 128, 256:] = imag


def series_kernel(
    notes, received, filters, analysis, synthesis, forward, backward, twist_cos, twist_sin,
    back, skips, scratch, packed,
):
    starts = notes[:1, :]
    counts = jnp.maximum(notes[1:2, :], 1.0)
    skip_one = notes[2:3, :1]
    skip_two = notes[3:4, :1]
    role = notes[4:5, :1]
    scratch[: received.shape[0], :] = received[...].astype(F32)

    def plane(row):
        return scratch[pl.ds(row, SEQ, stride=SEND_ROWS), :]

    def signal(at):
        return jnp.concatenate([plane(2 * at), plane(2 * at + 1)], 1)

    power = jnp.sum(plane(6) + plane(7), 0, keepdims=True)
    time = lax.broadcasted_iota(jnp.int32, (SEQ, CHUNK), 0) * CHUNK + lax.broadcasted_iota(
        jnp.int32, (SEQ, CHUNK), 1
    )
    time = time.astype(F32)
    lane = lax.broadcasted_iota(jnp.int32, (1, 128), 1)
    inverse_rms = lax.rsqrt(power / (WIDTH * counts) + EPSILON)
    scale = jnp.zeros((SEQ, CHUNK), F32)
    for p in range(CLIPS):
        scale = jnp.where(time >= starts[:, p : p + 1], inverse_rms[:, p : p + 1], scale)

    cosines = twist_cos[...]
    sines = twist_sin[...]

    def analyse(signals):
        return to_spectrum(signals, cosines, sines, analysis, forward)

    def synthesise(parts, table):
        return to_signal(parts, cosines, sines, table, backward)

    def times(a, b, sign):
        return (a[0] * b[0] - sign * (a[1] * b[1]), a[1] * b[0] + sign * (a[0] * b[1]))

    def half(values):
        lower = values[:PARTS, :]
        upper = values[PARTS:, :]
        return jnp.where(jnp.broadcast_to(role, lower.shape) == 0.0, lower, upper)

    value = signal(0) * scale
    gate_one = signal(1) * scale
    scaled_two = signal(2) * scale
    value_spec, second_spec = analyse([value, scaled_two])
    filter_one, filter_two = [
        (filters[128 * i : 128 * i + 128, :256], filters[128 * i : 128 * i + 128, 256:])
        for i in range(2)
    ]
    carry_one, level_grad = synthesise(
        [times(value_spec, filter_one, 1.0), times(second_spec, filter_two, -1.0)],
        synthesis[...],
    )
    carry_one = carry_one + skip_one * value
    level_grad = level_grad + skip_two * scaled_two
    level_one = gate_one * carry_one
    scaled_one = gate_one * level_grad
    level_spec, first_spec = analyse([level_one, scaled_one])
    carry_two, shape_two, value_grad, shape_one = synthesise(
        [
            times(level_spec, filter_two, 1.0),
            times(second_spec, level_spec, -1.0),
            times(first_spec, filter_one, -1.0),
            times(first_spec, value_spec, -1.0),
        ],
        half(synthesis[...].astype(F32)).astype(BF16),
    )
    scale_half = half(scale)
    carry_two = scale_half * (carry_two + skip_two * half(level_one))
    value_grad = scale_half * (value_grad + skip_one * half(scaled_one))
    gate_grad = scale_half * half(level_grad * carry_one)

    def total(values):
        return jnp.sum(jnp.sum(values, 0, keepdims=True), 1, keepdims=True)

    skip_row = jnp.zeros((1, 128), F32)
    for at, skip_grad in enumerate([total(scaled_one * value), total(scaled_two * level_one)]):
        high, low = split(skip_grad)
        mid = low.astype(F32)
        low = skip_grad - high.astype(F32) - mid
        for to, part in enumerate([high.astype(F32), mid, low]):
            skip_row = jnp.where(lane == 3 * at + to, part, skip_row)
    for at, values in enumerate([carry_two, shape_two, value_grad, shape_one, gate_grad]):
        packed[pl.ds(2 * at, PARTS, stride=BACK_ROWS), :] = values[:, :128]
        packed[pl.ds(2 * at + 1, PARTS, stride=BACK_ROWS), :] = values[:, 128:]
    skips[...] = jnp.broadcast_to(skip_row, (8, 128))
    back[...] = packed[: back.shape[0], :].astype(BF16)


def returned_signal(scratch, at):
    rows = [scratch[pl.ds(2 * at + half, LOCAL, stride=BACK_ROWS), :] for half in range(2)]
    return jnp.concatenate(rows, 1)


def weight_kernel(
    received, full, gate_in, grad_in, hidden, window, weights, gated_out, scaled_out,
    scratch, packed,
):
    scratch[: received.shape[0], :] = received[...].astype(F32)
    carry = returned_signal(scratch, 0)
    gated = (gate_in[...] * carry).astype(BF16)
    scaled_grad = jnp.concatenate(
        [
            returned_signal(scratch, 2).astype(BF16),
            returned_signal(scratch, 4).astype(BF16),
            (grad_in[...] * carry).astype(BF16),
        ],
        0,
    )
    gated_out[...] = gated
    scaled_out[...] = scaled_grad
    inputs = jnp.concatenate([full[128 * j : 128 * j + 64, :] for j in range(4)], 0)
    cotangent = jnp.concatenate([full[128 * j + 64 : 128 * j + 128, :] for j in range(4)], 0)
    last = ((1,), (1,))
    in_weight = dot(scaled_grad, inputs, last)
    out_weight = dot(gated, cotangent, last)
    blank = jnp.zeros((LOCAL, CHUNK), F32)
    shape_one = returned_signal(scratch, 3) * window[:LOCAL, :]
    shape_two = returned_signal(scratch, 1) * window[LOCAL:, :]
    filter_grad = dot(
        shape_one, jnp.concatenate([hidden[...], blank], 0), last, HIGHEST
    ) + dot(shape_two, jnp.concatenate([blank, hidden[...]], 0), last, HIGHEST)
    rows = [
        in_weight[64 * at : 64 * at + 64, 128 * half : 128 * half + 128]
        for at in range(3)
        for half in range(2)
    ]
    rows += [out_weight[:, :128], out_weight[:, 128:], filter_grad, jnp.zeros((PARTS, 128), F32)]
    for at, values in enumerate(rows):
        packed[pl.ds(at, PARTS, stride=PART_ROWS), :] = values
    weights[...] = packed[: weights.shape[0], :].astype(BF16)


def channel_kernel(place, gated, scaled_grad, in_proj, out_proj, given, kept):
    first = ((0,), (0,))
    mixed = dot(out_proj[...], gated[...], first)
    grad_inputs = dot(in_proj[...], scaled_grad[...], first)
    even = place[0] % 2 == 0
    for at in range(2):
        for to, values in enumerate([mixed, grad_inputs]):
            low = values[128 * at : 128 * at + 64, :]
            high = values[128 * at + 64 : 128 * at + 128, :]
            rows = slice(128 * at + 64 * to, 128 * at + 64 * to + 64)
            given[rows, :] = jnp.where(even, high, low).astype(BF16)
            kept[rows, :] = jnp.where(even, low, high)


def core_kernel(place, received, kept, given, left):
    total = kept[...] + received[...].astype(F32)
    near = place[0] < 2
    given[...] = jnp.where(near, total[128:, :], total[:128, :]).astype(BF16)
    left[...] = jnp.where(near, total[:128, :], total[128:, :])


def sum_kernel(received, skips, spread):
    four = 4 * PART_ROWS
    parts = jnp.sum(received[...].astype(F32).reshape(PARTS // 4, four, 128), 0)
    total = sum(parts[PART_ROWS * at : PART_ROWS * at + PART_ROWS, :] for at in range(4))
    row = lax.broadcasted_iota(jnp.int32, (PART_ROWS, 128), 0)
    total = jnp.where(row == PART_ROWS - 1, skips[:1, :], total * TOTAL ** (-0.5))
    total = jnp.concatenate([total] * 4, 0)
    total = jnp.broadcast_to(total[None], (SEQ // 4, four, 128)).reshape(SEQ * PART_ROWS, 128)
    spread[...] = total.astype(BF16)


def last_kernel(
    received, over_chips, left, mixed, grad_inputs, in_weight, out_weight, filter_grad, skip_grad,
    scratch,
):
    summed = (left[...] + over_chips[...].astype(F32)).astype(BF16)
    mixed[...] = summed[:64, :]
    grad_inputs[...] = summed[64:, :]
    scratch[: received.shape[0], :] = received[...].astype(F32)

    def block(at):
        first = scratch[pl.ds(at, PARTS, stride=PART_ROWS), :]
        return first + scratch[pl.ds(PARTS * PART_ROWS + at, PARTS, stride=PART_ROWS), :]

    for half in range(2):
        for at in range(3):
            in_weight[64 * at : 64 * at + 64, 128 * half : 128 * half + 128] = block(2 * at + half)
        out_weight[:, 128 * half : 128 * half + 128] = block(6 + half)
    filters = block(8)
    filter_grad[:LOCAL, :] = filters[:, :HIDDEN]
    filter_grad[LOCAL:, :] = filters[:, HIDDEN:]
    lane = lax.broadcasted_iota(jnp.int32, (8, 128), 1)
    order = lax.broadcasted_iota(jnp.int32, (8, 128), 0)
    pick = jnp.where((lane >= 3 * order) & (lane < 3 * order + 3), 1.0, 0.0).astype(BF16)
    skips = scratch[pl.ds(PART_ROWS - 1, PARTS, stride=PART_ROWS), :].astype(BF16)
    skip_grad[...] = dot(pick, skips, ((1,), (1,)))[:2, :] * TOTAL ** (-0.5)


def call(kernel, name, outs, scalars, arrays, scratch=(), spare=SPARE):
    def vmem():
        return pl.BlockSpec(memory_space=pltpu.VMEM)

    return pl.pallas_call(
        kernel,
        name=name,
        out_shape=[jax.ShapeDtypeStruct(shape, kind) for shape, kind in outs],
        in_specs=[pl.BlockSpec(memory_space=pltpu.SMEM)] * scalars + [vmem() for _ in range(arrays)],
        out_specs=[vmem() for _ in outs],
        scratch_shapes=[
            pltpu.VMEM((*shape[:-2], shape[-2] + spare, shape[-1]), F32) for shape in scratch
        ],
        compiler_params=pltpu.CompilerParams(vmem_limit_bytes=32 * 1024 * 1024),
    )


def front():
    return call(
        front_kernel,
        "project",
        [
            ((SEQ * SEND_ROWS, 128), BF16),
            ((LOCAL, CHUNK), F32),
            ((LOCAL, CHUNK), F32),
            ((HIDDEN, CHUNK), F32),
            ((2 * LOCAL, CHUNK), F32),
            ((8, 128), F32),
        ],
        1,
        8,
        [(LOCAL * SEND_ROWS, 128)],
    )


def filtering():
    return call(
        filter_kernel,
        "filters",
        [((2 * SEQ, 2 * CHUNK), F32)],
        1,
        12,
        [(8 * HIDDEN, 128)] * 4 + [(2, SEQ, CHUNK)],
        spare=0,
    )


def series():
    return call(
        series_kernel,
        "convolve",
        [((PARTS * BACK_ROWS, 128), BF16), ((8, 128), F32)],
        0,
        9,
        [(SEQ * SEND_ROWS, 128), (PARTS * BACK_ROWS, 128)],
    )


def weighing():
    return call(
        weight_kernel,
        "weigh",
        [
            ((PARTS * PART_ROWS, 128), BF16),
            ((LOCAL, CHUNK), BF16),
            ((3 * LOCAL, CHUNK), BF16),
        ],
        0,
        6,
        [(PARTS * BACK_ROWS, 128), (PARTS * PART_ROWS, 128)],
    )


def channels():
    return call(channel_kernel, "mix", [((256, CHUNK), BF16), ((256, CHUNK), F32)], 1, 4)


def core_sum():
    return call(core_kernel, "add_core", [((128, CHUNK), BF16), ((128, CHUNK), F32)], 1, 2)


def total():
    return call(sum_kernel, "add_up", [((SEQ * PART_ROWS, 128), BF16)], 0, 2)


def finish():
    return call(
        last_kernel,
        "unpack",
        [
            ((64, CHUNK), BF16),
            ((64, CHUNK), BF16),
            ((3 * LOCAL, WIDTH), F32),
            ((LOCAL, WIDTH), F32),
            ((2 * LOCAL, HIDDEN), F32),
            ((2, LOCAL), F32),
        ],
        0,
        3,
        [(SEQ * PART_ROWS, 128)],
    )


def swap(values, group, among=None):
    tiles = values.reshape(values.shape[0] // group, group, 128)
    tiles = lax.all_to_all(
        tiles, "seq", split_axis=0, concat_axis=0, axis_index_groups=among, tiled=True
    )
    return tiles.reshape(values.shape)


def shards(
    inputs,
    clip_len,
    clip_order,
    in_proj,
    out_proj,
    filt_in,
    filt_out,
    decay_rate,
    skip_gain,
    cotangent,
):
    rank = lax.axis_index("seq").astype(jnp.int32).reshape(1)
    place = lax.axis_index("ch").astype(jnp.int32).reshape(1)
    rank, place = lax.optimization_barrier((rank, place))
    halves = [list(range(at * PARTS, at * PARTS + PARTS)) for at in range(SEQ // PARTS)]
    in_rows = in_proj.reshape(3 * LOCAL, WIDTH)
    out_rows = out_proj.T
    full = lax.all_gather(jnp.concatenate([inputs, cotangent], 0), "ch", axis=0, tiled=True)
    send, gate_two, out_grad, hidden, window, notes = front()(
        rank, clip_len.reshape(1, CLIPS), clip_order.reshape(1, CLIPS), skip_gain, full, in_rows,
        out_rows, filt_in, decay_rate,
    )
    received = swap(send, 4)
    analysis, synthesis, forward, backward, twist_cos, twist_sin = [
        jnp.asarray(x) for x in tables()
    ]
    (spectra,) = filtering()(
        rank, filt_in, filt_out.reshape(2 * LOCAL, HIDDEN), decay_rate,
        *[jnp.asarray(x) for x in wave_tables()], analysis, forward, twist_cos, twist_sin,
    )
    back, skips = series()(
        notes, received, spectra, analysis, synthesis, forward, backward, twist_cos, twist_sin
    )
    returned = swap(back, 2, halves)
    weights, gated, scaled_grad = weighing()(
        returned, full, gate_two, out_grad, hidden, window
    )
    given, kept = channels()(place, gated, scaled_grad, in_rows, out_rows)
    over_cores = lax.ppermute(given, "ch", [(0, 1), (1, 0), (2, 3), (3, 2)])
    given, left = core_sum()(place, over_cores, kept)
    (spread,) = total()(swap(weights, 2, halves), skips)
    spread, given = lax.optimization_barrier((spread, given))
    over_chips = lax.ppermute(given, "ch", [(0, 2), (2, 0), (1, 3), (3, 1)])
    mixed, grad_inputs, in_weight, out_weight, filter_grad, grad_skip = finish()(
        swap(spread, 2), over_chips, left
    )
    return (
        mixed,
        grad_inputs,
        in_weight.reshape(3, LOCAL, WIDTH),
        out_weight.T,
        filter_grad.reshape(2, LOCAL, HIDDEN),
        grad_skip,
    )


def solution(mesh):
    return jax.shard_map(
        shards,
        mesh=mesh,
        in_specs=(
            P("ch", "seq"),
            P(),
            P(),
            P(None, "ch", None),
            P(None, "ch"),
            P(),
            P(None, "ch", None),
            P(None, "ch"),
            P(None, "ch"),
            P("ch", "seq"),
        ),
        out_specs=(
            P("ch", "seq"),
            P("ch", "seq"),
            P(None, "ch", None),
            P(None, "ch"),
            P(None, "ch", None),
            P(None, "ch"),
        ),
        check_vma=False,
    )
```
